256 devices in a mesh: dp: 8 (over z_lo, y), section: 8 (over z_hi, core), fsdp: 4 (over x).
Axes of the slice: x: 4, y: 4, z: 8 (z_hi: 4, z_lo: 2; z = z_hi * 2 + z_lo), core: 2. Of those that a mesh axis runs over, the one named last changes fastest.
Arguments:
- checkpoints: bfloat16 [8, 2, 4096, 1024], P('section', None, ('dp', 'fsdp')), may hold values from -150 to 150
- cotangent: bfloat16 [2, 4096, 1024], P(None, ('dp', 'fsdp')), may hold values from -6 to 6
- weights: bfloat16 [8, 4, 1024, 1024], P('section', None, ('dp', 'fsdp')), may hold values from -6 to 6
- gains: bfloat16 [8, 1024], P('section', ('dp', 'fsdp')), may hold values from 0.099609375 to 1.8984375
- lengths: int32 [2, 31], replicated, may hold values from 1 to 256, 3840 in all within a row
Outputs:
- frame_grad: bfloat16 [8, 2, 4096, 1024], P('section', None, ('dp', 'fsdp'))
- weight_grad: float32 [8, 4, 1024, 1024], P('section', None, ('dp', 'fsdp'))
- gain_grad: float32 [8, 1024], P('section', ('dp', 'fsdp'))
The draws below stay inside these ranges and needn't reach their ends.
Inputs may be any that keep to these rules, and one draw needn't show every extreme that they name: Each row of lengths adds up to 3840, and its longest utterance has exactly 256 frames; the last utterance, not listed, has 256 frames.
All inputs are finite; a program needn't handle non-finite values.
Results may differ from the reference program's by a relative error of at most 0.035.
The reference program's roundings to bfloat16 on the way count: a program that leaves them out, or rounds other values in their place, can miss the bound.
Values may be sent and summed in bfloat16 or wider, within the bound.
No kernel may reach another device: no remote copies, remote signals or barrier semaphores. Data moves between devices by JAX's collectives and lax.ppermute only.
A program may use at most 128 MiB of HBM per device.

```python
import math
import jax
import jax.numpy as jnp
import numpy as np
from jax import lax

HEAD = 128
D = 1024
STRETCH = 128
F = 128
MICRO = 2
NSEG = 32
SECTIONS = 8
FRAMES = 4096
MOST = 256


def draw_checkpoints(key, part):
    key = jax.random.fold_in(key, 11)
    key_base = jax.random.fold_in(key, 1)
    key_cols = jax.random.fold_in(key, 2)
    key_rows = jax.random.fold_in(key, 3)
    full_shape = (SECTIONS, MICRO, FRAMES, D)
    column_scale = jnp.exp(jax.random.uniform(key_cols, (SECTIONS, 1, 1, D), jnp.float32, math.log(0.3), math.log(3.0)))
    row_scale = jnp.exp(jax.random.uniform(key_rows, (SECTIONS, MICRO, FRAMES, 1), jnp.float32, math.log(0.5), math.log(5.0)))
    values_base = jax.random.normal(key_base, full_shape, jnp.float32)
    return (values_base * column_scale * row_scale).astype(jnp.bfloat16)


def draw_weights(key, part):
    key = jax.random.fold_in(key, 23)
    full_shape = (SECTIONS, 4, D, D)
    values_base = jax.random.normal(key, full_shape, jnp.float32) * D ** (-0.5)
    return values_base.astype(jnp.bfloat16)


def block_scale(rng, shape, split, low, top_value):
    def one(dim, parts):
        draws = jax.random.uniform(jax.random.fold_in(jax.random.fold_in(rng, 6), dim), (parts,), jnp.float32, low / len(split), top_value / len(split))
        return jnp.repeat(jnp.exp(draws), shape[dim] // parts).reshape((-1,) + (1,) * (len(shape) - dim - 1))

    level = one(*split[0])
    for cut in split[1:]:
        level = level * one(*cut)
    return level


def split_up(amount, total, reach, slope):
    weights = [(1 << 20) // math.isqrt(standing ** slope) + 1 for standing in range(2, amount + 1)]
    spare, given = total - reach - (amount - 1), [1] * (amount - 1)
    while spare > 0:
        candidates = [i for i in range(amount - 1) if given[i] < reach]
        whole, budget = sum([weights[i] for i in candidates]), spare
        for i in candidates:
            more = min(reach - given[i], max(1, budget * weights[i] // whole), spare)
            given[i] = given[i] + more
            spare = spare - more
    return np.array([reach] + given)


def ragged(stream_key, number_of, total, limit, slope):
    if number_of == 2:
        one = jax.random.randint(stream_key, (), max(1, total - limit), min(limit, total - 1) + 1)
        return jnp.stack([one, total - one])
    tallies = jnp.asarray(split_up(number_of, total, limit, slope), jnp.int32)
    couples = (number_of - 1) // 2
    giver, sink = tallies[1:1 + 2 * couples:2], tallies[2:2 + 2 * couples:2]
    slack = jnp.minimum(giver - 1, limit - sink)
    moved = jax.random.randint(jax.random.fold_in(stream_key, 1), (couples,), 0, 1 << 20) % (slack + 1)
    tallies = tallies.at[1:1 + 2 * couples:2].set(giver - moved).at[2:2 + 2 * couples:2].set(sink + moved)
    return tallies[jax.random.permutation(jax.random.fold_in(stream_key, 2), number_of)]


def scatter_about(stream_key, shape, deviation, reach, shards=(), kind=jnp.bfloat16):
    factor_of = block_scale(stream_key, shape, shards, -0.22, 0.18) if shards else 1.0
    array = jax.random.normal(stream_key, shape, jnp.float32) * deviation * factor_of
    return jnp.minimum(jnp.maximum(array, -reach), reach).astype(kind)


def setup_inputs(seed: int = 0) -> dict:
    seeds = jax.random.split(jax.random.key(seed), 6)
    checkpoints = draw_checkpoints(jax.random.fold_in(seeds[5], 71), 0)
    cotangent = scatter_about(seeds[1], (MICRO, FRAMES, D), 1.0, 6.0, ((1, 32),))
    weights = draw_weights(jax.random.fold_in(seeds[5], 71), 0)
    gains = jnp.clip(1.0 + 0.18 * jax.random.normal(seeds[3], (SECTIONS, D), jnp.float32), 0.099609375, 1.8984375).astype(jnp.bfloat16)
    lengths = jax.vmap(lambda own: ragged(own, NSEG - 1, FRAMES - MOST, MOST, 2))(jax.random.split(seeds[4], MICRO)).reshape((MICRO, NSEG - 1)).astype(jnp.int32)
    return dict(checkpoints=checkpoints, cotangent=cotangent, weights=weights, gains=gains, lengths=lengths)


def to_bf16(values_in):
    return lax.optimization_barrier(values_in.astype(jnp.bfloat16))

def rounded(values_in):
    return to_bf16(values_in).astype(jnp.float32)

def normalize(inputs, gain_row):
    as_float = inputs.astype(jnp.float32)
    rscale = lax.rsqrt(lax.optimization_barrier(jnp.mean(as_float * as_float, axis=-1, keepdims=True)) + 1e-06)
    normed = to_bf16(as_float * rscale * gain_row.astype(jnp.float32))
    return (as_float, rscale, normed)

def segment_ids(bounds, places):
    counted = lax.optimization_barrier(jnp.sum((places[:, None] >= bounds[None, :]).astype(jnp.int32), axis=1))
    return jnp.where(places < 0, -1, counted).astype(jnp.int32)

def allowed_mask(block_start, bounds, frames, stretch_len):
    left_span = 2 * stretch_len
    q_index = jnp.arange(frames, dtype=jnp.int32)
    k_index = jnp.arange(left_span + frames, dtype=jnp.int32) - left_span
    q_seg = segment_ids(bounds, block_start + q_index)
    k_seg = segment_ids(bounds, block_start + k_index)
    q_stretch = jnp.floor_divide(q_index, stretch_len)
    k_stretch = jnp.floor_divide(k_index, stretch_len)
    nearby = (k_stretch[None, :] <= q_stretch[:, None]) & (k_stretch[None, :] >= q_stretch[:, None] - 2)
    return nearby & (q_seg[:, None] == k_seg[None, :])

def project(rows_in, weight):
    full_shape = rows_in.shape
    flat_rows = rows_in.reshape(-1, full_shape[-1])
    return to_bf16(jnp.dot(flat_rows, weight, preferred_element_type=jnp.float32)).reshape(full_shape)

def project_back(rows_in, weight):
    full_shape = rows_in.shape
    flat_rows = rows_in.reshape(-1, full_shape[-1])
    return jnp.dot(flat_rows, weight.T, preferred_element_type=jnp.float32).reshape(full_shape)

def contract_rows(left_in, right_in):
    return lax.dot_general(left_in, right_in, (((0,), (0,)), ((), ())), preferred_element_type=jnp.float32)

def split_heads(rows_in, head_count):
    return rows_in.astype(jnp.float32).reshape(rows_in.shape[:-1] + (head_count, HEAD))

def attend(queries, key_rows, values, allowed, head_count, score_scale):
    query_heads = split_heads(queries, head_count)
    key_heads = split_heads(key_rows, head_count)
    value_heads = split_heads(values, head_count)
    scores = jnp.einsum('...qhd,...khd->...hqk', query_heads, key_heads) * score_scale
    mask_rows = allowed[..., None, :, :]
    scores = jnp.where(mask_rows, scores, -1e+30)
    top_score = lax.optimization_barrier(jnp.max(scores, axis=-1, keepdims=True))
    expo = jnp.where(mask_rows, jnp.exp(scores - top_score), 0.0)
    soft_probs = expo / lax.optimization_barrier(jnp.sum(expo, axis=-1, keepdims=True))
    mixed = jnp.einsum('...hqk,...khd->...qhd', rounded(soft_probs), value_heads)
    attended = to_bf16(mixed.reshape(queries.shape))
    return (soft_probs, attended)

def backward_pieces(grad_rows, queries, key_rows, values, soft_probs, w_query, w_key, w_value, w_out, head_count, score_scale, left_span):
    d_att = to_bf16(project_back(grad_rows, w_out))
    att_heads = split_heads(d_att, head_count)
    value_heads = split_heads(values, head_count)
    key_heads = split_heads(key_rows, head_count)
    query_heads = split_heads(queries, head_count)
    d_probs = jnp.einsum('...qhd,...khd->...hqk', att_heads, value_heads)
    d_values = jnp.einsum('...hqk,...qhd->...khd', rounded(soft_probs), att_heads)
    d_values = to_bf16(d_values.reshape(values.shape))
    d_scores = soft_probs * (d_probs - lax.optimization_barrier(jnp.sum(d_probs * soft_probs, axis=-1, keepdims=True))) * score_scale
    score_grad = rounded(d_scores)
    d_query = to_bf16(jnp.einsum('...hqk,...khd->...qhd', score_grad, key_heads).reshape(queries.shape))
    d_keys = to_bf16(jnp.einsum('...hqk,...qhd->...khd', score_grad, query_heads).reshape(key_rows.shape))
    key_left = d_keys[..., :left_span, :]
    key_same = d_keys[..., left_span:, :]
    val_left = d_values[..., :left_span, :]
    val_same = d_values[..., left_span:, :]
    to_left = to_bf16(project_back(key_left, w_key) + project_back(val_left, w_value))
    own_part = project_back(d_query, w_query) + project_back(key_same, w_key) + project_back(val_same, w_value)
    return (own_part, to_left, d_query, key_same, val_same, key_left, val_left)

def finish(grad_rows, as_float, rscale, gain_row, d_normed):
    scaled = gain_row.astype(jnp.float32) * d_normed
    cubic = rscale * rscale * rscale
    frame_f = grad_rows.astype(jnp.float32) + rscale * scaled - as_float * cubic * lax.optimization_barrier(jnp.mean(scaled * as_float, axis=-1, keepdims=True))
    gain_part = d_normed * as_float * rscale
    return (frame_f, gain_part)

def from_left(tail_block, offset):
    padding = jnp.zeros_like(tail_block[:, :offset])
    return jnp.concatenate([padding, tail_block[:, :-offset]], axis=1)

def from_right(left_part, offset):
    padding = jnp.zeros_like(left_part[:, :offset])
    return jnp.concatenate([left_part[:, offset:], padding], axis=1)

def reference(checkpoints, cotangent, weights, gains, lengths):
    blocks = FRAMES // F
    left_span = 2 * STRETCH
    tail_rows = min(F, left_span)
    reach_count = left_span // tail_rows
    head_count = D // HEAD
    score_scale = 1.0 / math.sqrt(HEAD)
    bounds = jnp.cumsum(lengths, axis=1).astype(jnp.int32)
    starts = jnp.arange(blocks, dtype=jnp.int32) * F
    allowed = jax.vmap(lambda bound_row: jax.vmap(lambda block_start: allowed_mask(block_start, bound_row, F, STRETCH))(starts))(bounds)
    grad_rows = cotangent.reshape(MICRO, blocks, F, D)
    frame_list = []
    weight_list = []
    gain_list = []
    for section_at in range(SECTIONS - 1, -1, -1):
        w_query = weights[section_at, 0]
        w_key = weights[section_at, 1]
        w_value = weights[section_at, 2]
        w_out = weights[section_at, 3]
        gain_row = gains[section_at]
        inputs = checkpoints[section_at].reshape(MICRO, blocks, F, D)
        as_float, rscale, normed = normalize(inputs, gain_row)
        tail_block = normed[:, :, F - tail_rows:, :]
        left_rows = jnp.concatenate([from_left(tail_block, offset) for offset in range(reach_count, 0, -1)], axis=2)
        key_input = jnp.concatenate([left_rows, normed], axis=2)
        queries = project(normed, w_query)
        key_rows = project(key_input, w_key)
        values = project(key_input, w_value)
        soft_probs, attended = attend(queries, key_rows, values, allowed, head_count, score_scale)
        own_part, to_left, d_query, key_same, val_same, key_left, val_left = backward_pieces(grad_rows, queries, key_rows, values, soft_probs, w_query, w_key, w_value, w_out, head_count, score_scale, left_span)
        received = jnp.zeros((MICRO, blocks, tail_rows, D), jnp.float32)
        for offset in range(1, reach_count + 1):
            left_part = to_left[:, :, (reach_count - offset) * tail_rows:(reach_count - offset + 1) * tail_rows, :]
            received = received + from_right(left_part, offset).astype(jnp.float32)
        d_normed = own_part.at[:, :, F - tail_rows:, :].add(received)
        frame_f, gain_part = finish(grad_rows, as_float, rscale, gain_row, d_normed)
        frame_out = to_bf16(frame_f)
        gain_terms = lax.optimization_barrier(jnp.sum(gain_part, axis=(0, 2)))
        gain_list.append(lax.optimization_barrier(jnp.sum(rounded(gain_terms), axis=0)))
        stacked = tuple((jnp.moveaxis(item, 1, 0) for item in (normed, left_rows, attended, grad_rows, d_query, key_same, val_same, key_left, val_left)))

        def add_block(weight_total, items):
            h_own, h_left, att_rows, grad_block, dq_rows, ks_rows, vs_rows, kl_rows, vl_rows = [item.reshape(-1, D) for item in items]
            term = jnp.stack([contract_rows(h_own, dq_rows), contract_rows(h_own, ks_rows) + contract_rows(h_left, kl_rows), contract_rows(h_own, vs_rows) + contract_rows(h_left, vl_rows), contract_rows(att_rows, grad_block)])
            return (weight_total + rounded(term), None)
        weight_total, _ = lax.scan(add_block, jnp.zeros((4, D, D), jnp.float32), stacked)
        weight_list.append(weight_total)
        frame_list.append(frame_out.reshape(MICRO, FRAMES, D))
        grad_rows = frame_out
    return (jnp.stack(frame_list[::-1]), jnp.stack(weight_list[::-1]), jnp.stack(gain_list[::-1]))
```

```python
from functools import partial
import math

import jax
import jax.numpy as jnp
from jax import lax
from jax.experimental import pallas as pl
from jax.experimental.pallas import tpu as pltpu
from jax.sharding import PartitionSpec as P

HEAD = 128
BLOCK = 128
WIDTH = 1024
HEADS = WIDTH // HEAD
MICRO = 2
SCALE = 1.0 / math.sqrt(HEAD)
GROUP = ("dp", "fsdp")
EVERY = ("dp", "section", "fsdp")
VMEM_LIMIT = 52 * 1024 * 1024


def dot(left, right):
    return lax.dot_general(left, right, (((1,), (0,)), ((), ())), preferred_element_type=jnp.float32)


def dot_nt(left, right):
    return lax.dot_general(left, right, (((1,), (1,)), ((), ())), preferred_element_type=jnp.float32)


def dot_tn(left, right):
    return lax.dot_general(left, right, (((0,), (0,)), ((), ())), preferred_element_type=jnp.float32)


def shift(value, steps):
    count = lax.axis_size(GROUP)
    pairs = [(b, b + steps) for b in range(count) if 0 <= b + steps < count]
    return lax.ppermute(value, GROUP, pairs)


def hop(value, source, target, back):
    sections, rows = lax.axis_size("section"), lax.axis_size("fsdp")
    count = lax.axis_size(GROUP)

    def place(section, block):
        return (block // rows * sections + section) * rows + block % rows

    pairs = [(place(source, b), place(target, b - back)) for b in range(back, count)]
    return lax.ppermute(value, EVERY, pairs)


def group_dims():
    dp, fsdp = lax.axis_size("dp"), lax.axis_size("fsdp")
    planes = 2 if dp % 2 == 0 else 1
    return (planes, dp // planes, fsdp)


def turn(value, axis, steps):
    dims = group_dims()
    pairs = []
    for z in range(dims[0]):
        for y in range(dims[1]):
            for x in range(dims[2]):
                at = [z, y, x]
                to = list(at)
                to[axis] = (at[axis] + steps) % dims[axis]
                index = lambda p: (p[0] * dims[1] + p[1]) * dims[2] + p[2]
                pairs.append((index(at), index(to)))
    return lax.ppermute(value, GROUP, pairs)


def group_sum(value):
    for axis, size in enumerate(group_dims()):
        value = sum([turn(value, axis, steps) for steps in range(1, size)], value)
    return value


def normed(x, gain):
    as_float = x.astype(jnp.float32)
    rscale = lax.rsqrt(jnp.mean(as_float * as_float, axis=-1, keepdims=True) + 1e-06)
    return (as_float * rscale * gain).astype(jnp.bfloat16)


def forward_kernel(
    l2, l1, own, r1, r2, w, gain, seg_col, seg_row,
    h_out, q_out, k_out, v_out, p_out, pt_out, o_out, a_out,
    h5, q3, k5, v5,
):
    gain_row = gain[0:1, :]
    for at, part in enumerate((l2, l1, own, r1, r2)):
        h5[at * BLOCK : (at + 1) * BLOCK, :] = normed(part[0], gain_row)
    h_out[0] = h5[2 * BLOCK : 3 * BLOCK, :]
    for n in range(0, WIDTH, 256):
        cols = slice(n, n + 256)
        q3[:, cols] = dot(h5[2 * BLOCK :, :], w[0, :, cols]).astype(jnp.bfloat16)
        k5[:, cols] = dot(h5[...], w[1, :, cols]).astype(jnp.bfloat16)
        v5[:, cols] = dot(h5[...], w[2, :, cols]).astype(jnp.bfloat16)
    q_out[0] = q3[...]
    k_out[0] = k5[: 3 * BLOCK, :]
    v_out[0] = v5[: 3 * BLOCK, :]
    for head in range(HEADS):
        cols = slice(head * HEAD, (head + 1) * HEAD)
        for j in range(3):
            rows = slice(j * BLOCK, (j + 1) * BLOCK)
            keys = slice(j * BLOCK, (j + 3) * BLOCK)
            allowed = seg_col[0, (j + 2) * BLOCK : (j + 3) * BLOCK, 0:1] == seg_row[0, 0:1, keys]
            score = jnp.where(allowed, dot_nt(q3[rows, cols], k5[keys, cols]) * SCALE, -1e30)
            top = jnp.max(score, axis=-1, keepdims=True)
            expo = jnp.where(allowed, jnp.exp(score - top), 0.0)
            p = expo / jnp.sum(expo, axis=-1, keepdims=True)
            high = p.astype(jnp.bfloat16)
            low = (p - high.astype(jnp.float32)).astype(jnp.bfloat16)
            values = v5[keys, cols]
            mixed = dot(high, values)
            o_out[0, rows, cols] = mixed + dot(low, values)
            if j == 0:
                p_out[0, head] = p
                a_out[0, :, cols] = mixed.astype(jnp.bfloat16)
            pt_out[0, head, :, rows] = p[:, (2 - j) * BLOCK : (3 - j) * BLOCK].T


def forward(parts, w, gain, seg_col, seg_row):
    def per_micro(shape):
        return pl.BlockSpec((1,) + shape, lambda m: (m,) + (0,) * len(shape))

    def whole(shape):
        return pl.BlockSpec(shape, lambda m: (0,) * len(shape), pipeline_mode=pl.Buffered(1))

    outs = [
        ((BLOCK, WIDTH), jnp.bfloat16),
        ((3 * BLOCK, WIDTH), jnp.bfloat16),
        ((3 * BLOCK, WIDTH), jnp.bfloat16),
        ((3 * BLOCK, WIDTH), jnp.bfloat16),
        ((HEADS, BLOCK, 3 * BLOCK), jnp.float32),
        ((HEADS, BLOCK, 3 * BLOCK), jnp.float32),
        ((3 * BLOCK, WIDTH), jnp.float32),
        ((BLOCK, WIDTH), jnp.bfloat16),
    ]
    return pl.pallas_call(
        forward_kernel,
        grid=(MICRO,),
        in_specs=[per_micro((BLOCK, WIDTH))] * 5
        + [
            whole((3, WIDTH, WIDTH)),
            whole((8, WIDTH)),
            per_micro((5 * BLOCK, 1)),
            per_micro((1, 5 * BLOCK)),
        ],
        out_specs=[per_micro(shape) for shape, _ in outs],
        out_shape=[jax.ShapeDtypeStruct((MICRO,) + shape, kind) for shape, kind in outs],
        scratch_shapes=[
            pltpu.VMEM((5 * BLOCK, WIDTH), jnp.bfloat16),
            pltpu.VMEM((3 * BLOCK, WIDTH), jnp.bfloat16),
            pltpu.VMEM((5 * BLOCK, WIDTH), jnp.bfloat16),
            pltpu.VMEM((5 * BLOCK, WIDTH), jnp.bfloat16),
        ],
        compiler_params=pltpu.CompilerParams(vmem_limit_bytes=VMEM_LIMIT),
        cost_estimate=pl.CostEstimate(
            flops=2 * 2 * 15 * BLOCK * WIDTH * WIDTH, bytes_accessed=28 << 20, transcendentals=0
        ),
        name="forward",
    )(*parts, w, gain, seg_col, seg_row)


def backward_kernel(micro, first, *refs):
    flag, g0, g1, g2, w, q_in, k_in, v_in, p_in, pt_in, o_in, x_in, gain_in = refs[:13]
    refs = refs[13 if first else 19 :]
    frame_out, g_out, dq_out, dk_out, dv_out, gain_out = refs[:6]
    g, wv, q, k, v, p, pt, o, x, gain, da, dq, dk, dv, dh, frame, gain_sum, sems = refs[6:]

    @pl.when(flag[0] == 1)
    def _():
        def move(at, source, target):
            copy = pltpu.make_async_copy(source, target, sems.at[at])
            copy.start()
            return copy

        load_g = [
            move(at, part, g.at[pl.ds(at * BLOCK, BLOCK), :]) for at, part in enumerate((g0, g1, g2))
        ]
        load_wo = move(3, w.at[3], wv.at[3])
        load_o = move(4, o_in.at[micro], o)
        load_v = move(5, v_in.at[micro], v)
        load_p = move(6, p_in.at[micro], p)
        load_k = move(7, k_in.at[micro], k)
        load_pt = move(8, pt_in.at[micro], pt)
        load_q = move(9, q_in.at[micro], q)
        load_w = move(10, w.at[pl.ds(0, 3)], wv.at[pl.ds(0, 3)])
        load_x = move(11, x_in.at[micro], x)
        load_gain = move(12, gain_in, gain)
        for copy in load_g:
            copy.wait()
        load_wo.wait()
        store_g = move(13, g.at[pl.ds(0, BLOCK), :], g_out)
        for n in range(0, WIDTH, 256):
            cols = slice(n, n + 256)
            da[:, cols] = dot_nt(g[...], wv[3, cols, :]).astype(jnp.bfloat16)
        for copy in (load_o, load_v, load_p, load_k, load_pt, load_q):
            copy.wait()
        for head in range(HEADS):
            cols = slice(head * HEAD, (head + 1) * HEAD)
            da_h = da[:, cols]
            inner = jnp.sum(da_h.astype(jnp.float32) * o[:, cols], axis=-1, keepdims=True)
            dp = dot_nt(da_h[:BLOCK], v[:, cols])
            ds = (p[head] * (dp - inner[:BLOCK]) * SCALE).astype(jnp.bfloat16)
            dq[:, cols] = dot(ds, k[:, cols]).astype(jnp.bfloat16)
            inner_row = jnp.broadcast_to(inner, (3 * BLOCK, HEAD)).T
            p_t = pt[head]
            dp_t = dot_nt(v[2 * BLOCK :, cols], da_h)
            ds_t = (p_t * (dp_t - inner_row) * SCALE).astype(jnp.bfloat16)
            dk[:, cols] = dot(ds_t, q[:, cols]).astype(jnp.bfloat16)
            dv[:, cols] = dot(p_t.astype(jnp.bfloat16), da_h).astype(jnp.bfloat16)
        stores = [
            store_g,
            move(14, dq, dq_out),
            move(15, dk, dk_out),
            move(16, dv, dv_out),
        ]
        load_w.wait()
        for n in range(0, WIDTH, 256):
            cols = slice(n, n + 256)
            dh[:, cols] = (
                dot_nt(dq[...], wv[0, cols, :])
                + dot_nt(dk[...], wv[1, cols, :])
                + dot_nt(dv[...], wv[2, cols, :])
            )
        load_x.wait()
        load_gain.wait()
        as_float = x[...].astype(jnp.float32)
        rscale = lax.rsqrt(jnp.mean(as_float * as_float, axis=-1, keepdims=True) + 1e-06)
        d_normed = dh[...]
        scaled = gain[0:1, :] * d_normed
        cubic = rscale * rscale * rscale
        frame_f = (
            g[:BLOCK, :].astype(jnp.float32)
            + rscale * scaled
            - as_float * (cubic * jnp.mean(scaled * as_float, axis=-1, keepdims=True))
        )
        frame[...] = frame_f.astype(jnp.bfloat16)
        stores.append(move(17, frame, frame_out))
        term = jnp.sum(d_normed * as_float * rscale, axis=0, keepdims=True)
        gain_sum[...] = jnp.broadcast_to(term, (8, WIDTH))
        stores.append(move(18, gain_sum, gain_out))
        for copy in stores:
            copy.wait()


def backward(micro, flag, incoming, w, kept, x, gain, stash):
    block = jax.ShapeDtypeStruct((BLOCK, WIDTH), jnp.bfloat16)
    outs = [block] * 5 + [jax.ShapeDtypeStruct((8, WIDTH), jnp.float32)]
    first = stash is None
    operands = [flag, *incoming, w, *kept, x, gain] + ([] if first else list(stash))
    anywhere = pl.BlockSpec(memory_space=pl.ANY)
    bf16, f32 = jnp.bfloat16, jnp.float32
    scratch = [
        ((3 * BLOCK, WIDTH), bf16),
        ((4, WIDTH, WIDTH), bf16),
        ((3 * BLOCK, WIDTH), bf16),
        ((3 * BLOCK, WIDTH), bf16),
        ((3 * BLOCK, WIDTH), bf16),
        ((HEADS, BLOCK, 3 * BLOCK), f32),
        ((HEADS, BLOCK, 3 * BLOCK), f32),
        ((3 * BLOCK, WIDTH), f32),
        ((BLOCK, WIDTH), bf16),
        ((8, WIDTH), f32),
        ((3 * BLOCK, WIDTH), bf16),
        ((BLOCK, WIDTH), bf16),
        ((BLOCK, WIDTH), bf16),
        ((BLOCK, WIDTH), bf16),
        ((BLOCK, WIDTH), f32),
        ((BLOCK, WIDTH), bf16),
        ((8, WIDTH), f32),
    ]
    return pl.pallas_call(
        partial(backward_kernel, micro, first),
        in_specs=[pl.BlockSpec(memory_space=pltpu.SMEM)] + [anywhere] * (len(operands) - 1),
        out_specs=[anywhere] * 6,
        out_shape=outs,
        scratch_shapes=[pltpu.VMEM(shape, kind) for shape, kind in scratch]
        + [pltpu.SemaphoreType.DMA((19,))],
        input_output_aliases={} if first else {13 + at: at for at in range(6)},
        compiler_params=pltpu.CompilerParams(vmem_limit_bytes=VMEM_LIMIT),
        cost_estimate=pl.CostEstimate(
            flops=2 * 7 * BLOCK * WIDTH * WIDTH, bytes_accessed=16 << 20, transcendentals=0
        ),
        name="backward",
    )(*operands)


def segments(lengths, block):
    bounds = jnp.cumsum(lengths, axis=1)
    total = lax.axis_size(GROUP) * BLOCK
    places = (block - 2) * BLOCK + jnp.arange(5 * BLOCK, dtype=jnp.int32)
    counted = jnp.sum((places[None, :, None] >= bounds[:, None, :]).astype(jnp.int32), axis=2)
    return jnp.where(places < 0, -1, jnp.where(places >= total, -2, counted))


def body(checkpoints, cotangent, weights, gains, lengths):
    sections, section = lax.axis_size("section"), lax.axis_index("section")
    block = lax.axis_index(GROUP)
    share = gains.shape[1]

    gathered = lax.all_gather(weights[0], GROUP, axis=1, tiled=True)
    spread = lax.dynamic_update_slice(
        jnp.zeros((1, WIDTH), jnp.float32), gains.astype(jnp.float32), (0, block * share)
    )
    gain = jnp.broadcast_to(group_sum(spread), (8, WIDTH))

    x = checkpoints[0]
    left, right = shift(x, 1), shift(x, -1)
    parts = (shift(left, 1), left, x, right, shift(right, -1))
    source = max(sections - 3, 0)
    cot = (cotangent, hop(cotangent, source, sections - 1, 1), hop(cotangent, source, sections - 1, 2))

    segs = segments(lengths, block)
    h, q, k, v, p, pt, o, a = forward(parts, gathered, gain, segs[:, :, None], segs[:, None, :])
    kept = (q, k, v, p, pt, o)

    stash = [None] * MICRO
    incoming = [[part[micro] for part in cot] for micro in range(MICRO)]
    for at in range(sections - 1, -1, -1):
        flag = (section == at).astype(jnp.int32).reshape(1)
        for micro in range(MICRO):
            stash[micro] = backward(
                micro, flag, incoming[micro], gathered, kept, x, gain, stash[micro]
            )
            if at > 0:
                incoming[micro] = [hop(stash[micro][0], at, at - 1, back) for back in range(3)]

    frame, g, dq, dk, dv, gain_part = (
        [stash[micro][at] for micro in range(MICRO)] for at in range(6)
    )
    h, a = h.reshape(-1, WIDTH), a.reshape(-1, WIDTH)
    term = jnp.stack(
        [
            dot_tn(h, jnp.concatenate(dq)),
            dot_tn(h, jnp.concatenate(dk)),
            dot_tn(h, jnp.concatenate(dv)),
            dot_tn(a, jnp.concatenate(g)),
        ]
    )
    weight_part = lax.psum_scatter(
        term.astype(jnp.bfloat16), GROUP, scatter_dimension=1, tiled=True
    ).astype(jnp.float32)
    gain_term = (gain_part[0][0:1] + gain_part[1][0:1]).astype(jnp.bfloat16).astype(jnp.float32)
    gain_sum = lax.dynamic_slice(group_sum(gain_term), (0, block * share), (1, share))
    return (jnp.stack(frame)[None], weight_part[None], gain_sum)


def solution(mesh):
    placed = (
        P("section", None, ("dp", "fsdp"), None),
        P(None, ("dp", "fsdp"), None),
        P("section", None, ("dp", "fsdp"), None),
        P("section", ("dp", "fsdp")),
        P(),
    )
    return jax.shard_map(
        body,
        mesh=mesh,
        in_specs=placed,
        out_specs=(
            P("section", None, ("dp", "fsdp"), None),
            P("section", None, ("dp", "fsdp"), None),
            P("section", ("dp", "fsdp")),
        ),
        check_vma=False,
    )
```

```python
from functools import partial
import math

import jax
import jax.numpy as jnp
from jax import lax
from jax.experimental import pallas as pl
from jax.experimental.pallas import tpu as pltpu
from jax.sharding import PartitionSpec as P

HEAD = 128
BLOCK = 128
WIDTH = 1024
HEADS = WIDTH // HEAD
MICRO = 2
SCALE = 1.0 / math.sqrt(HEAD)
GROUP = ("dp", "fsdp")
EVERY = ("dp", "section", "fsdp")
VMEM_LIMIT = 52 * 1024 * 1024


def dot(left, right):
    return lax.dot_general(left, right, (((1,), (0,)), ((), ())), preferred_element_type=jnp.float32)


def dot_nt(left, right):
    return lax.dot_general(left, right, (((1,), (1,)), ((), ())), preferred_element_type=jnp.float32)


def dot_tn(left, right):
    return lax.dot_general(left, right, (((0,), (0,)), ((), ())), preferred_element_type=jnp.float32)


def shift(value, steps):
    count = lax.axis_size(GROUP)
    pairs = [(b, b + steps) for b in range(count) if 0 <= b + steps < count]
    return lax.ppermute(value, GROUP, pairs)


def hop(value, source, target, back):
    sections, rows = lax.axis_size("section"), lax.axis_size("fsdp")
    count = lax.axis_size(GROUP)

    def place(section, block):
        return (block // rows * sections + section) * rows + block % rows

    pairs = [(place(source, b), place(target, b - back)) for b in range(back, count)]
    return lax.ppermute(value, EVERY, pairs)


def group_dims():
    dp, fsdp = lax.axis_size("dp"), lax.axis_size("fsdp")
    planes = 2 if dp % 2 == 0 else 1
    return (planes, dp // planes, fsdp)


def turn(value, axis, steps):
    dims = group_dims()
    pairs = []
    for z in range(dims[0]):
        for y in range(dims[1]):
            for x in range(dims[2]):
                at = [z, y, x]
                to = list(at)
                to[axis] = (at[axis] + steps) % dims[axis]
                index = lambda p: (p[0] * dims[1] + p[1]) * dims[2] + p[2]
                pairs.append((index(at), index(to)))
    return lax.ppermute(value, GROUP, pairs)


def group_sum(value):
    for axis, size in enumerate(group_dims()):
        moving = value
        for _ in range(size - 1):
            moving = turn(moving, axis, 1)
            value = value + moving
    return value


def normed(x, gain):
    as_float = x.astype(jnp.float32)
    rscale = lax.rsqrt(jnp.mean(as_float * as_float, axis=-1, keepdims=True) + 1e-06)
    return (as_float * rscale * gain).astype(jnp.bfloat16)


def forward_kernel(
    l2, l1, own, r1, r2, w, gain, seg_col, seg_row,
    h_out, q_out, k_out, v_out, p_out, pt_out, o_out, a_out,
    h5, q3, k5, v5,
):
    gain_row = gain[0:1, :]
    for at, part in enumerate((l2, l1, own, r1, r2)):
        h5[at * BLOCK : (at + 1) * BLOCK, :] = normed(part[0], gain_row)
    h_out[0] = h5[2 * BLOCK : 3 * BLOCK, :]
    for n in range(0, WIDTH, 256):
        cols = slice(n, n + 256)
        q3[:, cols] = dot(h5[2 * BLOCK :, :], w[0, :, cols]).astype(jnp.bfloat16)
        k5[:, cols] = dot(h5[...], w[1, :, cols]).astype(jnp.bfloat16)
        v5[:, cols] = dot(h5[...], w[2, :, cols]).astype(jnp.bfloat16)
    q_out[0] = q3[...]
    k_out[0] = k5[: 3 * BLOCK, :]
    v_out[0] = v5[: 3 * BLOCK, :]
    for head in range(HEADS):
        cols = slice(head * HEAD, (head + 1) * HEAD)
        for j in range(3):
            rows = slice(j * BLOCK, (j + 1) * BLOCK)
            keys = slice(j * BLOCK, (j + 3) * BLOCK)
            allowed = seg_col[0, (j + 2) * BLOCK : (j + 3) * BLOCK, 0:1] == seg_row[0, 0:1, keys]
            score = jnp.where(allowed, dot_nt(q3[rows, cols], k5[keys, cols]) * SCALE, -1e30)
            top = jnp.max(score, axis=-1, keepdims=True)
            expo = jnp.where(allowed, jnp.exp(score - top), 0.0)
            p = expo / jnp.sum(expo, axis=-1, keepdims=True)
            high = p.astype(jnp.bfloat16)
            low = (p - high.astype(jnp.float32)).astype(jnp.bfloat16)
            values = v5[keys, cols]
            mixed = dot(high, values)
            o_out[0, rows, cols] = mixed + dot(low, values)
            if j == 0:
                p_out[0, head] = p
                a_out[0, :, cols] = mixed.astype(jnp.bfloat16)
            pt_out[0, head, :, rows] = p[:, (2 - j) * BLOCK : (3 - j) * BLOCK].T


def forward(parts, w, gain, seg_col, seg_row):
    def per_micro(shape):
        return pl.BlockSpec((1,) + shape, lambda m: (m,) + (0,) * len(shape))

    def whole(shape):
        return pl.BlockSpec(shape, lambda m: (0,) * len(shape), pipeline_mode=pl.Buffered(1))

    outs = [
        ((BLOCK, WIDTH), jnp.bfloat16),
        ((3 * BLOCK, WIDTH), jnp.bfloat16),
        ((3 * BLOCK, WIDTH), jnp.bfloat16),
        ((3 * BLOCK, WIDTH), jnp.bfloat16),
        ((HEADS, BLOCK, 3 * BLOCK), jnp.float32),
        ((HEADS, BLOCK, 3 * BLOCK), jnp.float32),
        ((3 * BLOCK, WIDTH), jnp.float32),
        ((BLOCK, WIDTH), jnp.bfloat16),
    ]
    return pl.pallas_call(
        forward_kernel,
        grid=(MICRO,),
        in_specs=[per_micro((BLOCK, WIDTH))] * 5
        + [
            whole((3, WIDTH, WIDTH)),
            whole((8, WIDTH)),
            per_micro((5 * BLOCK, 1)),
            per_micro((1, 5 * BLOCK)),
        ],
        out_specs=[per_micro(shape) for shape, _ in outs],
        out_shape=[jax.ShapeDtypeStruct((MICRO,) + shape, kind) for shape, kind in outs],
        scratch_shapes=[
            pltpu.VMEM((5 * BLOCK, WIDTH), jnp.bfloat16),
            pltpu.VMEM((3 * BLOCK, WIDTH), jnp.bfloat16),
            pltpu.VMEM((5 * BLOCK, WIDTH), jnp.bfloat16),
            pltpu.VMEM((5 * BLOCK, WIDTH), jnp.bfloat16),
        ],
        compiler_params=pltpu.CompilerParams(vmem_limit_bytes=VMEM_LIMIT),
        cost_estimate=pl.CostEstimate(
            flops=2 * 2 * 15 * BLOCK * WIDTH * WIDTH, bytes_accessed=28 << 20, transcendentals=0
        ),
        name="forward",
    )(*parts, w, gain, seg_col, seg_row)


def backward_kernel(micro, first, *refs):
    flag, g0, g1, g2, w, q_in, k_in, v_in, p_in, pt_in, o_in, x_in, gain_in = refs[:13]
    refs = refs[13 if first else 19 :]
    frame_out, g_out, dq_out, dk_out, dv_out, gain_out = refs[:6]
    g, wv, q, k, v, p, pt, o, x, gain, da, dq, dk, dv, dh, frame, gain_sum, sems = refs[6:]

    @pl.when(flag[0] == 1)
    def _():
        def move(at, source, target):
            copy = pltpu.make_async_copy(source, target, sems.at[at])
            copy.start()
            return copy

        load_g = [
            move(at, part, g.at[pl.ds(at * BLOCK, BLOCK), :]) for at, part in enumerate((g0, g1, g2))
        ]
        load_wo = move(3, w.at[3], wv.at[3])
        load_o = move(4, o_in.at[micro], o)
        load_v = move(5, v_in.at[micro], v)
        load_p = move(6, p_in.at[micro], p)
        load_k = move(7, k_in.at[micro], k)
        load_pt = move(8, pt_in.at[micro], pt)
        load_q = move(9, q_in.at[micro], q)
        load_w = move(10, w.at[pl.ds(0, 3)], wv.at[pl.ds(0, 3)])
        load_x = move(11, x_in.at[micro], x)
        load_gain = move(12, gain_in, gain)
        for copy in load_g:
            copy.wait()
        load_wo.wait()
        store_g = move(13, g.at[pl.ds(0, BLOCK), :], g_out)
        for n in range(0, WIDTH, 256):
            cols = slice(n, n + 256)
            da[:, cols] = dot_nt(g[...], wv[3, cols, :]).astype(jnp.bfloat16)
        for copy in (load_o, load_v, load_p, load_k, load_pt, load_q):
            copy.wait()
        for head in range(HEADS):
            cols = slice(head * HEAD, (head + 1) * HEAD)
            da_h = da[:, cols]
            inner = jnp.sum(da_h.astype(jnp.float32) * o[:, cols], axis=-1, keepdims=True)
            dp = dot_nt(da_h[:BLOCK], v[:, cols])
            ds = (p[head] * (dp - inner[:BLOCK]) * SCALE).astype(jnp.bfloat16)
            dq[:, cols] = dot(ds, k[:, cols]).astype(jnp.bfloat16)
            inner_row = jnp.broadcast_to(inner, (3 * BLOCK, HEAD)).T
            p_t = pt[head]
            dp_t = dot_nt(v[2 * BLOCK :, cols], da_h)
            ds_t = (p_t * (dp_t - inner_row) * SCALE).astype(jnp.bfloat16)
            dk[:, cols] = dot(ds_t, q[:, cols]).astype(jnp.bfloat16)
            dv[:, cols] = dot(p_t.astype(jnp.bfloat16), da_h).astype(jnp.bfloat16)
        stores = [
            store_g,
            move(14, dq, dq_out),
            move(15, dk, dk_out),
            move(16, dv, dv_out),
        ]
        load_w.wait()
        for n in range(0, WIDTH, 256):
            cols = slice(n, n + 256)
            dh[:, cols] = (
                dot_nt(dq[...], wv[0, cols, :])
                + dot_nt(dk[...], wv[1, cols, :])
                + dot_nt(dv[...], wv[2, cols, :])
            )
        load_x.wait()
        load_gain.wait()
        as_float = x[...].astype(jnp.float32)
        rscale = lax.rsqrt(jnp.mean(as_float * as_float, axis=-1, keepdims=True) + 1e-06)
        d_normed = dh[...]
        scaled = gain[0:1, :] * d_normed
        cubic = rscale * rscale * rscale
        frame_f = (
            g[:BLOCK, :].astype(jnp.float32)
            + rscale * scaled
            - as_float * (cubic * jnp.mean(scaled * as_float, axis=-1, keepdims=True))
        )
        frame[...] = frame_f.astype(jnp.bfloat16)
        stores.append(move(17, frame, frame_out))
        term = jnp.sum(d_normed * as_float * rscale, axis=0, keepdims=True)
        gain_sum[...] = jnp.broadcast_to(term, (8, WIDTH))
        stores.append(move(18, gain_sum, gain_out))
        for copy in stores:
            copy.wait()


def backward(micro, flag, incoming, w, kept, x, gain, stash):
    block = jax.ShapeDtypeStruct((BLOCK, WIDTH), jnp.bfloat16)
    outs = [block] * 5 + [jax.ShapeDtypeStruct((8, WIDTH), jnp.float32)]
    first = stash is None
    operands = [flag, *incoming, w, *kept, x, gain] + ([] if first else list(stash))
    anywhere = pl.BlockSpec(memory_space=pl.ANY)
    bf16, f32 = jnp.bfloat16, jnp.float32
    scratch = [
        ((3 * BLOCK, WIDTH), bf16),
        ((4, WIDTH, WIDTH), bf16),
        ((3 * BLOCK, WIDTH), bf16),
        ((3 * BLOCK, WIDTH), bf16),
        ((3 * BLOCK, WIDTH), bf16),
        ((HEADS, BLOCK, 3 * BLOCK), f32),
        ((HEADS, BLOCK, 3 * BLOCK), f32),
        ((3 * BLOCK, WIDTH), f32),
        ((BLOCK, WIDTH), bf16),
        ((8, WIDTH), f32),
        ((3 * BLOCK, WIDTH), bf16),
        ((BLOCK, WIDTH), bf16),
        ((BLOCK, WIDTH), bf16),
        ((BLOCK, WIDTH), bf16),
        ((BLOCK, WIDTH), f32),
        ((BLOCK, WIDTH), bf16),
        ((8, WIDTH), f32),
    ]
    return pl.pallas_call(
        partial(backward_kernel, micro, first),
        in_specs=[pl.BlockSpec(memory_space=pltpu.SMEM)] + [anywhere] * (len(operands) - 1),
        out_specs=[anywhere] * 6,
        out_shape=outs,
        scratch_shapes=[pltpu.VMEM(shape, kind) for shape, kind in scratch]
        + [pltpu.SemaphoreType.DMA((19,))],
        input_output_aliases={} if first else {13 + at: at for at in range(6)},
        compiler_params=pltpu.CompilerParams(vmem_limit_bytes=VMEM_LIMIT),
        cost_estimate=pl.CostEstimate(
            flops=2 * 7 * BLOCK * WIDTH * WIDTH, bytes_accessed=16 << 20, transcendentals=0
        ),
        name="backward",
    )(*operands)


def tie_kernel(*refs):
    del refs


def tie(value, *others):
    anywhere = pl.BlockSpec(memory_space=pl.ANY)
    return pl.pallas_call(
        tie_kernel,
        in_specs=[anywhere] * (1 + len(others)),
        out_specs=anywhere,
        out_shape=jax.ShapeDtypeStruct(value.shape, value.dtype),
        input_output_aliases={0: 0},
        name="tie",
    )(value, *others)


def segments(lengths, block):
    bounds = jnp.cumsum(lengths, axis=1)
    total = lax.axis_size(GROUP) * BLOCK
    places = (block - 2) * BLOCK + jnp.arange(5 * BLOCK, dtype=jnp.int32)
    counted = jnp.sum((places[None, :, None] >= bounds[:, None, :]).astype(jnp.int32), axis=2)
    return jnp.where(places < 0, -1, jnp.where(places >= total, -2, counted))


def body(checkpoints, cotangent, weights, gains, lengths):
    sections, section = lax.axis_size("section"), lax.axis_index("section")
    block = lax.axis_index(GROUP)
    share = gains.shape[1]

    gathered = lax.all_gather(weights[0], GROUP, axis=1, tiled=True)
    spread = lax.dynamic_update_slice(
        jnp.zeros((1, WIDTH), jnp.float32), gains.astype(jnp.float32), (0, block * share)
    )
    gain = jnp.broadcast_to(group_sum(spread), (8, WIDTH))

    x = checkpoints[0]
    left, right = shift(x, 1), shift(x, -1)
    parts = (shift(left, 1), left, x, right, shift(right, -1))
    source = max(sections - 3, 0)
    cot = (cotangent, hop(cotangent, source, sections - 1, 1), hop(cotangent, source, sections - 1, 2))

    segs = segments(lengths, block)
    h, q, k, v, p, pt, o, a = forward(parts, gathered, gain, segs[:, :, None], segs[:, None, :])
    kept = (q, k, v, p, pt, o)

    stash = [None] * MICRO
    incoming = [[part[micro] for part in cot] for micro in range(MICRO)]
    for at in range(sections - 1, -1, -1):
        flag = (section == at).astype(jnp.int32).reshape(1)
        for micro in range(MICRO):
            stash[micro] = list(
                backward(micro, flag, incoming[micro], gathered, kept, x, gain, stash[micro])
            )
            if at > 0:
                if micro > 0:
                    stash[micro][0] = tie(stash[micro][0], *incoming[micro - 1])
                incoming[micro] = [hop(stash[micro][0], at, at - 1, back) for back in range(3)]

    frame, g, dq, dk, dv, gain_part = (
        [stash[micro][at] for micro in range(MICRO)] for at in range(6)
    )
    h, a = h.reshape(-1, WIDTH), a.reshape(-1, WIDTH)
    term = jnp.stack(
        [
            dot_tn(h, jnp.concatenate(dq)),
            dot_tn(h, jnp.concatenate(dk)),
            dot_tn(h, jnp.concatenate(dv)),
            dot_tn(a, jnp.concatenate(g)),
        ]
    )
    weight_part = lax.psum_scatter(
        term.astype(jnp.bfloat16), GROUP, scatter_dimension=1, tiled=True
    ).astype(jnp.float32)
    gain_term = (gain_part[0][0:1] + gain_part[1][0:1]).astype(jnp.bfloat16).astype(jnp.float32)
    gain_sum = lax.dynamic_slice(group_sum(gain_term), (0, block * share), (1, share))
    return (jnp.stack(frame)[None], weight_part[None], gain_sum)


def solution(mesh):
    placed = (
        P("section", None, ("dp", "fsdp"), None),
        P(None, ("dp", "fsdp"), None),
        P("section", None, ("dp", "fsdp"), None),
        P("section", ("dp", "fsdp")),
        P(),
    )
    return jax.shard_map(
        body,
        mesh=mesh,
        in_specs=placed,
        out_specs=(
            P("section", None, ("dp", "fsdp"), None),
            P("section", None, ("dp", "fsdp"), None),
            P("section", ("dp", "fsdp")),
        ),
        check_vma=False,
    )
```

```python
from functools import partial
import math

import jax
import jax.numpy as jnp
from jax import lax
from jax.experimental import pallas as pl
from jax.experimental.pallas import tpu as pltpu
from jax.sharding import PartitionSpec as P

HEAD = 128
BLOCK = 128
WIDTH = 1024
HEADS = WIDTH // HEAD
MICRO = 2
SCALE = 1.0 / math.sqrt(HEAD)
GROUP = ("dp", "fsdp")
EVERY = ("dp", "section", "fsdp")
VMEM_LIMIT = 52 * 1024 * 1024


def dot(left, right):
    return lax.dot_general(left, right, (((1,), (0,)), ((), ())), preferred_element_type=jnp.float32)


def dot_nt(left, right):
    return lax.dot_general(left, right, (((1,), (1,)), ((), ())), preferred_element_type=jnp.float32)


def dot_tn(left, right):
    return lax.dot_general(left, right, (((0,), (0,)), ((), ())), preferred_element_type=jnp.float32)


def shift(value, steps):
    count = lax.axis_size(GROUP)
    pairs = [(b, b + steps) for b in range(count) if 0 <= b + steps < count]
    return lax.ppermute(value, GROUP, pairs)


def hop(value, source, target, back):
    sections, rows = lax.axis_size("section"), lax.axis_size("fsdp")
    count = lax.axis_size(GROUP)

    def place(section, block):
        return (block // rows * sections + section) * rows + block % rows

    pairs = [(place(source, b), place(target, b - back)) for b in range(back, count)]
    return lax.ppermute(value, EVERY, pairs)


def group_dims():
    dp, fsdp = lax.axis_size("dp"), lax.axis_size("fsdp")
    planes = 2 if dp % 2 == 0 else 1
    return (planes, dp // planes, fsdp)


def turn(value, axis, steps):
    dims = group_dims()
    pairs = []
    for z in range(dims[0]):
        for y in range(dims[1]):
            for x in range(dims[2]):
                at = [z, y, x]
                to = list(at)
                to[axis] = (at[axis] + steps) % dims[axis]
                index = lambda p: (p[0] * dims[1] + p[1]) * dims[2] + p[2]
                pairs.append((index(at), index(to)))
    return lax.ppermute(value, GROUP, pairs)


def group_sum(value):
    for axis, size in enumerate(group_dims()):
        moving = value
        for _ in range(size - 1):
            moving = turn(moving, axis, 1)
            value = value + moving
    return value


def tie_kernel(*refs):
    del refs


def tie(value, *others):
    anywhere = pl.BlockSpec(memory_space=pl.ANY)
    return pl.pallas_call(
        tie_kernel,
        in_specs=[anywhere] * (1 + len(others)),
        out_specs=anywhere,
        out_shape=jax.ShapeDtypeStruct(value.shape, value.dtype),
        input_output_aliases={0: 0},
        name="tie",
    )(value, *others)


def ring(value, axis):
    size, rows = group_dims()[axis], value.shape[0]
    pieces = [(0, 0, value)]
    if size == 2:
        pieces.append((1, 0, turn(value, axis, 1)))
    if size == 4:
        half = rows // 2
        behind, ahead = turn(value, axis, 1), turn(value, axis, -1)
        pieces.append((1, 0, ahead))
        pieces.append((2, 0, turn(behind[:half], axis, 1)))
        pieces.append((2, half, turn(ahead[half:], axis, -1)))
        pieces.append((3, 0, behind))
    return pieces


def gather_weights(shard):
    pair = ring(shard[None], 0)
    firsts = []
    for part, axis in zip((slice(0, 2), slice(2, 4)), (1, 2)):
        value = jnp.concatenate([piece[:, part] for _, _, piece in pair])
        firsts.append(jnp.concatenate([piece for _, _, piece in ring(value, axis)]))
    firsts = [tie(firsts[0], firsts[1]), tie(firsts[1], firsts[0])]
    return [ring(first, axis) for first, axis in zip(firsts, (2, 1))]


def normed(x, gain):
    as_float = x.astype(jnp.float32)
    rscale = lax.rsqrt(jnp.mean(as_float * as_float, axis=-1, keepdims=True) + 1e-06)
    return (as_float * rscale * gain).astype(jnp.bfloat16)


def forward_kernel(layout, dims, *refs):
    count = sum(len(pieces) for pieces in layout)
    spot, pieces, refs = refs[0], refs[1 : 1 + count], refs[1 + count :]
    l2, l1, own, r1, r2, gain, seg_col, seg_row = refs[:8]
    w_out, h_out, q_out, k_out, v_out, p_out, pt_out, o_out, a_out = refs[8:17]
    w, h5, q3, k5, v5, sems = refs[17:]
    step = pl.program_id(0)
    planes, size_y, size_x = dims
    z, y, x = spot[0], spot[1], spot[2]

    def loads(pair):
        copies, offset = [], sum(len(pieces) for pieces in layout[:pair])
        for at, (place, first, rows) in enumerate(layout[pair]):
            for row in range(rows):
                one, plane = divmod(first + row, planes)
                ahead_y, ahead_x = (one, place) if pair == 0 else (place, one)
                to = lax.rem(z + plane, planes) * size_y + lax.rem(y + ahead_y, size_y)
                to = to * size_x + lax.rem(x + ahead_x, size_x)
                share = WIDTH // (planes * size_y * size_x)
                target = w.at[pl.ds(2 * pair, 2), pl.ds(pl.multiple_of(to * share, share), share), :]
                copies.append(
                    pltpu.make_async_copy(
                        pieces[offset + at].at[row], target, sems.at[pair, len(copies)]
                    )
                )
        return copies

    def store(pair):
        half = pl.ds(2 * pair, 2)
        return pltpu.make_async_copy(w.at[half], w_out.at[half], sems.at[2, pair])

    @pl.when(step == 0)
    def _():
        for copy in loads(0) + loads(1):
            copy.start()

    gain_row = gain[0:1, :]
    for at, part in enumerate((l2, l1, own, r1, r2)):
        h5[at * BLOCK : (at + 1) * BLOCK, :] = normed(part[0], gain_row)
    h_out[0] = h5[2 * BLOCK : 3 * BLOCK, :]

    @pl.when(step == 0)
    def _():
        for copy in loads(0):
            copy.wait()
        store(0).start()

    for n in range(0, WIDTH, 256):
        cols = slice(n, n + 256)
        q3[:, cols] = dot(h5[2 * BLOCK :, :], w[0, :, cols]).astype(jnp.bfloat16)
        k5[:, cols] = dot(h5[...], w[1, :, cols]).astype(jnp.bfloat16)

    @pl.when(step == 0)
    def _():
        for copy in loads(1):
            copy.wait()
        store(1).start()

    for n in range(0, WIDTH, 256):
        cols = slice(n, n + 256)
        v5[:, cols] = dot(h5[...], w[2, :, cols]).astype(jnp.bfloat16)
    q_out[0] = q3[...]
    k_out[0] = k5[: 3 * BLOCK, :]
    v_out[0] = v5[: 3 * BLOCK, :]
    for head in range(HEADS):
        cols = slice(head * HEAD, (head + 1) * HEAD)
        for j in range(3):
            rows = slice(j * BLOCK, (j + 1) * BLOCK)
            keys = slice(j * BLOCK, (j + 3) * BLOCK)
            allowed = seg_col[0, (j + 2) * BLOCK : (j + 3) * BLOCK, 0:1] == seg_row[0, 0:1, keys]
            score = jnp.where(allowed, dot_nt(q3[rows, cols], k5[keys, cols]), -1e30)
            top = jnp.max(score, axis=-1, keepdims=True)
            expo = jnp.exp((score - top) * SCALE)
            p = expo * (1.0 / jnp.sum(expo, axis=-1, keepdims=True))
            high = p.astype(jnp.bfloat16)
            low = (p - high.astype(jnp.float32)).astype(jnp.bfloat16)
            values = v5[keys, cols]
            mixed = dot(high, values)
            o_out[0, rows, cols] = mixed + dot(low, values)
            if j == 0:
                p_out[0, head] = p
                a_out[0, :, cols] = mixed.astype(jnp.bfloat16)
            pt_out[0, head, :, rows] = p[:, (2 - j) * BLOCK : (3 - j) * BLOCK].T

    @pl.when(step == MICRO - 1)
    def _():
        store(0).wait()
        store(1).wait()


def forward(spot, pairs, parts, gain, seg_col, seg_row):
    anywhere = pl.BlockSpec(memory_space=pl.ANY)
    pieces = [piece for pair in pairs for _, _, piece in pair]
    layout = [[(place, first, piece.shape[0]) for place, first, piece in pair] for pair in pairs]
    dims = group_dims()
    most = dims[0] * dims[1] * dims[2]

    def per_micro(shape):
        return pl.BlockSpec((1,) + shape, lambda m: (m,) + (0,) * len(shape))

    def whole(shape):
        return pl.BlockSpec(shape, lambda m: (0,) * len(shape), pipeline_mode=pl.Buffered(1))

    outs = [
        ((BLOCK, WIDTH), jnp.bfloat16),
        ((3 * BLOCK, WIDTH), jnp.bfloat16),
        ((3 * BLOCK, WIDTH), jnp.bfloat16),
        ((3 * BLOCK, WIDTH), jnp.bfloat16),
        ((HEADS, BLOCK, 3 * BLOCK), jnp.float32),
        ((HEADS, BLOCK, 3 * BLOCK), jnp.float32),
        ((3 * BLOCK, WIDTH), jnp.float32),
        ((BLOCK, WIDTH), jnp.bfloat16),
    ]
    return pl.pallas_call(
        partial(forward_kernel, layout, dims),
        grid=(MICRO,),
        in_specs=[pl.BlockSpec(memory_space=pltpu.SMEM)]
        + [anywhere] * len(pieces)
        + [per_micro((BLOCK, WIDTH))] * 5
        + [
            whole((8, WIDTH)),
            per_micro((5 * BLOCK, 1)),
            per_micro((1, 5 * BLOCK)),
        ],
        out_specs=[anywhere] + [per_micro(shape) for shape, _ in outs],
        out_shape=[jax.ShapeDtypeStruct((4, WIDTH, WIDTH), jnp.bfloat16)]
        + [jax.ShapeDtypeStruct((MICRO,) + shape, kind) for shape, kind in outs],
        scratch_shapes=[
            pltpu.VMEM((4, WIDTH, WIDTH), jnp.bfloat16),
            pltpu.VMEM((5 * BLOCK, WIDTH), jnp.bfloat16),
            pltpu.VMEM((3 * BLOCK, WIDTH), jnp.bfloat16),
            pltpu.VMEM((5 * BLOCK, WIDTH), jnp.bfloat16),
            pltpu.VMEM((5 * BLOCK, WIDTH), jnp.bfloat16),
            pltpu.SemaphoreType.DMA((3, most)),
        ],
        compiler_params=pltpu.CompilerParams(vmem_limit_bytes=VMEM_LIMIT),
        cost_estimate=pl.CostEstimate(
            flops=2 * 2 * 15 * BLOCK * WIDTH * WIDTH, bytes_accessed=28 << 20, transcendentals=0
        ),
        name="forward",
    )(spot, *pieces, *parts, gain, seg_col, seg_row)


def backward_kernel(micro, first, *refs):
    flag, g0, g1, g2, w, q_in, k_in, v_in, p_in, pt_in, o_in, x_in, gain_in = refs[:13]
    refs = refs[13 if first else 19 :]
    frame_out, g_out, dq_out, dk_out, dv_out, gain_out = refs[:6]
    g, wv, q, k, v, p, pt, o, x, gain, da, dq, dk, dv, dh, frame, gain_sum, sems = refs[6:]

    @pl.when(flag[0] == 1)
    def _():
        def move(at, source, target):
            copy = pltpu.make_async_copy(source, target, sems.at[at])
            copy.start()
            return copy

        load_g = [
            move(at, part, g.at[pl.ds(at * BLOCK, BLOCK), :]) for at, part in enumerate((g0, g1, g2))
        ]
        load_wo = move(3, w.at[3], wv.at[3])
        load_o = move(4, o_in.at[micro], o)
        load_v = move(5, v_in.at[micro], v)
        load_p = move(6, p_in.at[micro], p)
        load_k = move(7, k_in.at[micro], k)
        load_pt = move(8, pt_in.at[micro], pt)
        load_q = move(9, q_in.at[micro], q)
        load_w = move(10, w.at[pl.ds(0, 3)], wv.at[pl.ds(0, 3)])
        load_x = move(11, x_in.at[micro], x)
        load_gain = move(12, gain_in, gain)
        for copy in load_g:
            copy.wait()
        load_wo.wait()
        store_g = move(13, g.at[pl.ds(0, BLOCK), :], g_out)
        for n in range(0, WIDTH, 256):
            cols = slice(n, n + 256)
            da[:, cols] = dot_nt(g[...], wv[3, cols, :]).astype(jnp.bfloat16)
        for copy in (load_o, load_v, load_p, load_k, load_pt, load_q):
            copy.wait()
        for head in range(HEADS):
            cols = slice(head * HEAD, (head + 1) * HEAD)
            da_h = da[:, cols]
            inner = jnp.sum(da_h.astype(jnp.float32) * o[:, cols], axis=-1, keepdims=True)
            dp = dot_nt(da_h[:BLOCK], v[:, cols])
            ds = (p[head] * (dp - inner[:BLOCK]) * SCALE).astype(jnp.bfloat16)
            dq[:, cols] = dot(ds, k[:, cols]).astype(jnp.bfloat16)
            inner_row = jnp.broadcast_to(inner, (3 * BLOCK, HEAD)).T
            p_t = pt[head]
            dp_t = dot_nt(v[2 * BLOCK :, cols], da_h)
            ds_t = (p_t * (dp_t - inner_row) * SCALE).astype(jnp.bfloat16)
            dk[:, cols] = dot(ds_t, q[:, cols]).astype(jnp.bfloat16)
            dv[:, cols] = dot(p_t.astype(jnp.bfloat16), da_h).astype(jnp.bfloat16)
        stores = [
            store_g,
            move(14, dq, dq_out),
            move(15, dk, dk_out),
            move(16, dv, dv_out),
        ]
        load_w.wait()
        for n in range(0, WIDTH, 256):
            cols = slice(n, n + 256)
            dh[:, cols] = (
                dot_nt(dq[...], wv[0, cols, :])
                + dot_nt(dk[...], wv[1, cols, :])
                + dot_nt(dv[...], wv[2, cols, :])
            )
        load_x.wait()
        load_gain.wait()
        as_float = x[...].astype(jnp.float32)
        rscale = lax.rsqrt(jnp.mean(as_float * as_float, axis=-1, keepdims=True) + 1e-06)
        d_normed = dh[...]
        scaled = gain[0:1, :] * d_normed
        cubic = rscale * rscale * rscale
        frame_f = (
            g[:BLOCK, :].astype(jnp.float32)
            + rscale * scaled
            - as_float * (cubic * jnp.mean(scaled * as_float, axis=-1, keepdims=True))
        )
        frame[...] = frame_f.astype(jnp.bfloat16)
        stores.append(move(17, frame, frame_out))
        term = jnp.sum(d_normed * as_float * rscale, axis=0, keepdims=True)
        gain_sum[...] = jnp.broadcast_to(term, (8, WIDTH))
        stores.append(move(18, gain_sum, gain_out))
        for copy in stores:
            copy.wait()


def backward(micro, flag, incoming, w, kept, x, gain, stash):
    block = jax.ShapeDtypeStruct((BLOCK, WIDTH), jnp.bfloat16)
    outs = [block] * 5 + [jax.ShapeDtypeStruct((8, WIDTH), jnp.float32)]
    first = stash is None
    operands = [flag, *incoming, w, *kept, x, gain] + ([] if first else list(stash))
    anywhere = pl.BlockSpec(memory_space=pl.ANY)
    bf16, f32 = jnp.bfloat16, jnp.float32
    scratch = [
        ((3 * BLOCK, WIDTH), bf16),
        ((4, WIDTH, WIDTH), bf16),
        ((3 * BLOCK, WIDTH), bf16),
        ((3 * BLOCK, WIDTH), bf16),
        ((3 * BLOCK, WIDTH), bf16),
        ((HEADS, BLOCK, 3 * BLOCK), f32),
        ((HEADS, BLOCK, 3 * BLOCK), f32),
        ((3 * BLOCK, WIDTH), f32),
        ((BLOCK, WIDTH), bf16),
        ((8, WIDTH), f32),
        ((3 * BLOCK, WIDTH), bf16),
        ((BLOCK, WIDTH), bf16),
        ((BLOCK, WIDTH), bf16),
        ((BLOCK, WIDTH), bf16),
        ((BLOCK, WIDTH), f32),
        ((BLOCK, WIDTH), bf16),
        ((8, WIDTH), f32),
    ]
    return pl.pallas_call(
        partial(backward_kernel, micro, first),
        in_specs=[pl.BlockSpec(memory_space=pltpu.SMEM)] + [anywhere] * (len(operands) - 1),
        out_specs=[anywhere] * 6,
        out_shape=outs,
        scratch_shapes=[pltpu.VMEM(shape, kind) for shape, kind in scratch]
        + [pltpu.SemaphoreType.DMA((19,))],
        input_output_aliases={} if first else {13 + at: at for at in range(6)},
        compiler_params=pltpu.CompilerParams(vmem_limit_bytes=VMEM_LIMIT),
        cost_estimate=pl.CostEstimate(
            flops=2 * 7 * BLOCK * WIDTH * WIDTH, bytes_accessed=16 << 20, transcendentals=0
        ),
        name="backward",
    )(*operands)


def segments(lengths, block):
    bounds = jnp.cumsum(lengths, axis=1)
    total = lax.axis_size(GROUP) * BLOCK
    places = (block - 2) * BLOCK + jnp.arange(5 * BLOCK, dtype=jnp.int32)
    counted = jnp.sum((places[None, :, None] >= bounds[:, None, :]).astype(jnp.int32), axis=2)
    return jnp.where(places < 0, -1, jnp.where(places >= total, -2, counted))


def body(checkpoints, cotangent, weights, gains, lengths):
    sections, section = lax.axis_size("section"), lax.axis_index("section")
    block = lax.axis_index(GROUP)
    share = gains.shape[1]

    pairs = gather_weights(weights[0])
    planes, size_y, _ = group_dims()
    dp = lax.axis_index("dp")
    spot = jnp.stack([dp // size_y, dp % size_y, lax.axis_index("fsdp")]).astype(jnp.int32)
    spread = lax.dynamic_update_slice(
        jnp.zeros((1, WIDTH), jnp.float32), gains.astype(jnp.float32), (0, block * share)
    )
    gain = jnp.broadcast_to(group_sum(spread), (8, WIDTH))

    x = checkpoints[0]
    left, right = shift(x, 1), shift(x, -1)
    parts = (shift(left, 1), left, x, right, shift(right, -1))
    source = max(sections - 3, 0)
    cot = (cotangent, hop(cotangent, source, sections - 1, 1), hop(cotangent, source, sections - 1, 2))

    segs = segments(lengths, block)
    gathered, h, q, k, v, p, pt, o, a = forward(
        spot, pairs, parts, gain, segs[:, :, None], segs[:, None, :]
    )
    kept = (q, k, v, p, pt, o)

    stash = [None] * MICRO
    incoming = [[part[micro] for part in cot] for micro in range(MICRO)]
    for at in range(sections - 1, -1, -1):
        flag = (section == at).astype(jnp.int32).reshape(1)
        for micro in range(MICRO):
            stash[micro] = list(
                backward(micro, flag, incoming[micro], gathered, kept, x, gain, stash[micro])
            )
            if at > 0:
                if micro > 0:
                    stash[micro][0] = tie(stash[micro][0], *incoming[micro - 1])
                incoming[micro] = [hop(stash[micro][0], at, at - 1, back) for back in range(3)]

    frame, g, dq, dk, dv, gain_part = (
        [stash[micro][at] for micro in range(MICRO)] for at in range(6)
    )
    h, a = h.reshape(-1, WIDTH), a.reshape(-1, WIDTH)
    term = jnp.stack(
        [
            dot_tn(h, jnp.concatenate(dq)),
            dot_tn(h, jnp.concatenate(dk)),
            dot_tn(h, jnp.concatenate(dv)),
            dot_tn(a, jnp.concatenate(g)),
        ]
    )
    weight_part = lax.psum_scatter(
        term.astype(jnp.bfloat16), GROUP, scatter_dimension=1, tiled=True
    ).astype(jnp.float32)
    gain_term = (gain_part[0][0:1] + gain_part[1][0:1]).astype(jnp.bfloat16).astype(jnp.float32)
    gain_sum = lax.dynamic_slice(group_sum(gain_term), (0, block * share), (1, share))
    return (jnp.stack(frame)[None], weight_part[None], gain_sum)


def solution(mesh):
    placed = (
        P("section", None, ("dp", "fsdp"), None),
        P(None, ("dp", "fsdp"), None),
        P("section", None, ("dp", "fsdp"), None),
        P("section", ("dp", "fsdp")),
        P(),
    )
    return jax.shard_map(
        body,
        mesh=mesh,
        in_specs=placed,
        out_specs=(
            P("section", None, ("dp", "fsdp"), None),
            P("section", None, ("dp", "fsdp"), None),
            P("section", ("dp", "fsdp")),
        ),
        check_vma=False,
    )
```

```python
from functools import partial
import math

import jax
import jax.numpy as jnp
from jax import lax
from jax.experimental import pallas as pl
from jax.experimental.pallas import tpu as pltpu
from jax.sharding import PartitionSpec as P

HEAD = 128
BLOCK = 128
WIDTH = 1024
HEADS = WIDTH // HEAD
MICRO = 2
SCALE = 1.0 / math.sqrt(HEAD)
GROUP = ("dp", "fsdp")
EVERY = ("dp", "section", "fsdp")
VMEM_LIMIT = 52 * 1024 * 1024


def dot(left, right):
    return lax.dot_general(left, right, (((1,), (0,)), ((), ())), preferred_element_type=jnp.float32)


def dot_nt(left, right):
    return lax.dot_general(left, right, (((1,), (1,)), ((), ())), preferred_element_type=jnp.float32)


def dot_tn(left, right):
    return lax.dot_general(left, right, (((0,), (0,)), ((), ())), preferred_element_type=jnp.float32)


def shift(value, steps):
    count = lax.axis_size(GROUP)
    pairs = [(b, b + steps) for b in range(count) if 0 <= b + steps < count]
    return lax.ppermute(value, GROUP, pairs)


def hop(value, source, target, back):
    sections, rows = lax.axis_size("section"), lax.axis_size("fsdp")
    count = lax.axis_size(GROUP)

    def place(section, block):
        return (block // rows * sections + section) * rows + block % rows

    pairs = [(place(source, b), place(target, b - back)) for b in range(back, count)]
    return lax.ppermute(value, EVERY, pairs)


def group_dims():
    dp, fsdp = lax.axis_size("dp"), lax.axis_size("fsdp")
    planes = 2 if dp % 2 == 0 else 1
    return (planes, dp // planes, fsdp)


def turn(value, axis, steps):
    dims = group_dims()
    pairs = []
    for z in range(dims[0]):
        for y in range(dims[1]):
            for x in range(dims[2]):
                at = [z, y, x]
                to = list(at)
                to[axis] = (at[axis] + steps) % dims[axis]
                index = lambda p: (p[0] * dims[1] + p[1]) * dims[2] + p[2]
                pairs.append((index(at), index(to)))
    return lax.ppermute(value, GROUP, pairs)


def tie_kernel(*refs):
    del refs


def tie(value, *others):
    anywhere = pl.BlockSpec(memory_space=pl.ANY)
    return pl.pallas_call(
        tie_kernel,
        in_specs=[anywhere] * (1 + len(others)),
        out_specs=anywhere,
        out_shape=jax.ShapeDtypeStruct(value.shape, value.dtype),
        input_output_aliases={0: 0},
        name="tie",
    )(value, *others)


def ring(value, axis):
    size, rows = group_dims()[axis], value.shape[0]
    pieces = [(0, 0, value)]
    if size == 2:
        pieces.append((1, 0, turn(value, axis, 1)))
    if size == 4:
        half = rows // 2
        behind, ahead = turn(value, axis, 1), turn(value, axis, -1)
        pieces.append((1, 0, ahead))
        pieces.append((2, 0, turn(behind[:half], axis, 1)))
        pieces.append((2, half, turn(ahead[half:], axis, -1)))
        pieces.append((3, 0, behind))
    return pieces


def gather_weights(shard):
    pair = ring(shard[None], 0)
    firsts = []
    for part, axis in zip((slice(0, 2), slice(2, 4)), (1, 2)):
        value = jnp.concatenate([piece[:, part] for _, _, piece in pair])
        firsts.append(jnp.concatenate([piece for _, _, piece in ring(value, axis)]))
    firsts = [tie(firsts[0], firsts[1]), tie(firsts[1], firsts[0])]
    return [ring(first, axis) for first, axis in zip(firsts, (2, 1))]


def normed(x, gain):
    as_float = x.astype(jnp.float32)
    rscale = lax.rsqrt(jnp.mean(as_float * as_float, axis=-1, keepdims=True) + 1e-06)
    return (as_float * rscale * gain).astype(jnp.bfloat16)


def forward_kernel(layout, dims, *refs):
    count = sum(len(pieces) for pieces in layout)
    spot, pieces, refs = refs[0], refs[1 : 1 + count], refs[1 + count :]
    l2, l1, own, r1, r2, gain, seg_col, seg_row = refs[:8]
    w_out, h_out, q_out, k_out, v_out, p_out, pt_out, o_out, a_out = refs[8:17]
    w, h5, q3, k5, v5, sems = refs[17:]
    step = pl.program_id(0)
    planes, size_y, size_x = dims
    z, y, x = spot[0], spot[1], spot[2]

    def loads(pair):
        copies, offset = [], sum(len(pieces) for pieces in layout[:pair])
        for at, (place, first, rows) in enumerate(layout[pair]):
            for row in range(rows):
                one, plane = divmod(first + row, planes)
                ahead_y, ahead_x = (one, place) if pair == 0 else (place, one)
                to = lax.rem(z + plane, planes) * size_y + lax.rem(y + ahead_y, size_y)
                to = to * size_x + lax.rem(x + ahead_x, size_x)
                share = WIDTH // (planes * size_y * size_x)
                target = w.at[pl.ds(2 * pair, 2), pl.ds(pl.multiple_of(to * share, share), share), :]
                copies.append(
                    pltpu.make_async_copy(
                        pieces[offset + at].at[row], target, sems.at[pair, len(copies)]
                    )
                )
        return copies

    def store(pair):
        half = pl.ds(2 * pair, 2)
        return pltpu.make_async_copy(w.at[half], w_out.at[half], sems.at[2, pair])

    @pl.when(step == 0)
    def _():
        for copy in loads(0) + loads(1):
            copy.start()

    gain_row = gain[0:1, :]
    for at, part in enumerate((l2, l1, own, r1, r2)):
        h5[at * BLOCK : (at + 1) * BLOCK, :] = normed(part[0], gain_row)
    h_out[0] = h5[2 * BLOCK : 3 * BLOCK, :]

    @pl.when(step == 0)
    def _():
        for copy in loads(0):
            copy.wait()
        store(0).start()

    for n in range(0, WIDTH, 256):
        cols = slice(n, n + 256)
        q3[:, cols] = dot(h5[2 * BLOCK :, :], w[0, :, cols]).astype(jnp.bfloat16)
        k5[:, cols] = dot(h5[...], w[1, :, cols]).astype(jnp.bfloat16)

    @pl.when(step == 0)
    def _():
        for copy in loads(1):
            copy.wait()
        store(1).start()

    for n in range(0, WIDTH, 256):
        cols = slice(n, n + 256)
        v5[:, cols] = dot(h5[...], w[2, :, cols]).astype(jnp.bfloat16)
    q_out[0] = q3[...]
    k_out[0] = k5[: 3 * BLOCK, :]
    v_out[0] = v5[: 3 * BLOCK, :]
    for head in range(HEADS):
        cols = slice(head * HEAD, (head + 1) * HEAD)
        for j in range(3):
            rows = slice(j * BLOCK, (j + 1) * BLOCK)
            keys = slice(j * BLOCK, (j + 3) * BLOCK)
            allowed = seg_col[0, (j + 2) * BLOCK : (j + 3) * BLOCK, 0:1] == seg_row[0, 0:1, keys]
            score = jnp.where(allowed, dot_nt(q3[rows, cols], k5[keys, cols]), -1e30)
            top = jnp.max(score, axis=-1, keepdims=True)
            expo = jnp.exp((score - top) * SCALE)
            p = expo * (1.0 / jnp.sum(expo, axis=-1, keepdims=True))
            high = p.astype(jnp.bfloat16)
            low = (p - high.astype(jnp.float32)).astype(jnp.bfloat16)
            values = v5[keys, cols]
            mixed = dot(high, values)
            o_out[0, rows, cols] = mixed + dot(low, values)
            if j == 0:
                p_out[0, head] = p
                a_out[0, :, cols] = mixed.astype(jnp.bfloat16)
            pt_out[0, head, :, rows] = p[:, (2 - j) * BLOCK : (3 - j) * BLOCK].T

    @pl.when(step == MICRO - 1)
    def _():
        store(0).wait()
        store(1).wait()


def forward(spot, pairs, parts, gain, seg_col, seg_row):
    anywhere = pl.BlockSpec(memory_space=pl.ANY)
    pieces = [piece for pair in pairs for _, _, piece in pair]
    layout = [[(place, first, piece.shape[0]) for place, first, piece in pair] for pair in pairs]
    dims = group_dims()
    most = dims[0] * dims[1] * dims[2]

    def per_micro(shape):
        return pl.BlockSpec((1,) + shape, lambda m: (m,) + (0,) * len(shape))

    def whole(shape):
        return pl.BlockSpec(shape, lambda m: (0,) * len(shape), pipeline_mode=pl.Buffered(1))

    outs = [
        ((BLOCK, WIDTH), jnp.bfloat16),
        ((3 * BLOCK, WIDTH), jnp.bfloat16),
        ((3 * BLOCK, WIDTH), jnp.bfloat16),
        ((3 * BLOCK, WIDTH), jnp.bfloat16),
        ((HEADS, BLOCK, 3 * BLOCK), jnp.float32),
        ((HEADS, BLOCK, 3 * BLOCK), jnp.float32),
        ((3 * BLOCK, WIDTH), jnp.float32),
        ((BLOCK, WIDTH), jnp.bfloat16),
    ]
    return pl.pallas_call(
        partial(forward_kernel, layout, dims),
        grid=(MICRO,),
        in_specs=[pl.BlockSpec(memory_space=pltpu.SMEM)]
        + [anywhere] * len(pieces)
        + [per_micro((BLOCK, WIDTH))] * 5
        + [
            whole((8, WIDTH)),
            per_micro((5 * BLOCK, 1)),
            per_micro((1, 5 * BLOCK)),
        ],
        out_specs=[anywhere] + [per_micro(shape) for shape, _ in outs],
        out_shape=[jax.ShapeDtypeStruct((4, WIDTH, WIDTH), jnp.bfloat16)]
        + [jax.ShapeDtypeStruct((MICRO,) + shape, kind) for shape, kind in outs],
        scratch_shapes=[
            pltpu.VMEM((4, WIDTH, WIDTH), jnp.bfloat16),
            pltpu.VMEM((5 * BLOCK, WIDTH), jnp.bfloat16),
            pltpu.VMEM((3 * BLOCK, WIDTH), jnp.bfloat16),
            pltpu.VMEM((5 * BLOCK, WIDTH), jnp.bfloat16),
            pltpu.VMEM((5 * BLOCK, WIDTH), jnp.bfloat16),
            pltpu.SemaphoreType.DMA((3, most)),
        ],
        compiler_params=pltpu.CompilerParams(vmem_limit_bytes=VMEM_LIMIT),
        cost_estimate=pl.CostEstimate(
            flops=2 * 2 * 15 * BLOCK * WIDTH * WIDTH, bytes_accessed=28 << 20, transcendentals=0
        ),
        name="forward",
    )(spot, *pieces, *parts, gain, seg_col, seg_row)


def backward_kernel(micro, *refs):
    flag, g0, g1, g2, w, q_in, k_in, v_in, p_in, pt_in, o_in, x_in, gain_in = refs[:13]
    refs = refs[13:]
    frame_out, g_out, dq_out, dk_out, dv_out, gain_out = refs[:6]
    g, wv, q, k, v, p, pt, o, x, gain, da, dq, dk, dv, dh, frame, gain_sum, sems = refs[6:]

    @pl.when(flag[0] == 1)
    def _():
        def move(at, source, target):
            copy = pltpu.make_async_copy(source, target, sems.at[at])
            copy.start()
            return copy

        load_g = [
            move(at, part, g.at[pl.ds(at * BLOCK, BLOCK), :]) for at, part in enumerate((g0, g1, g2))
        ]
        load_wo = move(3, w.at[3], wv.at[3])
        load_o = move(4, o_in.at[micro], o)
        load_v = move(5, v_in.at[micro], v)
        load_p = move(6, p_in.at[micro], p)
        load_k = move(7, k_in.at[micro], k)
        load_pt = move(8, pt_in.at[micro], pt)
        load_q = move(9, q_in.at[micro], q)
        load_w = move(10, w.at[pl.ds(0, 3)], wv.at[pl.ds(0, 3)])
        load_x = move(11, x_in.at[micro], x)
        load_gain = move(12, gain_in, gain)
        for copy in load_g:
            copy.wait()
        load_wo.wait()
        store_g = move(13, g.at[pl.ds(0, BLOCK), :], g_out)
        for n in range(0, WIDTH, 256):
            cols = slice(n, n + 256)
            da[:, cols] = dot_nt(g[...], wv[3, cols, :]).astype(jnp.bfloat16)
        for copy in (load_o, load_v, load_p, load_k, load_pt, load_q):
            copy.wait()
        for head in range(HEADS):
            cols = slice(head * HEAD, (head + 1) * HEAD)
            da_h = da[:, cols]
            inner = jnp.sum(da_h.astype(jnp.float32) * o[:, cols], axis=-1, keepdims=True)
            dp = dot_nt(da_h[:BLOCK], v[:, cols])
            ds = (p[head] * (dp - inner[:BLOCK]) * SCALE).astype(jnp.bfloat16)
            dq[:, cols] = dot(ds, k[:, cols]).astype(jnp.bfloat16)
            inner_row = jnp.broadcast_to(inner, (3 * BLOCK, HEAD)).T
            p_t = pt[head]
            dp_t = dot_nt(v[2 * BLOCK :, cols], da_h)
            ds_t = (p_t * (dp_t - inner_row) * SCALE).astype(jnp.bfloat16)
            dk[:, cols] = dot(ds_t, q[:, cols]).astype(jnp.bfloat16)
            dv[:, cols] = dot(p_t.astype(jnp.bfloat16), da_h).astype(jnp.bfloat16)
        stores = [
            store_g,
            move(14, dq, dq_out),
            move(15, dk, dk_out),
            move(16, dv, dv_out),
        ]
        load_w.wait()
        for n in range(0, WIDTH, 256):
            cols = slice(n, n + 256)
            dh[:, cols] = (
                dot_nt(dq[...], wv[0, cols, :])
                + dot_nt(dk[...], wv[1, cols, :])
                + dot_nt(dv[...], wv[2, cols, :])
            )
        load_x.wait()
        load_gain.wait()
        as_float = x[...].astype(jnp.float32)
        rscale = lax.rsqrt(jnp.mean(as_float * as_float, axis=-1, keepdims=True) + 1e-06)
        d_normed = dh[...]
        scaled = gain[0:1, :] * d_normed
        cubic = rscale * rscale * rscale
        frame_f = (
            g[:BLOCK, :].astype(jnp.float32)
            + rscale * scaled
            - as_float * (cubic * jnp.mean(scaled * as_float, axis=-1, keepdims=True))
        )
        frame[...] = frame_f.astype(jnp.bfloat16)
        stores.append(move(17, frame, frame_out))
        term = jnp.sum(d_normed * as_float * rscale, axis=0, keepdims=True)
        gain_sum[...] = jnp.broadcast_to(term, (8, WIDTH))
        stores.append(move(18, gain_sum, gain_out))
        for copy in stores:
            copy.wait()


def backward(micro, flag, incoming, w, kept, x, gain):
    block = jax.ShapeDtypeStruct((BLOCK, WIDTH), jnp.bfloat16)
    outs = [block] * 5 + [jax.ShapeDtypeStruct((8, WIDTH), jnp.float32)]
    operands = [flag, *incoming, w, *kept, x, gain]
    anywhere = pl.BlockSpec(memory_space=pl.ANY)
    in_hbm = pl.BlockSpec(memory_space=pltpu.HBM)
    bf16, f32 = jnp.bfloat16, jnp.float32
    scratch = [
        ((3 * BLOCK, WIDTH), bf16),
        ((4, WIDTH, WIDTH), bf16),
        ((3 * BLOCK, WIDTH), bf16),
        ((3 * BLOCK, WIDTH), bf16),
        ((3 * BLOCK, WIDTH), bf16),
        ((HEADS, BLOCK, 3 * BLOCK), f32),
        ((HEADS, BLOCK, 3 * BLOCK), f32),
        ((3 * BLOCK, WIDTH), f32),
        ((BLOCK, WIDTH), bf16),
        ((8, WIDTH), f32),
        ((3 * BLOCK, WIDTH), bf16),
        ((BLOCK, WIDTH), bf16),
        ((BLOCK, WIDTH), bf16),
        ((BLOCK, WIDTH), bf16),
        ((BLOCK, WIDTH), f32),
        ((BLOCK, WIDTH), bf16),
        ((8, WIDTH), f32),
    ]
    return pl.pallas_call(
        partial(backward_kernel, micro),
        in_specs=[pl.BlockSpec(memory_space=pltpu.SMEM)] + [anywhere] * (len(operands) - 1),
        out_specs=[in_hbm] * 6,
        out_shape=outs,
        scratch_shapes=[pltpu.VMEM(shape, kind) for shape, kind in scratch]
        + [pltpu.SemaphoreType.DMA((19,))],
        compiler_params=pltpu.CompilerParams(vmem_limit_bytes=VMEM_LIMIT),
        cost_estimate=pl.CostEstimate(
            flops=2 * 7 * BLOCK * WIDTH * WIDTH, bytes_accessed=16 << 20, transcendentals=0
        ),
        name="backward",
    )(*operands)


def ring_slots(size):
    if size == 4:
        return (2, 2, 2, 1, 1), {
            (0, 0): (0, 0), (1, 0): (0, 1),
            (0, 1): (3, 0), (1, 1): (1, 1),
            (0, 2): (1, 0), (1, 2): (2, 1),
            (0, 3): (2, 0), (1, 3): (4, 0),
        }
    return (2,) * size, {(m, f): (f, m) for m in range(2) for f in range(size)}


def add(*values):
    return sum(value.astype(jnp.float32) for value in values)


def ring_sum(parts, axis):
    size = group_dims()[axis]
    if size == 4:
        keep, up, down, late_up, late_down = parts
        up, down = turn(up, axis, 1), turn(down, axis, -1)
        late_up = add(late_up[0], up[0]).astype(jnp.bfloat16)
        late_down = add(late_down[0], down[1]).astype(jnp.bfloat16)
        late_up, late_down = turn(late_up, axis, 1), turn(late_down, axis, -1)
        return jnp.stack([add(keep[0], late_up, down[0]), add(keep[1], up[1], late_down)])
    if size == 2:
        return add(parts[0], turn(parts[1], axis, 1))
    return parts[0].astype(jnp.float32)


def collect_kernel(sections, dims, counts, *refs):
    place, spot, h_in, a_in = refs[:4]
    kept = refs[4 : 4 + 12 * sections]
    refs = refs[4 + 12 * sections :]
    frame_out, gain_out, outs = refs[0], refs[1], refs[2 : 2 + sum(counts)]
    left, right, term, frame, gain, sems, out_sems = refs[2 + sum(counts) :]
    planes, size_y, size_x = dims
    share = WIDTH // (planes * size_y * size_x)
    own_y, own_x = spot[1], spot[2]
    names = ("frame", "g", "dq", "dk", "dv", "gain")

    def copies(at):
        found = []
        for micro in range(MICRO):
            results = dict(zip(names, kept[(at * MICRO + micro) * 6 : (at * MICRO + micro + 1) * 6]))
            rows = pl.ds(micro * BLOCK, BLOCK)
            pairs = [(results[name], right.at[n, rows]) for n, name in enumerate(("dq", "dk", "dv", "g"))]
            pairs += [(results["frame"], frame.at[micro]), (results["gain"], gain.at[micro])]
            pairs += [(h_in.at[micro], left.at[0, rows]), (a_in.at[micro], left.at[1, rows])]
            found += [
                pltpu.make_async_copy(source, target, sems.at[micro, n])
                for n, (source, target) in enumerate(pairs)
            ]
        return found

    for at in range(sections):

        @pl.when(place[0] == at)
        def _(at=at):
            started = copies(at)
            for copy in started:
                copy.start()
            for copy in started:
                copy.wait()

    frame_copy = pltpu.make_async_copy(frame, frame_out, out_sems.at[4, 0])
    frame_copy.start()
    gain[0] = gain[0] + gain[1]
    gain_copy = pltpu.make_async_copy(gain.at[0], gain_out, out_sems.at[4, 1])
    gain_copy.start()

    started = [frame_copy, gain_copy]
    for m in range(4):
        pair = m // 2
        first_size, second_size = (size_x, size_y) if pair == 0 else (size_y, size_x)
        _, slots = ring_slots(first_size)
        arrays = outs[: counts[0]] if pair == 0 else outs[counts[0] :]
        factor = left[1 if m == 3 else 0]
        for n in range(0, WIDTH, 256):
            cols = slice(n, n + 256)
            term[m, :, cols] = dot_tn(factor, right[m, :, cols]).astype(jnp.bfloat16)
        number = 0
        for f in range(first_size):
            array, row = slots[m % 2, f]
            for r in range(second_size):
                ahead_x, ahead_y = (f, r) if pair == 0 else (r, f)
                column = lax.rem(own_y + ahead_y, size_y) * size_x + lax.rem(own_x + ahead_x, size_x)
                for plane in range(planes):
                    at = (plane * size_y * size_x + column) * share
                    copy = pltpu.make_async_copy(
                        term.at[m, pl.ds(pl.multiple_of(at, share), share), :],
                        arrays[array].at[row, r, plane],
                        out_sems.at[m, number],
                    )
                    copy.start()
                    started.append(copy)
                    number += 1
    for copy in started:
        copy.wait()


def collect(section, spot, h, a, kept):
    dims, sections = group_dims(), len(kept)
    planes, size_y, size_x = dims
    total = planes * size_y * size_x
    share = WIDTH // total
    anywhere = pl.BlockSpec(memory_space=pl.ANY)
    in_hbm = pl.BlockSpec(memory_space=pltpu.HBM)
    smem = pl.BlockSpec(memory_space=pltpu.SMEM)
    shapes, counts = [], []
    for first_size, second_size in ((size_x, size_y), (size_y, size_x)):
        rows, _ = ring_slots(first_size)
        counts.append(len(rows))
        shapes += [
            jax.ShapeDtypeStruct((n, second_size, planes, share, WIDTH), jnp.bfloat16) for n in rows
        ]
    operands = [result for both in kept for results in both for result in results]
    outs = pl.pallas_call(
        partial(collect_kernel, sections, dims, counts),
        in_specs=[smem, smem] + [anywhere] * (2 + len(operands)),
        out_specs=[in_hbm] * (2 + len(shapes)),
        out_shape=[
            jax.ShapeDtypeStruct((MICRO, BLOCK, WIDTH), jnp.bfloat16),
            jax.ShapeDtypeStruct((8, WIDTH), jnp.float32),
        ]
        + shapes,
        scratch_shapes=[
            pltpu.VMEM((2, MICRO * BLOCK, WIDTH), jnp.bfloat16),
            pltpu.VMEM((4, MICRO * BLOCK, WIDTH), jnp.bfloat16),
            pltpu.VMEM((4, WIDTH, WIDTH), jnp.bfloat16),
            pltpu.VMEM((MICRO, BLOCK, WIDTH), jnp.bfloat16),
            pltpu.VMEM((MICRO, 8, WIDTH), jnp.float32),
            pltpu.SemaphoreType.DMA((MICRO, 8)),
            pltpu.SemaphoreType.DMA((5, max(total, 2))),
        ],
        compiler_params=pltpu.CompilerParams(vmem_limit_bytes=VMEM_LIMIT),
        cost_estimate=pl.CostEstimate(
            flops=2 * 8 * BLOCK * WIDTH * WIDTH, bytes_accessed=14 << 20, transcendentals=0
        ),
        name="collect",
    )(section, spot, h, a, *operands)
    frame, gain = outs[:2]
    return frame, gain, [outs[2 : 2 + counts[0]], outs[2 + counts[0] :]]


def sum_terms(parts, plane):
    totals = []
    for pair, (first, second) in zip(parts, ((2, 1), (1, 2))):
        value = ring_sum(pair, first).astype(jnp.bfloat16)
        rows, slots = ring_slots(group_dims()[second])
        arrays = [[None] * n for n in rows]
        for (m, f), (array, row) in slots.items():
            arrays[array][row] = value[m, f]
        value = ring_sum([jnp.stack(array) for array in arrays], second)
        totals.append(value)
    value = jnp.concatenate(totals)
    if group_dims()[0] == 1:
        return value[:, 0]
    other = lax.dynamic_index_in_dim(value, 1 - plane, 1, keepdims=False).astype(jnp.bfloat16)
    return add(lax.dynamic_index_in_dim(value, plane, 1, keepdims=False), turn(other, 0, 1))


def segments(lengths, block):
    bounds = jnp.cumsum(lengths, axis=1)
    total = lax.axis_size(GROUP) * BLOCK
    places = (block - 2) * BLOCK + jnp.arange(5 * BLOCK, dtype=jnp.int32)
    counted = jnp.sum((places[None, :, None] >= bounds[:, None, :]).astype(jnp.int32), axis=2)
    return jnp.where(places < 0, -1, jnp.where(places >= total, -2, counted))


def body(checkpoints, cotangent, weights, gains, lengths):
    sections, section = lax.axis_size("section"), lax.axis_index("section")
    block = lax.axis_index(GROUP)
    share = gains.shape[1]

    pairs = gather_weights(weights[0])
    planes, size_y, _ = group_dims()
    dp = lax.axis_index("dp")
    spot = jnp.stack([dp // size_y, dp % size_y, lax.axis_index("fsdp")]).astype(jnp.int32)
    spread = jnp.zeros((8, max(share, 128)), jnp.float32).at[:1, :share].set(gains.astype(jnp.float32))
    spread = lax.all_gather(spread, GROUP, axis=0)
    gain = jnp.broadcast_to(spread[:, 0, :share].reshape(1, WIDTH), (8, WIDTH))

    x = checkpoints[0]
    left, right = shift(x, 1), shift(x, -1)
    parts = (shift(left, 1), left, x, right, shift(right, -1))
    source = max(sections - 3, 0)
    cot = (cotangent, hop(cotangent, source, sections - 1, 1), hop(cotangent, source, sections - 1, 2))

    segs = segments(lengths, block)
    gathered, h, q, k, v, p, pt, o, a = forward(
        spot, pairs, parts, gain, segs[:, :, None], segs[:, None, :]
    )
    kept = (q, k, v, p, pt, o)

    kept_grads = [[None] * MICRO for _ in range(sections)]
    incoming = [[part[micro] for part in cot] for micro in range(MICRO)]
    for at in range(sections - 1, -1, -1):
        flag = (section == at).astype(jnp.int32).reshape(1)
        for micro in range(MICRO):
            grads = list(backward(micro, flag, incoming[micro], gathered, kept, x, gain))
            if at > 0:
                if micro > 0:
                    grads[0] = tie(grads[0], *incoming[micro - 1])
                incoming[micro] = [hop(grads[0], at, at - 1, back) for back in range(3)]
            kept_grads[at][micro] = grads

    place = section.astype(jnp.int32).reshape(1)
    frame, gain_part, parts = collect(place, spot, h, a, kept_grads)
    weight_part = sum_terms(parts, spot[0])
    gain_term = gain_part[0:1].astype(jnp.bfloat16).astype(jnp.float32)
    gain_term = lax.all_gather(gain_term.reshape(8, WIDTH // 8), GROUP, axis=0)
    gain_sum = jnp.sum(gain_term, axis=0).reshape(1, WIDTH)
    gain_sum = lax.dynamic_slice(gain_sum, (0, block * share), (1, share))
    return (frame[None], weight_part[None], gain_sum)


def solution(mesh):
    placed = (
        P("section", None, ("dp", "fsdp"), None),
        P(None, ("dp", "fsdp"), None),
        P("section", None, ("dp", "fsdp"), None),
        P("section", ("dp", "fsdp")),
        P(),
    )
    return jax.shard_map(
        body,
        mesh=mesh,
        in_specs=placed,
        out_specs=(
            P("section", None, ("dp", "fsdp"), None),
            P("section", None, ("dp", "fsdp"), None),
            P("section", ("dp", "fsdp")),
        ),
        check_vma=False,
    )
```

```python
from functools import partial
import math

import jax
import jax.numpy as jnp
from jax import lax
from jax.experimental import pallas as pl
from jax.experimental.pallas import tpu as pltpu
from jax.sharding import PartitionSpec as P

HEAD = 128
BLOCK = 128
WIDTH = 1024
HEADS = WIDTH // HEAD
MICRO = 2
SCALE = 1.0 / math.sqrt(HEAD)
GROUP = ("dp", "fsdp")
EVERY = ("dp", "section", "fsdp")
MIB = 1024 * 1024
HEAD_ROWS = 16


def dot(left, right):
    return lax.dot_general(left, right, (((1,), (0,)), ((), ())), preferred_element_type=jnp.float32)


def dot_nt(left, right):
    return lax.dot_general(left, right, (((1,), (1,)), ((), ())), preferred_element_type=jnp.float32)


def dot_tn(left, right):
    return lax.dot_general(left, right, (((0,), (0,)), ((), ())), preferred_element_type=jnp.float32)


def shift(value, steps):
    count = lax.axis_size(GROUP)
    pairs = [(b, b + steps) for b in range(count) if 0 <= b + steps < count]
    return lax.ppermute(value, GROUP, pairs)


def hop(value, source, target, back):
    sections, rows = lax.axis_size("section"), lax.axis_size("fsdp")
    count = lax.axis_size(GROUP)

    def place(section, block):
        return (block // rows * sections + section) * rows + block % rows

    pairs = [(place(source, b), place(target, b - back)) for b in range(back, count)]
    return lax.ppermute(value, EVERY, pairs)


def group_dims():
    dp, fsdp = lax.axis_size("dp"), lax.axis_size("fsdp")
    planes = 2 if dp % 2 == 0 else 1
    return (planes, dp // planes, fsdp)


def turn(value, axis, steps):
    dims = group_dims()
    pairs = []
    for z in range(dims[0]):
        for y in range(dims[1]):
            for x in range(dims[2]):
                at = [z, y, x]
                to = list(at)
                to[axis] = (at[axis] + steps) % dims[axis]
                index = lambda p: (p[0] * dims[1] + p[1]) * dims[2] + p[2]
                pairs.append((index(at), index(to)))
    return lax.ppermute(value, GROUP, pairs)


def tie_kernel(*refs):
    del refs


def tie(value, *others):
    if not others:
        return value
    anywhere = pl.BlockSpec(memory_space=pl.ANY)
    return pl.pallas_call(
        tie_kernel,
        in_specs=[anywhere] * (1 + len(others)),
        out_specs=anywhere,
        out_shape=jax.ShapeDtypeStruct(value.shape, value.dtype),
        input_output_aliases={0: 0},
        name="tie",
    )(value, *others)


def ring(value, axis, head):
    size, half = group_dims()[axis], (value.shape[0] - head) // 2
    pieces = [(0, 0, value, head)]
    heads = [value[:head]]
    if size == 2:
        other = turn(value, axis, 1)
        pieces.append((1, 0, other, head))
        heads.append(other[:head])
    if size == 4:
        behind, ahead = turn(value, axis, 1), turn(value, axis, -1)
        up = turn(behind[: head + half], axis, 1)
        down = turn(ahead[head + half :], axis, -1)
        pieces += [(1, 0, ahead, head), (2, 0, up, head), (2, half, down, 0), (3, 0, behind, head)]
        heads += [ahead[:head], behind[:head], up[:head]]
    return pieces, sum(heads[1:], heads[0])


def gather_weights(shard, gain):
    share = shard.shape[1]
    value = jnp.concatenate([gain, shard.reshape(4 * share, WIDTH)])
    pair, gain = ring(value, 0, HEAD_ROWS)
    firsts = []
    for begin, axis in ((0, 1), (2 * share, 2)):
        parts = [piece[at + begin : at + begin + 2 * share] for _, _, piece, at in pair]
        head = HEAD_ROWS if begin == 0 else 0
        found, heads = ring(jnp.concatenate(([gain] if head else []) + parts), axis, head)
        gain = heads if head else gain
        rows = [piece[at:] for _, _, piece, at in found]
        firsts.append((rows, head))
    values = [jnp.concatenate(([gain] if head else []) + rows) for rows, head in firsts]
    values = [tie(values[0], values[1]), tie(values[1], values[0])]
    first, gain = ring(values[0], 2, HEAD_ROWS)
    second, _ = ring(values[1], 1, 0)
    return [first, second], gain


def normed(x, gain):
    as_float = x.astype(jnp.float32)
    rscale = lax.rsqrt(jnp.mean(as_float * as_float, axis=-1, keepdims=True) + 1e-06)
    return (as_float * rscale * gain).astype(jnp.bfloat16)


def forward_kernel(layout, dims, *refs):
    count = sum(len(pieces) for pieces in layout)
    spot, pieces, refs = refs[0], refs[1 : 1 + count], refs[1 + count :]
    l2, l1, own, r1, r2, gain, seg_col, seg_row = refs[:8]
    w_out, h_out, q_out, k_out, v_out, p_out, pt_out, o_out, a_out = refs[8:17]
    w, h5, q3, k5, v5, barred, sems = refs[17:]
    step = pl.program_id(0)
    planes, size_y, size_x = dims
    z, y, x = spot[0], spot[1], spot[2]

    def loads(pair):
        copies, offset = [], sum(len(pieces) for pieces in layout[:pair])
        share = WIDTH // (planes * size_y * size_x)
        for at, (place, first, begin, rows) in enumerate(layout[pair]):
            for row in range(rows // (2 * share)):
                one, plane = divmod(first // (2 * share) + row, planes)
                ahead_y, ahead_x = (one, place) if pair == 0 else (place, one)
                to = lax.rem(z + plane, planes) * size_y + lax.rem(y + ahead_y, size_y)
                to = to * size_x + lax.rem(x + ahead_x, size_x)
                to = pl.ds(pl.multiple_of(to * share, share), share)
                for m in range(2):
                    source = pieces[offset + at].at[pl.ds(begin + (2 * row + m) * share, share), :]
                    copies.append(
                        pltpu.make_async_copy(
                            source, w.at[2 * pair + m, to, :], sems.at[pair, len(copies)]
                        )
                    )
        return copies

    def store(pair):
        half = pl.ds(2 * pair, 2)
        return pltpu.make_async_copy(w.at[half], w_out.at[half], sems.at[2, pair])

    @pl.when(step == 0)
    def _():
        for copy in loads(0) + loads(1):
            copy.start()

    gain_row = gain[0:1, :]
    for at, part in enumerate((l2, l1, own, r1, r2)):
        h5[at * BLOCK : (at + 1) * BLOCK, :] = normed(part[0], gain_row)
    h_out[0] = h5[2 * BLOCK : 3 * BLOCK, :]

    @pl.when(step == 0)
    def _():
        for copy in loads(0):
            copy.wait()
        store(0).start()

    for n in range(0, WIDTH, 256):
        cols = slice(n, n + 256)
        q3[:, cols] = dot(h5[2 * BLOCK :, :], w[0, :, cols]).astype(jnp.bfloat16)
        k5[:, cols] = dot(h5[...], w[1, :, cols]).astype(jnp.bfloat16)

    @pl.when(step == 0)
    def _():
        for copy in loads(1):
            copy.wait()
        store(1).start()

    for n in range(0, WIDTH, 256):
        cols = slice(n, n + 256)
        v5[:, cols] = dot(h5[...], w[2, :, cols]).astype(jnp.bfloat16)
    q_out[0] = q3[...]
    k_out[0] = k5[: 3 * BLOCK, :]
    v_out[0] = v5[: 3 * BLOCK, :]
    for j in range(3):
        allowed = (
            seg_col[0, (j + 2) * BLOCK : (j + 3) * BLOCK, 0:1]
            == seg_row[0, 0:1, j * BLOCK : (j + 3) * BLOCK]
        )
        barred[j * BLOCK : (j + 1) * BLOCK, :] = jnp.where(allowed, 0.0, -1e30)
    for head in range(HEADS):
        cols = slice(head * HEAD, (head + 1) * HEAD)
        for j in range(3):
            rows = slice(j * BLOCK, (j + 1) * BLOCK)
            keys = slice(j * BLOCK, (j + 3) * BLOCK)
            score = dot_nt(q3[rows, cols], k5[keys, cols]) + barred[rows, :]
            top = jnp.max(score, axis=-1, keepdims=True)
            expo = jnp.exp((score - top) * SCALE)
            p = expo * (1.0 / jnp.sum(expo, axis=-1, keepdims=True))
            high = p.astype(jnp.bfloat16)
            low = (p - high.astype(jnp.float32)).astype(jnp.bfloat16)
            both = dot(jnp.concatenate([high, low]), v5[keys, cols])
            mixed = both[:BLOCK]
            o_out[0, rows, cols] = mixed + both[BLOCK:]
            if j == 0:
                p_out[0, head] = p
                a_out[0, :, cols] = mixed.astype(jnp.bfloat16)
            pt_out[0, head, :, rows] = p[:, (2 - j) * BLOCK : (3 - j) * BLOCK].T

    @pl.when(step == MICRO - 1)
    def _():
        store(0).wait()
        store(1).wait()


def forward(spot, pairs, parts, gain, seg_col, seg_row):
    anywhere = pl.BlockSpec(memory_space=pl.ANY)
    pieces = [piece for pair in pairs for _, _, piece, _ in pair]
    layout = [
        [(place, first, begin, piece.shape[0] - begin) for place, first, piece, begin in pair]
        for pair in pairs
    ]
    dims = group_dims()
    most = 2 * dims[0] * dims[1] * dims[2]

    def per_micro(shape):
        return pl.BlockSpec((1,) + shape, lambda m: (m,) + (0,) * len(shape))

    def whole(shape):
        return pl.BlockSpec(shape, lambda m: (0,) * len(shape), pipeline_mode=pl.Buffered(1))

    outs = [
        ((BLOCK, WIDTH), jnp.bfloat16),
        ((3 * BLOCK, WIDTH), jnp.bfloat16),
        ((3 * BLOCK, WIDTH), jnp.bfloat16),
        ((3 * BLOCK, WIDTH), jnp.bfloat16),
        ((HEADS, BLOCK, 3 * BLOCK), jnp.float32),
        ((HEADS, BLOCK, 3 * BLOCK), jnp.float32),
        ((3 * BLOCK, WIDTH), jnp.float32),
        ((BLOCK, WIDTH), jnp.bfloat16),
    ]
    return pl.pallas_call(
        partial(forward_kernel, layout, dims),
        grid=(MICRO,),
        in_specs=[pl.BlockSpec(memory_space=pltpu.SMEM)]
        + [anywhere] * len(pieces)
        + [per_micro((BLOCK, WIDTH))] * 5
        + [
            whole((8, WIDTH)),
            per_micro((5 * BLOCK, 1)),
            per_micro((1, 5 * BLOCK)),
        ],
        out_specs=[anywhere] + [per_micro(shape) for shape, _ in outs],
        out_shape=[jax.ShapeDtypeStruct((4, WIDTH, WIDTH), jnp.bfloat16)]
        + [jax.ShapeDtypeStruct((MICRO,) + shape, kind) for shape, kind in outs],
        scratch_shapes=[
            pltpu.VMEM((4, WIDTH, WIDTH), jnp.bfloat16),
            pltpu.VMEM((5 * BLOCK, WIDTH), jnp.bfloat16),
            pltpu.VMEM((3 * BLOCK, WIDTH), jnp.bfloat16),
            pltpu.VMEM((5 * BLOCK, WIDTH), jnp.bfloat16),
            pltpu.VMEM((5 * BLOCK, WIDTH), jnp.bfloat16),
            pltpu.VMEM((3 * BLOCK, 3 * BLOCK), jnp.float32),
            pltpu.SemaphoreType.DMA((3, most)),
        ],
        compiler_params=pltpu.CompilerParams(vmem_limit_bytes=44 * MIB),
        cost_estimate=pl.CostEstimate(
            flops=2 * 2 * 15 * BLOCK * WIDTH * WIDTH, bytes_accessed=28 << 20, transcendentals=0
        ),
        name="forward",
    )(spot, *pieces, *parts, gain, seg_col, seg_row)


def backward_kernel(micro, *refs):
    flag, g0, g1, g2, w, q_in, k_in, v_in, p_in, pt_in, o_in, x_in, gain_in = refs[:13]
    refs = refs[13:]
    frame_out, g_out, dq_out, dk_out, dv_out, gain_out = refs[:6]
    g, wv, q, k, v, p, pt, o, x, gain, da, dq, dk, dv, dh, frame, gain_sum, sems = refs[6:]

    @pl.when(flag[0] == 1)
    def _():
        def move(at, source, target):
            copy = pltpu.make_async_copy(source, target, sems.at[at])
            copy.start()
            return copy

        load_g = [
            move(at, part, g.at[pl.ds(at * BLOCK, BLOCK), :]) for at, part in enumerate((g0, g1, g2))
        ]
        load_wo = move(3, w.at[3], wv.at[3])
        load_o = move(4, o_in.at[micro], o)
        load_v = move(5, v_in.at[micro], v)
        load_p = move(6, p_in.at[micro], p)
        load_k = move(7, k_in.at[micro], k)
        load_pt = move(8, pt_in.at[micro], pt)
        load_q = move(9, q_in.at[micro], q)
        load_w = move(10, w.at[pl.ds(0, 3)], wv.at[pl.ds(0, 3)])
        load_x = move(11, x_in.at[micro], x)
        load_gain = move(12, gain_in, gain)
        for copy in load_g:
            copy.wait()
        load_wo.wait()
        store_g = move(13, g.at[pl.ds(0, BLOCK), :], g_out)
        for n in range(0, WIDTH, 256):
            cols = slice(n, n + 256)
            da[:, cols] = dot_nt(g[...], wv[3, cols, :]).astype(jnp.bfloat16)
        for copy in (load_o, load_v, load_p, load_k, load_pt, load_q):
            copy.wait()
        for head in range(HEADS):
            cols = slice(head * HEAD, (head + 1) * HEAD)
            da_h = da[:, cols]
            inner = jnp.sum(da_h.astype(jnp.float32) * o[:, cols], axis=-1, keepdims=True)
            dp = dot_nt(da_h[:BLOCK], v[:, cols])
            ds = (p[head] * (dp - inner[:BLOCK]) * SCALE).astype(jnp.bfloat16)
            dq[:, cols] = dot(ds, k[:, cols]).astype(jnp.bfloat16)
            inner_row = jnp.broadcast_to(inner, (3 * BLOCK, HEAD)).T
            p_t = pt[head]
            dp_t = dot_nt(v[2 * BLOCK :, cols], da_h)
            ds_t = (p_t * (dp_t - inner_row) * SCALE).astype(jnp.bfloat16)
            dk[:, cols] = dot(ds_t, q[:, cols]).astype(jnp.bfloat16)
            dv[:, cols] = dot(p_t.astype(jnp.bfloat16), da_h).astype(jnp.bfloat16)
        stores = [
            store_g,
            move(14, dq, dq_out),
            move(15, dk, dk_out),
            move(16, dv, dv_out),
        ]
        load_w.wait()
        for n in range(0, WIDTH, 256):
            cols = slice(n, n + 256)
            dh[:, cols] = (
                dot_nt(dq[...], wv[0, cols, :])
                + dot_nt(dk[...], wv[1, cols, :])
                + dot_nt(dv[...], wv[2, cols, :])
            )
        load_x.wait()
        load_gain.wait()
        as_float = x[...].astype(jnp.float32)
        rscale = lax.rsqrt(jnp.mean(as_float * as_float, axis=-1, keepdims=True) + 1e-06)
        d_normed = dh[...]
        scaled = gain[0:1, :] * d_normed
        cubic = rscale * rscale * rscale
        frame_f = (
            g[:BLOCK, :].astype(jnp.float32)
            + rscale * scaled
            - as_float * (cubic * jnp.mean(scaled * as_float, axis=-1, keepdims=True))
        )
        frame[...] = frame_f.astype(jnp.bfloat16)
        stores.append(move(17, frame, frame_out))
        term = jnp.sum(d_normed * as_float * rscale, axis=0, keepdims=True)
        gain_sum[...] = jnp.broadcast_to(term, (8, WIDTH))
        stores.append(move(18, gain_sum, gain_out))
        for copy in stores:
            copy.wait()


def backward(micro, flag, incoming, w, kept, x, gain):
    block = jax.ShapeDtypeStruct((BLOCK, WIDTH), jnp.bfloat16)
    outs = [block] * 5 + [jax.ShapeDtypeStruct((8, WIDTH), jnp.float32)]
    operands = [flag, *incoming, w, *kept, x, gain]
    anywhere = pl.BlockSpec(memory_space=pl.ANY)
    in_hbm = pl.BlockSpec(memory_space=pltpu.HBM)
    bf16, f32 = jnp.bfloat16, jnp.float32
    scratch = [
        ((3 * BLOCK, WIDTH), bf16),
        ((4, WIDTH, WIDTH), bf16),
        ((3 * BLOCK, WIDTH), bf16),
        ((3 * BLOCK, WIDTH), bf16),
        ((3 * BLOCK, WIDTH), bf16),
        ((HEADS, BLOCK, 3 * BLOCK), f32),
        ((HEADS, BLOCK, 3 * BLOCK), f32),
        ((3 * BLOCK, WIDTH), f32),
        ((BLOCK, WIDTH), bf16),
        ((8, WIDTH), f32),
        ((3 * BLOCK, WIDTH), bf16),
        ((BLOCK, WIDTH), bf16),
        ((BLOCK, WIDTH), bf16),
        ((BLOCK, WIDTH), bf16),
        ((BLOCK, WIDTH), f32),
        ((BLOCK, WIDTH), bf16),
        ((8, WIDTH), f32),
    ]
    return pl.pallas_call(
        partial(backward_kernel, micro),
        in_specs=[pl.BlockSpec(memory_space=pltpu.SMEM)] + [anywhere] * (len(operands) - 1),
        out_specs=[in_hbm] * 6,
        out_shape=outs,
        scratch_shapes=[pltpu.VMEM(shape, kind) for shape, kind in scratch]
        + [pltpu.SemaphoreType.DMA((19,))],
        compiler_params=pltpu.CompilerParams(vmem_limit_bytes=28 * MIB),
        cost_estimate=pl.CostEstimate(
            flops=2 * 7 * BLOCK * WIDTH * WIDTH, bytes_accessed=16 << 20, transcendentals=0
        ),
        name="backward",
    )(*operands)


def ring_slots(size):
    if size == 4:
        return (2, 2, 2, 1, 1), {
            (0, 0): (0, 0), (1, 0): (0, 1),
            (0, 1): (3, 0), (1, 1): (1, 1),
            (0, 2): (1, 0), (1, 2): (2, 1),
            (0, 3): (2, 0), (1, 3): (4, 0),
        }
    return (2,) * size, {(m, f): (f, m) for m in range(2) for f in range(size)}


def ring_heads(size):
    return (1, 2) if size == 4 else (1,) * (size == 2)


def add(*values):
    return sum(value.astype(jnp.float32) for value in values)


def ring_sum(parts, axis, gain):
    size, head = group_dims()[axis], 0 if gain is None else HEAD_ROWS
    rows = parts[0].shape[0] // 2
    if size == 4:
        keep, up, down, late_up, late_down = parts
        up, down = turn(up, axis, 1), turn(down, axis, -1)
        late_up = add(late_up, up[head : head + rows]).astype(jnp.bfloat16)
        late_down = add(late_down, down[head + rows :]).astype(jnp.bfloat16)
        if head:
            late_up = jnp.concatenate([up[:head], late_up])
        late_up, late_down = turn(late_up, axis, 1), turn(late_down, axis, -1)
        total = [
            add(keep[:rows], late_up[head:], down[head : head + rows]),
            add(keep[rows:], up[head + rows :], late_down),
        ]
        if head:
            gain = add(gain, up[:head], down[:head], late_up[:head])
        return jnp.stack(total), gain
    if size == 2:
        other = turn(parts[1], axis, 1)
        if head:
            gain = add(gain, other[:head])
        return add(parts[0], other[head:]).reshape(2, rows, WIDTH), gain
    return parts[0].astype(jnp.float32).reshape(2, rows, WIDTH), gain


def collect_kernel(sections, dims, counts, *refs):
    place, spot, h_in, a_in = refs[:4]
    kept = refs[4 : 4 + 12 * sections]
    refs = refs[4 + 12 * sections :]
    frame_out, gain_out, outs = refs[0], refs[1], refs[2 : 2 + sum(counts)]
    left, right, term, frame, gain, gain_head, sems, out_sems = refs[2 + sum(counts) :]
    planes, size_y, size_x = dims
    share = WIDTH // (planes * size_y * size_x)
    own_y, own_x = spot[1], spot[2]
    names = ("frame", "g", "dq", "dk", "dv", "gain")

    def copies(at):
        found = []
        for micro in range(MICRO):
            results = dict(zip(names, kept[(at * MICRO + micro) * 6 : (at * MICRO + micro + 1) * 6]))
            rows = pl.ds(micro * BLOCK, BLOCK)
            pairs = [(results[name], right.at[n, rows]) for n, name in enumerate(("dq", "dk", "dv", "g"))]
            pairs += [(results["frame"], frame.at[micro]), (results["gain"], gain.at[micro])]
            pairs += [(h_in.at[micro], left.at[0, rows]), (a_in.at[micro], left.at[1, rows])]
            found += [
                pltpu.make_async_copy(source, target, sems.at[micro, n])
                for n, (source, target) in enumerate(pairs)
            ]
        return found

    for at in range(sections):

        @pl.when(place[0] == at)
        def _(at=at):
            started = copies(at)
            for copy in started:
                copy.start()
            for copy in started:
                copy.wait()

    frame_copy = pltpu.make_async_copy(frame, frame_out, out_sems.at[4, 0])
    frame_copy.start()
    gain_term = (gain[0, 0:1, :] + gain[1, 0:1, :]).astype(jnp.bfloat16)
    gain_head[...] = jnp.broadcast_to(gain_term, (HEAD_ROWS, WIDTH))
    started = [frame_copy]
    heads = [gain_out] + [outs[at].at[pl.ds(0, HEAD_ROWS), :] for at in ring_heads(size_x)]
    for at, target in enumerate(heads):
        copy = pltpu.make_async_copy(gain_head, target, out_sems.at[4, 1 + at])
        copy.start()
        started.append(copy)
    for m in range(4):
        pair = m // 2
        first_size, second_size = (size_x, size_y) if pair == 0 else (size_y, size_x)
        _, slots = ring_slots(first_size)
        arrays = outs[: counts[0]] if pair == 0 else outs[counts[0] :]
        factor = left[1 if m == 3 else 0]
        for n in range(0, WIDTH, 256):
            cols = slice(n, n + 256)
            term[m, :, cols] = dot_tn(factor, right[m, :, cols]).astype(jnp.bfloat16)
        number = 0
        for f in range(first_size):
            array, row = slots[m % 2, f]
            for r in range(second_size):
                ahead_x, ahead_y = (f, r) if pair == 0 else (r, f)
                column = lax.rem(own_y + ahead_y, size_y) * size_x + lax.rem(own_x + ahead_x, size_x)
                for plane in range(planes):
                    at = (plane * size_y * size_x + column) * share
                    to = ((row * second_size + r) * planes + plane) * share
                    if pair == 0 and array in ring_heads(first_size):
                        to += HEAD_ROWS
                    copy = pltpu.make_async_copy(
                        term.at[m, pl.ds(pl.multiple_of(at, share), share), :],
                        arrays[array].at[pl.ds(to, share), :],
                        out_sems.at[m, number],
                    )
                    copy.start()
                    started.append(copy)
                    number += 1
    for copy in started:
        copy.wait()


def collect(section, spot, h, a, kept):
    dims, sections = group_dims(), len(kept)
    planes, size_y, size_x = dims
    total = planes * size_y * size_x
    share = WIDTH // total
    anywhere = pl.BlockSpec(memory_space=pl.ANY)
    in_hbm = pl.BlockSpec(memory_space=pltpu.HBM)
    smem = pl.BlockSpec(memory_space=pltpu.SMEM)
    shapes, counts = [], []
    for first_size, second_size in ((size_x, size_y), (size_y, size_x)):
        rows, _ = ring_slots(first_size)
        counts.append(len(rows))
        for at, n in enumerate(rows):
            n = n * second_size * planes * share
            if len(counts) == 1 and at in ring_heads(first_size):
                n += HEAD_ROWS
            shapes.append(jax.ShapeDtypeStruct((n, WIDTH), jnp.bfloat16))
    operands = [result for both in kept for results in both for result in results]
    outs = pl.pallas_call(
        partial(collect_kernel, sections, dims, counts),
        in_specs=[smem, smem] + [anywhere] * (2 + len(operands)),
        out_specs=[in_hbm] * (2 + len(shapes)),
        out_shape=[
            jax.ShapeDtypeStruct((MICRO, BLOCK, WIDTH), jnp.bfloat16),
            jax.ShapeDtypeStruct((HEAD_ROWS, WIDTH), jnp.bfloat16),
        ]
        + shapes,
        scratch_shapes=[
            pltpu.VMEM((2, MICRO * BLOCK, WIDTH), jnp.bfloat16),
            pltpu.VMEM((4, MICRO * BLOCK, WIDTH), jnp.bfloat16),
            pltpu.VMEM((4, WIDTH, WIDTH), jnp.bfloat16),
            pltpu.VMEM((MICRO, BLOCK, WIDTH), jnp.bfloat16),
            pltpu.VMEM((MICRO, 8, WIDTH), jnp.float32),
            pltpu.VMEM((HEAD_ROWS, WIDTH), jnp.bfloat16),
            pltpu.SemaphoreType.DMA((MICRO, 8)),
            pltpu.SemaphoreType.DMA((5, max(total, 4))),
        ],
        compiler_params=pltpu.CompilerParams(vmem_limit_bytes=24 * MIB),
        cost_estimate=pl.CostEstimate(
            flops=2 * 8 * BLOCK * WIDTH * WIDTH, bytes_accessed=14 << 20, transcendentals=0
        ),
        name="collect",
    )(section, spot, h, a, *operands)
    frame, gain = outs[:2]
    return frame, gain, [outs[2 : 2 + counts[0]], outs[2 + counts[0] :]]


def sum_terms(parts, gain, plane):
    dims, totals = group_dims(), []
    for pair, (first, second) in zip(parts, ((2, 1), (1, 2))):
        own = gain if first == 2 else None
        value, own = ring_sum(pair, first, own)
        value = value.astype(jnp.bfloat16).reshape(2, dims[second], -1, WIDTH)
        rows, slots = ring_slots(dims[second])
        arrays = [[None] * n for n in rows]
        for (m, f), (array, row) in slots.items():
            arrays[array][row] = value[m, f]
        if own is not None:
            own = own.astype(jnp.bfloat16)
            for array in ring_heads(dims[second]):
                arrays[array].insert(0, own)
        value, own = ring_sum([jnp.concatenate(array) for array in arrays], second, own)
        totals.append(value)
        gain = gain if own is None else own
    value = jnp.concatenate(totals)
    if dims[0] == 1:
        return value, gain
    share = value.shape[1] // 2
    value = value.reshape(4, 2, share, WIDTH)
    other = lax.dynamic_index_in_dim(value, 1 - plane, 1, keepdims=False).astype(jnp.bfloat16)
    own = lax.dynamic_index_in_dim(value, plane, 1, keepdims=False)
    other = jnp.concatenate([gain.astype(jnp.bfloat16), other.reshape(4 * share, WIDTH)])
    other = turn(other, 0, 1)
    return add(own, other[HEAD_ROWS:].reshape(own.shape)), add(gain, other[:HEAD_ROWS])


def segments(lengths, block):
    bounds = jnp.cumsum(lengths, axis=1)
    total = lax.axis_size(GROUP) * BLOCK
    places = (block - 2) * BLOCK + jnp.arange(5 * BLOCK, dtype=jnp.int32)
    counted = jnp.sum((places[None, :, None] >= bounds[:, None, :]).astype(jnp.int32), axis=2)
    return jnp.where(places < 0, -1, jnp.where(places >= total, -2, counted))


def body(checkpoints, cotangent, weights, gains, lengths):
    sections, section = lax.axis_size("section"), lax.axis_index("section")
    block = lax.axis_index(GROUP)
    share = gains.shape[1]

    planes, size_y, _ = group_dims()
    dp = lax.axis_index("dp")
    spot = jnp.stack([dp // size_y, dp % size_y, lax.axis_index("fsdp")]).astype(jnp.int32)
    spread = lax.dynamic_update_slice(
        jnp.zeros((HEAD_ROWS, WIDTH), jnp.bfloat16), gains, (0, block * share)
    )
    pairs, gain = gather_weights(weights[0], spread)
    gain = jnp.broadcast_to(gain[0:1].astype(jnp.float32), (8, WIDTH))

    x = checkpoints[0]
    left, right = shift(x, 1), shift(x, -1)
    parts = (shift(left, 1), left, x, right, shift(right, -1))
    source = max(sections - 3, 0)
    cot = (cotangent, hop(cotangent, source, sections - 1, 1), hop(cotangent, source, sections - 1, 2))

    segs = segments(lengths, block)
    gathered, h, q, k, v, p, pt, o, a = forward(
        spot, pairs, parts, gain, segs[:, :, None], segs[:, None, :]
    )
    kept = (q, k, v, p, pt, o)

    kept_grads = [[None] * MICRO for _ in range(sections)]
    incoming = [[part[micro] for part in cot] for micro in range(MICRO)]
    for at in range(sections - 1, -1, -1):
        flag = (section == at).astype(jnp.int32).reshape(1)
        for micro in range(MICRO):
            grads = list(backward(micro, flag, incoming[micro], gathered, kept, x, gain))
            if at > 0:
                before = incoming[micro - 1] if micro > 0 else []
                if at % 2 == 1:
                    grads[0] = tie(grads[0], *before)
                    incoming[micro] = [hop(grads[0], at, at - 1, back) for back in range(3)]
                else:
                    grads[0] = tie(grads[0], *before[:1])
                    own = tie(hop(grads[0], at, at - 1, 0), *before[1:])
                    incoming[micro] = [own] + [hop(own, at - 1, at - 1, back) for back in (1, 2)]
            kept_grads[at][micro] = grads

    place = section.astype(jnp.int32).reshape(1)
    frame, gain_part, parts = collect(place, spot, h, a, kept_grads)
    weight_part, gain_sum = sum_terms(parts, gain_part, spot[0])
    gain_sum = lax.dynamic_slice(gain_sum, (0, block * share), (1, share))
    return (frame[None], weight_part[None], gain_sum)


def solution(mesh):
    placed = (
        P("section", None, ("dp", "fsdp"), None),
        P(None, ("dp", "fsdp"), None),
        P("section", None, ("dp", "fsdp"), None),
        P("section", ("dp", "fsdp")),
        P(),
    )
    return jax.shard_map(
        body,
        mesh=mesh,
        in_specs=placed,
        out_specs=(
            P("section", None, ("dp", "fsdp"), None),
            P("section", None, ("dp", "fsdp"), None),
            P("section", ("dp", "fsdp")),
        ),
        check_vma=False,
    )
```

```python
from functools import partial
import math

import jax
import jax.numpy as jnp
from jax import lax
from jax.experimental import pallas as pl
from jax.experimental.pallas import tpu as pltpu
from jax.sharding import PartitionSpec as P

HEAD = 128
BLOCK = 128
WIDTH = 1024
HEADS = WIDTH // HEAD
MICRO = 2
SCALE = 1.0 / math.sqrt(HEAD)
GROUP = ("dp", "fsdp")
EVERY = ("dp", "section", "fsdp")
MIB = 1024 * 1024
HEAD_ROWS = 16


def dot(left, right):
    return lax.dot_general(left, right, (((1,), (0,)), ((), ())), preferred_element_type=jnp.float32)


def dot_nt(left, right):
    return lax.dot_general(left, right, (((1,), (1,)), ((), ())), preferred_element_type=jnp.float32)


def dot_tn(left, right):
    return lax.dot_general(left, right, (((0,), (0,)), ((), ())), preferred_element_type=jnp.float32)


def shift(value, steps):
    count = lax.axis_size(GROUP)
    pairs = [(b, b + steps) for b in range(count) if 0 <= b + steps < count]
    return lax.ppermute(value, GROUP, pairs)


def hop(value, source, target, back):
    sections, rows = lax.axis_size("section"), lax.axis_size("fsdp")
    count = lax.axis_size(GROUP)

    def place(section, block):
        return (block // rows * sections + section) * rows + block % rows

    pairs = [(place(source, b), place(target, b - back)) for b in range(back, count)]
    return lax.ppermute(value, EVERY, pairs)


def group_dims():
    dp, fsdp = lax.axis_size("dp"), lax.axis_size("fsdp")
    planes = 2 if dp % 2 == 0 else 1
    return (planes, dp // planes, fsdp)


def turn(value, axis, steps):
    dims = group_dims()
    pairs = []
    for z in range(dims[0]):
        for y in range(dims[1]):
            for x in range(dims[2]):
                at = [z, y, x]
                to = list(at)
                to[axis] = (at[axis] + steps) % dims[axis]
                index = lambda p: (p[0] * dims[1] + p[1]) * dims[2] + p[2]
                pairs.append((index(at), index(to)))
    return lax.ppermute(value, GROUP, pairs)


def tie_kernel(*refs):
    del refs


def tie(value, *others):
    if not others:
        return value
    anywhere = pl.BlockSpec(memory_space=pl.ANY)
    return pl.pallas_call(
        tie_kernel,
        in_specs=[anywhere] * (1 + len(others)),
        out_specs=anywhere,
        out_shape=jax.ShapeDtypeStruct(value.shape, value.dtype),
        input_output_aliases={0: 0},
        name="tie",
    )(value, *others)


def ring(value, axis, head):
    size, half = group_dims()[axis], (value.shape[0] - head) // 2
    pieces = [(0, 0, value, head)]
    heads = [value[:head]]
    if size == 2:
        other = turn(value, axis, 1)
        pieces.append((1, 0, other, head))
        heads.append(other[:head])
    if size == 4:
        behind, ahead = turn(value, axis, 1), turn(value, axis, -1)
        up = turn(behind[: head + half], axis, 1)
        down = turn(ahead[head + half :], axis, -1)
        pieces += [(1, 0, ahead, head), (2, 0, up, head), (2, half, down, 0), (3, 0, behind, head)]
        heads += [ahead[:head], behind[:head], up[:head]]
    return pieces, sum(heads[1:], heads[0])


def gather_weights(shard, gain):
    share = shard.shape[1]
    value = jnp.concatenate([gain, shard.reshape(4 * share, WIDTH)])
    pair, gain = ring(value, 0, HEAD_ROWS)
    firsts = []
    for begin, axis in ((0, 1), (2 * share, 2)):
        parts = [piece[at + begin : at + begin + 2 * share] for _, _, piece, at in pair]
        head = HEAD_ROWS if begin == 0 else 0
        found, heads = ring(jnp.concatenate(([gain] if head else []) + parts), axis, head)
        gain = heads if head else gain
        rows = [piece[at:] for _, _, piece, at in found]
        firsts.append((rows, head))
    values = [jnp.concatenate(([gain] if head else []) + rows) for rows, head in firsts]
    values = [tie(values[0], values[1]), tie(values[1], values[0])]
    first, gain = ring(values[0], 2, HEAD_ROWS)
    second, _ = ring(values[1], 1, 0)
    return [first, second], gain


def normed(x, gain):
    as_float = x.astype(jnp.float32)
    rscale = lax.rsqrt(jnp.mean(as_float * as_float, axis=-1, keepdims=True) + 1e-06)
    return (as_float * rscale * gain).astype(jnp.bfloat16)


def forward_kernel(layout, dims, *refs):
    count = sum(len(pieces) for pieces in layout)
    spot, pieces, refs = refs[0], refs[1 : 1 + count], refs[1 + count :]
    l2, l1, own, r1, r2, gain, seg_col, seg_row = refs[:8]
    w_out, h_out, q_out, k_out, v_out, p_out, pt_out, o_out, a_out = refs[8:17]
    w, h5, q3, k5, v5, barred, sems = refs[17:]
    step = pl.program_id(0)
    planes, size_y, size_x = dims
    z, y, x = spot[0], spot[1], spot[2]

    def loads(pair):
        copies, offset = [], sum(len(pieces) for pieces in layout[:pair])
        share = WIDTH // (planes * size_y * size_x)
        for at, (place, first, begin, rows) in enumerate(layout[pair]):
            for row in range(rows // (2 * share)):
                one, plane = divmod(first // (2 * share) + row, planes)
                ahead_y, ahead_x = (one, place) if pair == 0 else (place, one)
                to = lax.rem(z + plane, planes) * size_y + lax.rem(y + ahead_y, size_y)
                to = to * size_x + lax.rem(x + ahead_x, size_x)
                to = pl.ds(pl.multiple_of(to * share, share), share)
                for m in range(2):
                    source = pieces[offset + at].at[pl.ds(begin + (2 * row + m) * share, share), :]
                    copies.append(
                        pltpu.make_async_copy(
                            source, w.at[2 * pair + m, to, :], sems.at[pair, len(copies)]
                        )
                    )
        return copies

    def store(pair):
        half = pl.ds(2 * pair, 2)
        return pltpu.make_async_copy(w.at[half], w_out.at[half], sems.at[2, pair])

    @pl.when(step == 0)
    def _():
        for copy in loads(0) + loads(1):
            copy.start()

    gain_row = gain[0:1, :]
    for at, part in enumerate((l2, l1, own, r1, r2)):
        h5[at * BLOCK : (at + 1) * BLOCK, :] = normed(part[0], gain_row)
    h_out[0] = h5[2 * BLOCK : 3 * BLOCK, :]

    @pl.when(step == 0)
    def _():
        for copy in loads(0):
            copy.wait()
        store(0).start()

    for n in range(0, WIDTH, 256):
        cols = slice(n, n + 256)
        q3[:, cols] = dot(h5[2 * BLOCK :, :], w[0, :, cols]).astype(jnp.bfloat16)
        k5[:, cols] = dot(h5[...], w[1, :, cols]).astype(jnp.bfloat16)

    @pl.when(step == 0)
    def _():
        for copy in loads(1):
            copy.wait()
        store(1).start()

    for n in range(0, WIDTH, 256):
        cols = slice(n, n + 256)
        v5[:, cols] = dot(h5[...], w[2, :, cols]).astype(jnp.bfloat16)
    q_out[0] = q3[...]
    k_out[0] = k5[: 3 * BLOCK, :]
    v_out[0] = v5[: 3 * BLOCK, :]
    for j in range(3):
        allowed = (
            seg_col[0, (j + 2) * BLOCK : (j + 3) * BLOCK, 0:1]
            == seg_row[0, 0:1, j * BLOCK : (j + 3) * BLOCK]
        )
        barred[j * BLOCK : (j + 1) * BLOCK, :] = jnp.where(allowed, 0.0, -1e30)
    for head in range(HEADS):
        cols = slice(head * HEAD, (head + 1) * HEAD)
        for j in range(3):
            rows = slice(j * BLOCK, (j + 1) * BLOCK)
            keys = slice(j * BLOCK, (j + 3) * BLOCK)
            score = dot_nt(q3[rows, cols], k5[keys, cols]) + barred[rows, :]
            top = jnp.max(score, axis=-1, keepdims=True)
            expo = jnp.exp((score - top) * SCALE)
            p = expo * (1.0 / jnp.sum(expo, axis=-1, keepdims=True))
            high = p.astype(jnp.bfloat16)
            low = (p - high.astype(jnp.float32)).astype(jnp.bfloat16)
            both = dot(jnp.concatenate([high, low]), v5[keys, cols])
            mixed = both[:BLOCK]
            o_out[0, rows, cols] = mixed + both[BLOCK:]
            if j == 0:
                p_out[0, head] = p
                a_out[0, :, cols] = mixed.astype(jnp.bfloat16)
            pt_out[0, head, :, rows] = p[:, (2 - j) * BLOCK : (3 - j) * BLOCK].T

    @pl.when(step == MICRO - 1)
    def _():
        store(0).wait()
        store(1).wait()


def forward(spot, pairs, parts, gain, seg_col, seg_row):
    anywhere = pl.BlockSpec(memory_space=pl.ANY)
    pieces = [piece for pair in pairs for _, _, piece, _ in pair]
    layout = [
        [(place, first, begin, piece.shape[0] - begin) for place, first, piece, begin in pair]
        for pair in pairs
    ]
    dims = group_dims()
    most = 2 * dims[0] * dims[1] * dims[2]

    def per_micro(shape):
        return pl.BlockSpec((1,) + shape, lambda m: (m,) + (0,) * len(shape))

    def whole(shape):
        return pl.BlockSpec(shape, lambda m: (0,) * len(shape), pipeline_mode=pl.Buffered(1))

    outs = [
        ((BLOCK, WIDTH), jnp.bfloat16),
        ((3 * BLOCK, WIDTH), jnp.bfloat16),
        ((3 * BLOCK, WIDTH), jnp.bfloat16),
        ((3 * BLOCK, WIDTH), jnp.bfloat16),
        ((HEADS, BLOCK, 3 * BLOCK), jnp.float32),
        ((HEADS, BLOCK, 3 * BLOCK), jnp.float32),
        ((3 * BLOCK, WIDTH), jnp.float32),
        ((BLOCK, WIDTH), jnp.bfloat16),
    ]
    return pl.pallas_call(
        partial(forward_kernel, layout, dims),
        grid=(MICRO,),
        in_specs=[pl.BlockSpec(memory_space=pltpu.SMEM)]
        + [anywhere] * len(pieces)
        + [per_micro((BLOCK, WIDTH))] * 5
        + [
            whole((8, WIDTH)),
            per_micro((5 * BLOCK, 1)),
            per_micro((1, 5 * BLOCK)),
        ],
        out_specs=[anywhere] + [per_micro(shape) for shape, _ in outs],
        out_shape=[jax.ShapeDtypeStruct((4, WIDTH, WIDTH), jnp.bfloat16)]
        + [jax.ShapeDtypeStruct((MICRO,) + shape, kind) for shape, kind in outs],
        scratch_shapes=[
            pltpu.VMEM((4, WIDTH, WIDTH), jnp.bfloat16),
            pltpu.VMEM((5 * BLOCK, WIDTH), jnp.bfloat16),
            pltpu.VMEM((3 * BLOCK, WIDTH), jnp.bfloat16),
            pltpu.VMEM((5 * BLOCK, WIDTH), jnp.bfloat16),
            pltpu.VMEM((5 * BLOCK, WIDTH), jnp.bfloat16),
            pltpu.VMEM((3 * BLOCK, 3 * BLOCK), jnp.float32),
            pltpu.SemaphoreType.DMA((3, most)),
        ],
        compiler_params=pltpu.CompilerParams(vmem_limit_bytes=44 * MIB),
        cost_estimate=pl.CostEstimate(
            flops=2 * 2 * 15 * BLOCK * WIDTH * WIDTH, bytes_accessed=28 << 20, transcendentals=0
        ),
        name="forward",
    )(spot, *pieces, *parts, gain, seg_col, seg_row)


def backward_kernel(micro, *refs):
    flag, g0, g1, g2, w, q_in, k_in, v_in, p_in, pt_in, o_in, x_in, gain_in = refs[:13]
    refs = refs[13:]
    frame_out, g_out, dq_out, dk_out, dv_out, gain_out = refs[:6]
    g, wv, q, k, v, p, pt, o, x, gain, da, dq, dk, dv, dh, frame, gain_sum, sems = refs[6:]

    @pl.when(flag[0] == 1)
    def _():
        def move(at, source, target):
            copy = pltpu.make_async_copy(source, target, sems.at[at])
            copy.start()
            return copy

        load_g = [
            move(at, part, g.at[pl.ds(at * BLOCK, BLOCK), :]) for at, part in enumerate((g0, g1, g2))
        ]
        load_wo = move(3, w.at[3], wv.at[3])
        load_o = move(4, o_in.at[micro], o)
        load_v = move(5, v_in.at[micro], v)
        load_p = move(6, p_in.at[micro], p)
        load_k = move(7, k_in.at[micro], k)
        load_pt = move(8, pt_in.at[micro], pt)
        load_q = move(9, q_in.at[micro], q)
        load_w = move(10, w.at[pl.ds(0, 3)], wv.at[pl.ds(0, 3)])
        load_x = move(11, x_in.at[micro], x)
        load_gain = move(12, gain_in, gain)
        for copy in load_g:
            copy.wait()
        load_wo.wait()
        store_g = move(13, g.at[pl.ds(0, BLOCK), :], g_out)
        for n in range(0, WIDTH, 256):
            cols = slice(n, n + 256)
            da[:, cols] = dot_nt(g[...], wv[3, cols, :]).astype(jnp.bfloat16)
        for copy in (load_o, load_v, load_p, load_k, load_pt, load_q):
            copy.wait()
        for head in range(HEADS):
            cols = slice(head * HEAD, (head + 1) * HEAD)
            da_h = da[:, cols]
            inner = jnp.sum(da_h.astype(jnp.float32) * o[:, cols], axis=-1, keepdims=True)
            dp = dot_nt(da_h[:BLOCK], v[:, cols])
            ds = (p[head] * (dp - inner[:BLOCK]) * SCALE).astype(jnp.bfloat16)
            dq[:, cols] = dot(ds, k[:, cols]).astype(jnp.bfloat16)
            inner_row = jnp.broadcast_to(inner, (3 * BLOCK, HEAD)).T
            p_t = pt[head]
            dp_t = dot_nt(v[2 * BLOCK :, cols], da_h)
            ds_t = (p_t * (dp_t - inner_row) * SCALE).astype(jnp.bfloat16)
            dk[:, cols] = dot(ds_t, q[:, cols]).astype(jnp.bfloat16)
            dv[:, cols] = dot(p_t.astype(jnp.bfloat16), da_h).astype(jnp.bfloat16)
        stores = [
            store_g,
            move(14, dq, dq_out),
            move(15, dk, dk_out),
            move(16, dv, dv_out),
        ]
        load_w.wait()
        for n in range(0, WIDTH, 256):
            cols = slice(n, n + 256)
            dh[:, cols] = (
                dot_nt(dq[...], wv[0, cols, :])
                + dot_nt(dk[...], wv[1, cols, :])
                + dot_nt(dv[...], wv[2, cols, :])
            )
        load_x.wait()
        load_gain.wait()
        as_float = x[...].astype(jnp.float32)
        rscale = lax.rsqrt(jnp.mean(as_float * as_float, axis=-1, keepdims=True) + 1e-06)
        d_normed = dh[...]
        scaled = gain[0:1, :] * d_normed
        cubic = rscale * rscale * rscale
        frame_f = (
            g[:BLOCK, :].astype(jnp.float32)
            + rscale * scaled
            - as_float * (cubic * jnp.mean(scaled * as_float, axis=-1, keepdims=True))
        )
        frame[...] = frame_f.astype(jnp.bfloat16)
        stores.append(move(17, frame, frame_out))
        term = jnp.sum(d_normed * as_float * rscale, axis=0, keepdims=True)
        gain_sum[...] = jnp.broadcast_to(term, (8, WIDTH))
        stores.append(move(18, gain_sum, gain_out))
        for copy in stores:
            copy.wait()


def in_place(value):
    return pltpu.with_memory_space_constraint(value, pltpu.HBM)


def backward(micro, flag, incoming, w, kept, x, gain):
    block = pltpu.HBM((BLOCK, WIDTH), jnp.bfloat16)
    outs = [block] * 5 + [pltpu.HBM((8, WIDTH), jnp.float32)]
    operands = [flag, *incoming] + [in_place(value) for value in (w, *kept, x, gain)]
    anywhere = pl.BlockSpec(memory_space=pl.ANY)
    in_hbm = pl.BlockSpec(memory_space=pltpu.HBM)
    bf16, f32 = jnp.bfloat16, jnp.float32
    scratch = [
        ((3 * BLOCK, WIDTH), bf16),
        ((4, WIDTH, WIDTH), bf16),
        ((3 * BLOCK, WIDTH), bf16),
        ((3 * BLOCK, WIDTH), bf16),
        ((3 * BLOCK, WIDTH), bf16),
        ((HEADS, BLOCK, 3 * BLOCK), f32),
        ((HEADS, BLOCK, 3 * BLOCK), f32),
        ((3 * BLOCK, WIDTH), f32),
        ((BLOCK, WIDTH), bf16),
        ((8, WIDTH), f32),
        ((3 * BLOCK, WIDTH), bf16),
        ((BLOCK, WIDTH), bf16),
        ((BLOCK, WIDTH), bf16),
        ((BLOCK, WIDTH), bf16),
        ((BLOCK, WIDTH), f32),
        ((BLOCK, WIDTH), bf16),
        ((8, WIDTH), f32),
    ]
    return pl.pallas_call(
        partial(backward_kernel, micro),
        in_specs=[pl.BlockSpec(memory_space=pltpu.SMEM)] + [anywhere] * (len(operands) - 1),
        out_specs=[in_hbm] * 6,
        out_shape=outs,
        scratch_shapes=[pltpu.VMEM(shape, kind) for shape, kind in scratch]
        + [pltpu.SemaphoreType.DMA((19,))],
        compiler_params=pltpu.CompilerParams(vmem_limit_bytes=48 * MIB),
        cost_estimate=pl.CostEstimate(
            flops=2 * 7 * BLOCK * WIDTH * WIDTH, bytes_accessed=16 << 20, transcendentals=0
        ),
        name="backward",
    )(*operands)


def ring_slots(size):
    if size == 4:
        return (2, 2, 2, 1, 1), {
            (0, 0): (0, 0), (1, 0): (0, 1),
            (0, 1): (3, 0), (1, 1): (1, 1),
            (0, 2): (1, 0), (1, 2): (2, 1),
            (0, 3): (2, 0), (1, 3): (4, 0),
        }
    return (2,) * size, {(m, f): (f, m) for m in range(2) for f in range(size)}


def ring_heads(size):
    return (1, 2) if size == 4 else (1,) * (size == 2)


def add(*values):
    return sum(value.astype(jnp.float32) for value in values)


def ring_sum(parts, axis, gain):
    size, head = group_dims()[axis], 0 if gain is None else HEAD_ROWS
    rows = parts[0].shape[0] // 2
    if size == 4:
        keep, up, down, late_up, late_down = parts
        up, down = turn(up, axis, 1), turn(down, axis, -1)
        late_up = add(late_up, up[head : head + rows]).astype(jnp.bfloat16)
        late_down = add(late_down, down[head + rows :]).astype(jnp.bfloat16)
        if head:
            late_up = jnp.concatenate([up[:head], late_up])
        late_up, late_down = turn(late_up, axis, 1), turn(late_down, axis, -1)
        total = [
            add(keep[:rows], late_up[head:], down[head : head + rows]),
            add(keep[rows:], up[head + rows :], late_down),
        ]
        if head:
            gain = add(gain, up[:head], down[:head], late_up[:head])
        return jnp.stack(total), gain
    if size == 2:
        other = turn(parts[1], axis, 1)
        if head:
            gain = add(gain, other[:head])
        return add(parts[0], other[head:]).reshape(2, rows, WIDTH), gain
    return parts[0].astype(jnp.float32).reshape(2, rows, WIDTH), gain


def collect_kernel(sections, dims, counts, *refs):
    place, spot, h_in, a_in = refs[:4]
    kept = refs[4 : 4 + 12 * sections]
    refs = refs[4 + 12 * sections :]
    frame_out, gain_out, outs = refs[0], refs[1], refs[2 : 2 + sum(counts)]
    left, right, term, frame, gain, gain_head, sems, out_sems = refs[2 + sum(counts) :]
    planes, size_y, size_x = dims
    share = WIDTH // (planes * size_y * size_x)
    own_y, own_x = spot[1], spot[2]
    names = ("frame", "g", "dq", "dk", "dv", "gain")

    def copies(at):
        found = []
        for micro in range(MICRO):
            results = dict(zip(names, kept[(at * MICRO + micro) * 6 : (at * MICRO + micro + 1) * 6]))
            rows = pl.ds(micro * BLOCK, BLOCK)
            pairs = [(results[name], right.at[n, rows]) for n, name in enumerate(("dq", "dk", "dv", "g"))]
            pairs += [(results["frame"], frame.at[micro]), (results["gain"], gain.at[micro])]
            pairs += [(h_in.at[micro], left.at[0, rows]), (a_in.at[micro], left.at[1, rows])]
            found += [
                pltpu.make_async_copy(source, target, sems.at[micro, n])
                for n, (source, target) in enumerate(pairs)
            ]
        return found

    for at in range(sections):

        @pl.when(place[0] == at)
        def _(at=at):
            started = copies(at)
            for copy in started:
                copy.start()
            for copy in started:
                copy.wait()

    frame_copy = pltpu.make_async_copy(frame, frame_out, out_sems.at[4, 0])
    frame_copy.start()
    gain_term = (gain[0, 0:1, :] + gain[1, 0:1, :]).astype(jnp.bfloat16)
    gain_head[...] = jnp.broadcast_to(gain_term, (HEAD_ROWS, WIDTH))
    started = [frame_copy]
    heads = [gain_out] + [outs[at].at[pl.ds(0, HEAD_ROWS), :] for at in ring_heads(size_x)]
    for at, target in enumerate(heads):
        copy = pltpu.make_async_copy(gain_head, target, out_sems.at[4, 1 + at])
        copy.start()
        started.append(copy)
    for m in range(4):
        pair = m // 2
        first_size, second_size = (size_x, size_y) if pair == 0 else (size_y, size_x)
        _, slots = ring_slots(first_size)
        arrays = outs[: counts[0]] if pair == 0 else outs[counts[0] :]
        factor = left[1 if m == 3 else 0]
        for n in range(0, WIDTH, 256):
            cols = slice(n, n + 256)
            term[m, :, cols] = dot_tn(factor, right[m, :, cols]).astype(jnp.bfloat16)
        number = 0
        for f in range(first_size):
            array, row = slots[m % 2, f]
            for r in range(second_size):
                ahead_x, ahead_y = (f, r) if pair == 0 else (r, f)
                column = lax.rem(own_y + ahead_y, size_y) * size_x + lax.rem(own_x + ahead_x, size_x)
                for plane in range(planes):
                    at = (plane * size_y * size_x + column) * share
                    to = ((row * second_size + r) * planes + plane) * share
                    if pair == 0 and array in ring_heads(first_size):
                        to += HEAD_ROWS
                    copy = pltpu.make_async_copy(
                        term.at[m, pl.ds(pl.multiple_of(at, share), share), :],
                        arrays[array].at[pl.ds(to, share), :],
                        out_sems.at[m, number],
                    )
                    copy.start()
                    started.append(copy)
                    number += 1
    for copy in started:
        copy.wait()


def collect(section, spot, h, a, kept):
    dims, sections = group_dims(), len(kept)
    planes, size_y, size_x = dims
    total = planes * size_y * size_x
    share = WIDTH // total
    anywhere = pl.BlockSpec(memory_space=pl.ANY)
    in_hbm = pl.BlockSpec(memory_space=pltpu.HBM)
    smem = pl.BlockSpec(memory_space=pltpu.SMEM)
    shapes, counts = [], []
    for first_size, second_size in ((size_x, size_y), (size_y, size_x)):
        rows, _ = ring_slots(first_size)
        counts.append(len(rows))
        for at, n in enumerate(rows):
            n = n * second_size * planes * share
            if len(counts) == 1 and at in ring_heads(first_size):
                n += HEAD_ROWS
            shapes.append(jax.ShapeDtypeStruct((n, WIDTH), jnp.bfloat16))
    operands = [in_place(result) for both in kept for results in both for result in results]
    outs = pl.pallas_call(
        partial(collect_kernel, sections, dims, counts),
        in_specs=[smem, smem] + [anywhere] * (2 + len(operands)),
        out_specs=[in_hbm] * (2 + len(shapes)),
        out_shape=[
            jax.ShapeDtypeStruct((MICRO, BLOCK, WIDTH), jnp.bfloat16),
            jax.ShapeDtypeStruct((HEAD_ROWS, WIDTH), jnp.bfloat16),
        ]
        + shapes,
        scratch_shapes=[
            pltpu.VMEM((2, MICRO * BLOCK, WIDTH), jnp.bfloat16),
            pltpu.VMEM((4, MICRO * BLOCK, WIDTH), jnp.bfloat16),
            pltpu.VMEM((4, WIDTH, WIDTH), jnp.bfloat16),
            pltpu.VMEM((MICRO, BLOCK, WIDTH), jnp.bfloat16),
            pltpu.VMEM((MICRO, 8, WIDTH), jnp.float32),
            pltpu.VMEM((HEAD_ROWS, WIDTH), jnp.bfloat16),
            pltpu.SemaphoreType.DMA((MICRO, 8)),
            pltpu.SemaphoreType.DMA((5, max(total, 4))),
        ],
        compiler_params=pltpu.CompilerParams(vmem_limit_bytes=48 * MIB),
        cost_estimate=pl.CostEstimate(
            flops=2 * 8 * BLOCK * WIDTH * WIDTH, bytes_accessed=14 << 20, transcendentals=0
        ),
        name="collect",
    )(section, spot, h, a, *operands)
    frame, gain = outs[:2]
    return frame, gain, [outs[2 : 2 + counts[0]], outs[2 + counts[0] :]]


def sum_terms(parts, gain, plane):
    dims, totals = group_dims(), []
    for pair, (first, second) in zip(parts, ((2, 1), (1, 2))):
        own = gain if first == 2 else None
        value, own = ring_sum(pair, first, own)
        value = value.astype(jnp.bfloat16).reshape(2, dims[second], -1, WIDTH)
        rows, slots = ring_slots(dims[second])
        arrays = [[None] * n for n in rows]
        for (m, f), (array, row) in slots.items():
            arrays[array][row] = value[m, f]
        if own is not None:
            own = own.astype(jnp.bfloat16)
            for array in ring_heads(dims[second]):
                arrays[array].insert(0, own)
        value, own = ring_sum([jnp.concatenate(array) for array in arrays], second, own)
        totals.append(value)
        gain = gain if own is None else own
    value = jnp.concatenate(totals)
    if dims[0] == 1:
        return value, gain
    share = value.shape[1] // 2
    value = value.reshape(4, 2, share, WIDTH)
    other = lax.dynamic_index_in_dim(value, 1 - plane, 1, keepdims=False).astype(jnp.bfloat16)
    own = lax.dynamic_index_in_dim(value, plane, 1, keepdims=False)
    other = jnp.concatenate([gain.astype(jnp.bfloat16), other.reshape(4 * share, WIDTH)])
    other = turn(other, 0, 1)
    return add(own, other[HEAD_ROWS:].reshape(own.shape)), add(gain, other[:HEAD_ROWS])


def segments(lengths, block):
    bounds = jnp.cumsum(lengths, axis=1)
    total = lax.axis_size(GROUP) * BLOCK
    places = (block - 2) * BLOCK + jnp.arange(5 * BLOCK, dtype=jnp.int32)
    counted = jnp.sum((places[None, :, None] >= bounds[:, None, :]).astype(jnp.int32), axis=2)
    return jnp.where(places < 0, -1, jnp.where(places >= total, -2, counted))


def body(checkpoints, cotangent, weights, gains, lengths):
    sections, section = lax.axis_size("section"), lax.axis_index("section")
    block = lax.axis_index(GROUP)
    share = gains.shape[1]

    planes, size_y, _ = group_dims()
    dp = lax.axis_index("dp")
    spot = jnp.stack([dp // size_y, dp % size_y, lax.axis_index("fsdp")]).astype(jnp.int32)
    spread = lax.dynamic_update_slice(
        jnp.zeros((HEAD_ROWS, WIDTH), jnp.bfloat16), gains, (0, block * share)
    )
    pairs, gain = gather_weights(weights[0], spread)
    gain = jnp.broadcast_to(gain[0:1].astype(jnp.float32), (8, WIDTH))

    x = checkpoints[0]
    left, right = shift(x, 1), shift(x, -1)
    parts = (shift(left, 1), left, x, right, shift(right, -1))
    source = max(sections - 3, 0)
    cot = (cotangent, hop(cotangent, source, sections - 1, 1), hop(cotangent, source, sections - 1, 2))

    segs = segments(lengths, block)
    gathered, h, q, k, v, p, pt, o, a = forward(
        spot, pairs, parts, gain, segs[:, :, None], segs[:, None, :]
    )
    kept = (q, k, v, p, pt, o)

    kept_grads = [[None] * MICRO for _ in range(sections)]
    incoming = [[part[micro] for part in cot] for micro in range(MICRO)]
    for at in range(sections - 1, -1, -1):
        flag = (section == at).astype(jnp.int32).reshape(1)
        for micro in range(MICRO):
            grads = list(backward(micro, flag, incoming[micro], gathered, kept, x, gain))
            if at > 0:
                before = incoming[micro - 1] if micro > 0 else []
                if at % 2 == 1:
                    grads[0] = tie(grads[0], *before)
                    incoming[micro] = [hop(grads[0], at, at - 1, back) for back in range(3)]
                else:
                    grads[0] = tie(grads[0], *before[:1])
                    own = tie(hop(grads[0], at, at - 1, 0), *before[1:])
                    incoming[micro] = [own] + [hop(own, at - 1, at - 1, back) for back in (1, 2)]
            kept_grads[at][micro] = grads

    place = section.astype(jnp.int32).reshape(1)
    frame, gain_part, parts = collect(place, spot, h, a, kept_grads)
    weight_part, gain_sum = sum_terms(parts, gain_part, spot[0])
    gain_sum = lax.dynamic_slice(gain_sum, (0, block * share), (1, share))
    return (frame[None], weight_part[None], gain_sum)


def solution(mesh):
    placed = (
        P("section", None, ("dp", "fsdp"), None),
        P(None, ("dp", "fsdp"), None),
        P("section", None, ("dp", "fsdp"), None),
        P("section", ("dp", "fsdp")),
        P(),
    )
    return jax.shard_map(
        body,
        mesh=mesh,
        in_specs=placed,
        out_specs=(
            P("section", None, ("dp", "fsdp"), None),
            P("section", None, ("dp", "fsdp"), None),
            P("section", ("dp", "fsdp")),
        ),
        check_vma=False,
    )
```

```python
from functools import partial
import math

import jax
import jax.numpy as jnp
from jax import lax
from jax.experimental import pallas as pl
from jax.experimental.pallas import tpu as pltpu
from jax.sharding import PartitionSpec as P

HEAD = 128
BLOCK = 128
WIDTH = 1024
HEADS = WIDTH // HEAD
MICRO = 2
SCALE = 1.0 / math.sqrt(HEAD)
GROUP = ("dp", "fsdp")
EVERY = ("dp", "section", "fsdp")
MIB = 1024 * 1024
HEAD_ROWS = 16


def dot(left, right):
    return lax.dot_general(left, right, (((1,), (0,)), ((), ())), preferred_element_type=jnp.float32)


def dot_nt(left, right):
    return lax.dot_general(left, right, (((1,), (1,)), ((), ())), preferred_element_type=jnp.float32)


def dot_tn(left, right):
    return lax.dot_general(left, right, (((0,), (0,)), ((), ())), preferred_element_type=jnp.float32)


def shift(value, steps):
    count = lax.axis_size(GROUP)
    pairs = [(b, b + steps) for b in range(count) if 0 <= b + steps < count]
    return lax.ppermute(value, GROUP, pairs)


def hop(value, source, target, back):
    sections, rows = lax.axis_size("section"), lax.axis_size("fsdp")
    count = lax.axis_size(GROUP)

    def place(section, block):
        return (block // rows * sections + section) * rows + block % rows

    pairs = [(place(source, b), place(target, b - back)) for b in range(back, count)]
    return lax.ppermute(value, EVERY, pairs)


def group_dims():
    dp, fsdp = lax.axis_size("dp"), lax.axis_size("fsdp")
    planes = 2 if dp % 2 == 0 else 1
    return (planes, dp // planes, fsdp)


def turn(value, axis, steps):
    dims = group_dims()
    pairs = []
    for z in range(dims[0]):
        for y in range(dims[1]):
            for x in range(dims[2]):
                at = [z, y, x]
                to = list(at)
                to[axis] = (at[axis] + steps) % dims[axis]
                index = lambda p: (p[0] * dims[1] + p[1]) * dims[2] + p[2]
                pairs.append((index(at), index(to)))
    return lax.ppermute(value, GROUP, pairs)


def tie_kernel(*refs):
    del refs


def tie(value, *others):
    if not others:
        return value
    anywhere = pl.BlockSpec(memory_space=pl.ANY)
    return pl.pallas_call(
        tie_kernel,
        in_specs=[anywhere] * (1 + len(others)),
        out_specs=anywhere,
        out_shape=jax.ShapeDtypeStruct(value.shape, value.dtype),
        input_output_aliases={0: 0},
        name="tie",
    )(value, *others)


def ring(value, axis, head):
    size, half = group_dims()[axis], (value.shape[0] - head) // 2
    both = (head, head + half)
    pieces, heads = [(0, value, both)], [value[:head]]
    if size == 2:
        other = turn(value, axis, 1)
        pieces.append((1, other, both))
        heads.append(other[:head])
    if size == 4:
        behind, ahead = turn(value, axis, 1), turn(value, axis, -1)
        up = turn(behind[: head + half], axis, 1)
        down = turn(ahead[head + half :], axis, -1)
        pieces += [(1, ahead, both), (2, up, (head, None)), (2, down, (None, 0)), (3, behind, both)]
        heads += [ahead[:head], behind[:head], up[:head]]
    return pieces, sum(heads[1:], heads[0])


def arrange_kernel(layouts, dims, *refs):
    spot, refs = refs[0], refs[1:]
    count = sum(len(layout) + (axis == 2) for axis, layout in layouts)
    ins, outs, sems = refs[:count], refs[count : count + 2], refs[count + 2]
    copies, offset = [], 0
    for out, (axis, layout) in zip(outs, layouts):
        head, size = int(axis == 2), dims[axis]
        if head:
            copies.append((ins[offset], out.at[pl.ds(0, 1)]))
            offset += 1
        for place, begins in layout:
            for m, begin in enumerate(begins):
                for plane in range(dims[0]):
                    if begin is not None:
                        to = head + (m * dims[0] + plane) * size
                        to += lax.rem(spot[axis] + place, size)
                        source = ins[offset].at[pl.ds(begin + plane, 1)]
                        copies.append((source, out.at[pl.ds(to, 1)]))
            offset += 1
    copies = [
        pltpu.make_async_copy(source, target, sems.at[at])
        for at, (source, target) in enumerate(copies)
    ]
    for copy in copies:
        copy.start()
    for copy in copies:
        copy.wait()


def arrange(spot, rings):
    dims = group_dims()
    operands, layouts, shapes = [], [], []
    for axis, head, pieces in rings:
        operands += ([] if head is None else [head]) + [piece for _, piece, _ in pieces]
        layouts.append((axis, [(place, begins) for place, _, begins in pieces]))
        units = (head is not None) + 2 * dims[0] * dims[axis]
        shapes.append(pltpu.HBM((units,) + pieces[0][1].shape[1:], jnp.bfloat16))
    return pl.pallas_call(
        partial(arrange_kernel, layouts, dims),
        in_specs=[pl.BlockSpec(memory_space=pltpu.SMEM)]
        + [pl.BlockSpec(memory_space=pl.ANY)] * len(operands),
        out_specs=[pl.BlockSpec(memory_space=pl.ANY)] * 2,
        out_shape=shapes,
        scratch_shapes=[pltpu.SemaphoreType.DMA((sum(shape.shape[0] for shape in shapes),))],
        name="arrange",
    )(spot, *operands)


def gather_weights(shard, gain, spot):
    value = jnp.concatenate([gain, shard])
    gains, planes = gain, [value]
    if group_dims()[0] == 2:
        other = turn(value, 0, 1)
        gains = gain + other[:1]
        planes = [jnp.where(spot[0] == 0, value, other), jnp.where(spot[0] == 0, other, value)]
    rows = [plane[1 + m : 2 + m] for m in range(4) for plane in planes]
    half = len(rows) // 2
    first, gains = ring(jnp.concatenate([gains] + rows[:half]), 2, 1)
    second, _ = ring(jnp.concatenate(rows[half:]), 1, 0)
    first, second = arrange(spot, [(2, gains, first), (1, None, second)])
    first, gains = ring(first, 1, 1)
    second, _ = ring(second, 2, 0)
    return [first, second], gains


def normed(x, gain):
    as_float = x.astype(jnp.float32)
    rscale = lax.rsqrt(jnp.mean(as_float * as_float, axis=-1, keepdims=True) + 1e-06)
    return (as_float * rscale * gain).astype(jnp.bfloat16)


def forward_kernel(layout, dims, *refs):
    count = sum(len(pieces) for pieces in layout)
    spot, pieces, refs = refs[0], refs[1 : 1 + count], refs[1 + count :]
    l2, l1, own, r1, r2, gain, seg_col, seg_row = refs[:8]
    w_out, h_out, q_out, k_out, v_out, p_out, pt_out, o_out, a_out = refs[8:17]
    w, h5, q3, k5, v5, barred, sems = refs[17:]
    step = pl.program_id(0)
    planes, size_y, size_x = dims

    def loads(pair):
        copies, offset = [], sum(len(pieces) for pieces in layout[:pair])
        axis, units = (1, size_x) if pair == 0 else (2, size_y)
        for at, (place, begins) in enumerate(layout[pair]):
            to = lax.rem(spot[axis] + place, dims[axis])
            for m, begin in enumerate(begins):
                for plane in range(planes):
                    if begin is not None:
                        target = w.at[2 * pair + m, plane]
                        target = target.at[to] if pair == 0 else target.at[:, to]
                        source = pieces[offset + at].at[pl.ds(begin + plane * units, units)]
                        copies.append(
                            pltpu.make_async_copy(source, target, sems.at[pair, len(copies)])
                        )
        return copies

    def projection(m, cols):
        return w[m, :, :, :, :, cols].reshape(WIDTH, 256)

    def store(pair):
        half = pl.ds(2 * pair, 2)
        return pltpu.make_async_copy(w.at[half], w_out.at[half], sems.at[2, pair])

    @pl.when(step == 0)
    def _():
        for copy in loads(0) + loads(1):
            copy.start()

    gain_row = gain[0:1, :]
    for at, part in enumerate((l2, l1, own, r1, r2)):
        h5[at * BLOCK : (at + 1) * BLOCK, :] = normed(part[0], gain_row)
    h_out[0] = h5[2 * BLOCK : 3 * BLOCK, :]

    @pl.when(step == 0)
    def _():
        for copy in loads(0):
            copy.wait()
        store(0).start()

    for n in range(0, WIDTH, 256):
        cols = slice(n, n + 256)
        q3[:, cols] = dot(h5[2 * BLOCK :, :], projection(0, cols)).astype(jnp.bfloat16)
        k5[:, cols] = dot(h5[...], projection(1, cols)).astype(jnp.bfloat16)

    @pl.when(step == 0)
    def _():
        for copy in loads(1):
            copy.wait()
        store(1).start()

    for n in range(0, WIDTH, 256):
        cols = slice(n, n + 256)
        v5[:, cols] = dot(h5[...], projection(2, cols)).astype(jnp.bfloat16)
    q_out[0] = q3[...]
    k_out[0] = k5[: 3 * BLOCK, :]
    v_out[0] = v5[: 3 * BLOCK, :]
    for j in range(3):
        allowed = (
            seg_col[0, (j + 2) * BLOCK : (j + 3) * BLOCK, 0:1]
            == seg_row[0, 0:1, j * BLOCK : (j + 3) * BLOCK]
        )
        barred[j * BLOCK : (j + 1) * BLOCK, :] = jnp.where(allowed, 0.0, -1e30)
    for head in range(HEADS):
        cols = slice(head * HEAD, (head + 1) * HEAD)
        for j in range(3):
            rows = slice(j * BLOCK, (j + 1) * BLOCK)
            keys = slice(j * BLOCK, (j + 3) * BLOCK)
            score = dot_nt(q3[rows, cols], k5[keys, cols]) + barred[rows, :]
            top = jnp.max(score, axis=-1, keepdims=True)
            expo = jnp.exp((score - top) * SCALE)
            p = expo * (1.0 / jnp.sum(expo, axis=-1, keepdims=True))
            high = p.astype(jnp.bfloat16)
            low = (p - high.astype(jnp.float32)).astype(jnp.bfloat16)
            both = dot(jnp.concatenate([high, low]), v5[keys, cols])
            mixed = both[:BLOCK]
            o_out[0, rows, cols] = mixed + both[BLOCK:]
            if j == 0:
                p_out[0, head] = p
                a_out[0, :, cols] = mixed.astype(jnp.bfloat16)
            own_keys = slice((2 - j) * BLOCK, (3 - j) * BLOCK)
            pt_out[0, head, :, rows] = p[:, own_keys].T

    @pl.when(step == MICRO - 1)
    def _():
        store(0).wait()
        store(1).wait()


def forward(spot, pairs, parts, gain, seg_col, seg_row):
    anywhere = pl.BlockSpec(memory_space=pl.ANY)
    pieces = [piece for pair in pairs for _, piece, _ in pair]
    layout = [[(place, begins) for place, _, begins in pair] for pair in pairs]
    dims = group_dims()
    wide = (4, *dims, WIDTH // (dims[0] * dims[1] * dims[2]), WIDTH)

    def per_micro(shape):
        return pl.BlockSpec((1,) + shape, lambda m: (m,) + (0,) * len(shape))

    def whole(shape):
        return pl.BlockSpec(shape, lambda m: (0,) * len(shape), pipeline_mode=pl.Buffered(1))

    outs = [
        ((BLOCK, WIDTH), jnp.bfloat16),
        ((3 * BLOCK, WIDTH), jnp.bfloat16),
        ((3 * BLOCK, WIDTH), jnp.bfloat16),
        ((3 * BLOCK, WIDTH), jnp.bfloat16),
        ((HEADS, BLOCK, 3 * BLOCK), jnp.float32),
        ((HEADS, BLOCK, 3 * BLOCK), jnp.float32),
        ((3 * BLOCK, WIDTH), jnp.float32),
        ((BLOCK, WIDTH), jnp.bfloat16),
    ]
    return pl.pallas_call(
        partial(forward_kernel, layout, dims),
        grid=(MICRO,),
        in_specs=[pl.BlockSpec(memory_space=pltpu.SMEM)]
        + [anywhere] * len(pieces)
        + [per_micro((BLOCK, WIDTH))] * 5
        + [
            whole((8, WIDTH)),
            per_micro((5 * BLOCK, 1)),
            per_micro((1, 5 * BLOCK)),
        ],
        out_specs=[anywhere] + [per_micro(shape) for shape, _ in outs],
        out_shape=[jax.ShapeDtypeStruct(wide, jnp.bfloat16)]
        + [jax.ShapeDtypeStruct((MICRO,) + shape, kind) for shape, kind in outs],
        scratch_shapes=[
            pltpu.VMEM(wide, jnp.bfloat16),
            pltpu.VMEM((5 * BLOCK, WIDTH), jnp.bfloat16),
            pltpu.VMEM((3 * BLOCK, WIDTH), jnp.bfloat16),
            pltpu.VMEM((5 * BLOCK, WIDTH), jnp.bfloat16),
            pltpu.VMEM((5 * BLOCK, WIDTH), jnp.bfloat16),
            pltpu.VMEM((3 * BLOCK, 3 * BLOCK), jnp.float32),
            pltpu.SemaphoreType.DMA((3, 16)),
        ],
        compiler_params=pltpu.CompilerParams(vmem_limit_bytes=44 * MIB),
        cost_estimate=pl.CostEstimate(
            flops=2 * 2 * 15 * BLOCK * WIDTH * WIDTH, bytes_accessed=28 << 20, transcendentals=0
        ),
        name="forward",
    )(spot, *pieces, *parts, gain, seg_col, seg_row)


def backward_kernel(micro, *refs):
    flag, g0, g1, g2, w, q_in, k_in, v_in, p_in, pt_in, o_in, x_in, gain_in = refs[:13]
    refs = refs[13:]
    frame_out, g_out, dq_out, dk_out, dv_out, gain_out = refs[:6]
    g, wv, q, k, v, p, pt, o, x, gain, da, dq, dk, dv, dh, frame, gain_sum, sems = refs[6:]

    @pl.when(flag[0] == 1)
    def _():
        def move(at, source, target):
            copy = pltpu.make_async_copy(source, target, sems.at[at])
            copy.start()
            return copy

        load_g = [
            move(at, part, g.at[pl.ds(at * BLOCK, BLOCK), :]) for at, part in enumerate((g0, g1, g2))
        ]
        load_wo = move(3, w.at[3], wv.at[3])
        load_o = move(4, o_in.at[micro], o)
        load_v = move(5, v_in.at[micro], v)
        load_p = move(6, p_in.at[micro], p)
        load_k = move(7, k_in.at[micro], k)
        load_pt = move(8, pt_in.at[micro], pt)
        load_q = move(9, q_in.at[micro], q)
        load_w = move(10, w.at[pl.ds(0, 3)], wv.at[pl.ds(0, 3)])
        load_x = move(11, x_in.at[micro], x)
        load_gain = move(12, gain_in, gain)
        for copy in load_g:
            copy.wait()
        load_wo.wait()
        store_g = move(13, g.at[pl.ds(0, BLOCK), :], g_out)
        for n in range(0, WIDTH, 256):
            cols = slice(n, n + 256)
            da[:, cols] = dot_nt(g[...], wv[3, cols, :]).astype(jnp.bfloat16)
        for copy in (load_o, load_v, load_p, load_k, load_pt, load_q):
            copy.wait()
        for head in range(HEADS):
            cols = slice(head * HEAD, (head + 1) * HEAD)
            da_h = da[:, cols]
            inner = jnp.sum(da_h.astype(jnp.float32) * o[:, cols], axis=-1, keepdims=True)
            dp = dot_nt(da_h[:BLOCK], v[:, cols])
            ds = (p[head] * (dp - inner[:BLOCK]) * SCALE).astype(jnp.bfloat16)
            dq[:, cols] = dot(ds, k[:, cols]).astype(jnp.bfloat16)
            inner_row = jnp.broadcast_to(inner, (3 * BLOCK, HEAD)).T
            p_t = pt[head]
            dp_t = dot_nt(v[2 * BLOCK :, cols], da_h)
            ds_t = (p_t * (dp_t - inner_row) * SCALE).astype(jnp.bfloat16)
            dk[:, cols] = dot(ds_t, q[:, cols]).astype(jnp.bfloat16)
            dv[:, cols] = dot(p_t.astype(jnp.bfloat16), da_h).astype(jnp.bfloat16)
        stores = [
            store_g,
            move(14, dq, dq_out),
            move(15, dk, dk_out),
            move(16, dv, dv_out),
        ]
        load_w.wait()
        for n in range(0, WIDTH, 256):
            cols = slice(n, n + 256)
            dh[:, cols] = (
                dot_nt(dq[...], wv[0, cols, :])
                + dot_nt(dk[...], wv[1, cols, :])
                + dot_nt(dv[...], wv[2, cols, :])
            )
        load_x.wait()
        load_gain.wait()
        as_float = x[...].astype(jnp.float32)
        rscale = lax.rsqrt(jnp.mean(as_float * as_float, axis=-1, keepdims=True) + 1e-06)
        d_normed = dh[...]
        scaled = gain[0:1, :] * d_normed
        cubic = rscale * rscale * rscale
        frame_f = (
            g[:BLOCK, :].astype(jnp.float32)
            + rscale * scaled
            - as_float * (cubic * jnp.mean(scaled * as_float, axis=-1, keepdims=True))
        )
        frame[...] = frame_f.astype(jnp.bfloat16)
        stores.append(move(17, frame, frame_out))
        term = jnp.sum(d_normed * as_float * rscale, axis=0, keepdims=True)
        gain_sum[...] = jnp.broadcast_to(term, (8, WIDTH))
        stores.append(move(18, gain_sum, gain_out))
        for copy in stores:
            copy.wait()


def in_place(value):
    return pltpu.with_memory_space_constraint(value, pltpu.HBM)


def backward(micro, flag, incoming, w, kept, x, gain):
    block = pltpu.HBM((BLOCK, WIDTH), jnp.bfloat16)
    outs = [block] * 5 + [pltpu.HBM((8, WIDTH), jnp.float32)]
    operands = [flag, *incoming] + [in_place(value) for value in (w, *kept, x, gain)]
    anywhere = pl.BlockSpec(memory_space=pl.ANY)
    in_hbm = pl.BlockSpec(memory_space=pltpu.HBM)
    bf16, f32 = jnp.bfloat16, jnp.float32
    scratch = [
        ((3 * BLOCK, WIDTH), bf16),
        ((4, WIDTH, WIDTH), bf16),
        ((3 * BLOCK, WIDTH), bf16),
        ((3 * BLOCK, WIDTH), bf16),
        ((3 * BLOCK, WIDTH), bf16),
        ((HEADS, BLOCK, 3 * BLOCK), f32),
        ((HEADS, BLOCK, 3 * BLOCK), f32),
        ((3 * BLOCK, WIDTH), f32),
        ((BLOCK, WIDTH), bf16),
        ((8, WIDTH), f32),
        ((3 * BLOCK, WIDTH), bf16),
        ((BLOCK, WIDTH), bf16),
        ((BLOCK, WIDTH), bf16),
        ((BLOCK, WIDTH), bf16),
        ((BLOCK, WIDTH), f32),
        ((BLOCK, WIDTH), bf16),
        ((8, WIDTH), f32),
    ]
    return pl.pallas_call(
        partial(backward_kernel, micro),
        in_specs=[pl.BlockSpec(memory_space=pltpu.SMEM)] + [anywhere] * (len(operands) - 1),
        out_specs=[in_hbm] * 6,
        out_shape=outs,
        scratch_shapes=[pltpu.VMEM(shape, kind) for shape, kind in scratch]
        + [pltpu.SemaphoreType.DMA((19,))],
        compiler_params=pltpu.CompilerParams(vmem_limit_bytes=48 * MIB),
        cost_estimate=pl.CostEstimate(
            flops=2 * 7 * BLOCK * WIDTH * WIDTH, bytes_accessed=16 << 20, transcendentals=0
        ),
        name="backward",
    )(*operands)


def ring_slots(size):
    if size == 4:
        return (2, 2, 2, 1, 1), {
            (0, 0): (0, 0), (1, 0): (0, 1),
            (0, 1): (3, 0), (1, 1): (1, 1),
            (0, 2): (1, 0), (1, 2): (2, 1),
            (0, 3): (2, 0), (1, 3): (4, 0),
        }
    return (2,) * size, {(m, f): (f, m) for m in range(2) for f in range(size)}


def ring_heads(size):
    return (1, 2) if size == 4 else (1,) * (size == 2)


def add(*values):
    return sum(value.astype(jnp.float32) for value in values)


def ring_sum(parts, axis, gain):
    size, head = group_dims()[axis], 0 if gain is None else HEAD_ROWS
    rows = parts[0].shape[0] // 2
    if size == 4:
        keep, up, down, late_up, late_down = parts
        up, down = turn(up, axis, 1), turn(down, axis, -1)
        late_up = add(late_up, up[head : head + rows]).astype(jnp.bfloat16)
        late_down = add(late_down, down[head + rows :]).astype(jnp.bfloat16)
        if head:
            late_up = jnp.concatenate([up[:head], late_up])
        late_up, late_down = turn(late_up, axis, 1), turn(late_down, axis, -1)
        total = [
            add(keep[:rows], late_up[head:], down[head : head + rows]),
            add(keep[rows:], up[head + rows :], late_down),
        ]
        if head:
            gain = add(gain, up[:head], down[:head], late_up[:head])
        return jnp.stack(total), gain
    if size == 2:
        other = turn(parts[1], axis, 1)
        if head:
            gain = add(gain, other[:head])
        return add(parts[0], other[head:]).reshape(2, rows, WIDTH), gain
    return parts[0].astype(jnp.float32).reshape(2, rows, WIDTH), gain


def collect_kernel(sections, dims, counts, *refs):
    place, spot, h_in, a_in = refs[:4]
    kept = refs[4 : 4 + 12 * sections]
    refs = refs[4 + 12 * sections :]
    frame_out, gain_out, outs = refs[0], refs[1], refs[2 : 2 + sum(counts)]
    left, right, term, frame, gain, gain_head, sems, out_sems = refs[2 + sum(counts) :]
    planes, size_y, size_x = dims
    share = WIDTH // (planes * size_y * size_x)
    own_y, own_x = spot[1], spot[2]
    names = ("frame", "g", "dq", "dk", "dv", "gain")

    def copies(at):
        found = []
        for micro in range(MICRO):
            results = dict(zip(names, kept[(at * MICRO + micro) * 6 : (at * MICRO + micro + 1) * 6]))
            rows = pl.ds(micro * BLOCK, BLOCK)
            pairs = [(results[name], right.at[n, rows]) for n, name in enumerate(("dq", "dk", "dv", "g"))]
            pairs += [(results["frame"], frame.at[micro]), (results["gain"], gain.at[micro])]
            pairs += [(h_in.at[micro], left.at[0, rows]), (a_in.at[micro], left.at[1, rows])]
            found += [
                pltpu.make_async_copy(source, target, sems.at[micro, n])
                for n, (source, target) in enumerate(pairs)
            ]
        return found

    for at in range(sections):

        @pl.when(place[0] == at)
        def _(at=at):
            started = copies(at)
            for copy in started:
                copy.start()
            for copy in started:
                copy.wait()

    frame_copy = pltpu.make_async_copy(frame, frame_out, out_sems.at[4, 0])
    frame_copy.start()
    gain_term = (gain[0, 0:1, :] + gain[1, 0:1, :]).astype(jnp.bfloat16)
    gain_head[...] = jnp.broadcast_to(gain_term, (HEAD_ROWS, WIDTH))
    started = [frame_copy]
    heads = [gain_out] + [outs[at].at[pl.ds(0, HEAD_ROWS), :] for at in ring_heads(size_x)]
    for at, target in enumerate(heads):
        copy = pltpu.make_async_copy(gain_head, target, out_sems.at[4, 1 + at])
        copy.start()
        started.append(copy)
    for m in range(4):
        pair = m // 2
        first_size, second_size = (size_x, size_y) if pair == 0 else (size_y, size_x)
        _, slots = ring_slots(first_size)
        arrays = outs[: counts[0]] if pair == 0 else outs[counts[0] :]
        factor = left[1 if m == 3 else 0]
        for n in range(0, WIDTH, 256):
            cols = slice(n, n + 256)
            term[m, :, cols] = dot_tn(factor, right[m, :, cols]).astype(jnp.bfloat16)
        number = 0
        for f in range(first_size):
            array, row = slots[m % 2, f]
            for r in range(second_size):
                ahead_x, ahead_y = (f, r) if pair == 0 else (r, f)
                column = lax.rem(own_y + ahead_y, size_y) * size_x + lax.rem(own_x + ahead_x, size_x)
                for plane in range(planes):
                    at = (plane * size_y * size_x + column) * share
                    to = ((row * second_size + r) * planes + plane) * share
                    if pair == 0 and array in ring_heads(first_size):
                        to += HEAD_ROWS
                    copy = pltpu.make_async_copy(
                        term.at[m, pl.ds(pl.multiple_of(at, share), share), :],
                        arrays[array].at[pl.ds(to, share), :],
                        out_sems.at[m, number],
                    )
                    copy.start()
                    started.append(copy)
                    number += 1
    for copy in started:
        copy.wait()


def collect(section, spot, h, a, kept):
    dims, sections = group_dims(), len(kept)
    planes, size_y, size_x = dims
    total = planes * size_y * size_x
    share = WIDTH // total
    anywhere = pl.BlockSpec(memory_space=pl.ANY)
    in_hbm = pl.BlockSpec(memory_space=pltpu.HBM)
    smem = pl.BlockSpec(memory_space=pltpu.SMEM)
    shapes, counts = [], []
    for first_size, second_size in ((size_x, size_y), (size_y, size_x)):
        rows, _ = ring_slots(first_size)
        counts.append(len(rows))
        for at, n in enumerate(rows):
            n = n * second_size * planes * share
            if len(counts) == 1 and at in ring_heads(first_size):
                n += HEAD_ROWS
            shapes.append(jax.ShapeDtypeStruct((n, WIDTH), jnp.bfloat16))
    operands = [in_place(result) for both in kept for results in both for result in results]
    outs = pl.pallas_call(
        partial(collect_kernel, sections, dims, counts),
        in_specs=[smem, smem] + [anywhere] * (2 + len(operands)),
        out_specs=[in_hbm] * (2 + len(shapes)),
        out_shape=[
            jax.ShapeDtypeStruct((MICRO, BLOCK, WIDTH), jnp.bfloat16),
            jax.ShapeDtypeStruct((HEAD_ROWS, WIDTH), jnp.bfloat16),
        ]
        + shapes,
        scratch_shapes=[
            pltpu.VMEM((2, MICRO * BLOCK, WIDTH), jnp.bfloat16),
            pltpu.VMEM((4, MICRO * BLOCK, WIDTH), jnp.bfloat16),
            pltpu.VMEM((4, WIDTH, WIDTH), jnp.bfloat16),
            pltpu.VMEM((MICRO, BLOCK, WIDTH), jnp.bfloat16),
            pltpu.VMEM((MICRO, 8, WIDTH), jnp.float32),
            pltpu.VMEM((HEAD_ROWS, WIDTH), jnp.bfloat16),
            pltpu.SemaphoreType.DMA((MICRO, 8)),
            pltpu.SemaphoreType.DMA((5, max(total, 4))),
        ],
        compiler_params=pltpu.CompilerParams(vmem_limit_bytes=48 * MIB),
        cost_estimate=pl.CostEstimate(
            flops=2 * 8 * BLOCK * WIDTH * WIDTH, bytes_accessed=14 << 20, transcendentals=0
        ),
        name="collect",
    )(section, spot, h, a, *operands)
    frame, gain = outs[:2]
    return frame, gain, [outs[2 : 2 + counts[0]], outs[2 + counts[0] :]]


def sum_terms(parts, gain, plane):
    dims, totals = group_dims(), []
    for pair, (first, second) in zip(parts, ((2, 1), (1, 2))):
        own = gain if first == 2 else None
        value, own = ring_sum(pair, first, own)
        value = value.astype(jnp.bfloat16).reshape(2, dims[second], -1, WIDTH)
        rows, slots = ring_slots(dims[second])
        arrays = [[None] * n for n in rows]
        for (m, f), (array, row) in slots.items():
            arrays[array][row] = value[m, f]
        if own is not None:
            own = own.astype(jnp.bfloat16)
            for array in ring_heads(dims[second]):
                arrays[array].insert(0, own)
        value, own = ring_sum([jnp.concatenate(array) for array in arrays], second, own)
        totals.append(value)
        gain = gain if own is None else own
    value = jnp.concatenate(totals)
    if dims[0] == 1:
        return value, gain
    share = value.shape[1] // 2
    value = value.reshape(4, 2, share, WIDTH)
    other = lax.dynamic_index_in_dim(value, 1 - plane, 1, keepdims=False).astype(jnp.bfloat16)
    own = lax.dynamic_index_in_dim(value, plane, 1, keepdims=False)
    other = jnp.concatenate([gain.astype(jnp.bfloat16), other.reshape(4 * share, WIDTH)])
    other = turn(other, 0, 1)
    return add(own, other[HEAD_ROWS:].reshape(own.shape)), add(gain, other[:HEAD_ROWS])


def segments(lengths, block):
    bounds = jnp.cumsum(lengths, axis=1)
    total = lax.axis_size(GROUP) * BLOCK
    places = (block - 2) * BLOCK + jnp.arange(5 * BLOCK, dtype=jnp.int32)
    counted = jnp.sum((places[None, :, None] >= bounds[:, None, :]).astype(jnp.int32), axis=2)
    return jnp.where(places < 0, -1, jnp.where(places >= total, -2, counted))


def body(checkpoints, cotangent, weights, gains, lengths):
    sections, section = lax.axis_size("section"), lax.axis_index("section")
    block = lax.axis_index(GROUP)
    share = gains.shape[1]

    planes, size_y, _ = group_dims()
    dp = lax.axis_index("dp")
    spot = jnp.stack([dp // size_y, dp % size_y, lax.axis_index("fsdp")]).astype(jnp.int32)
    spread = lax.dynamic_update_slice(
        jnp.zeros((1, share, WIDTH), jnp.bfloat16), gains[None], (0, 0, block * share)
    )
    pairs, gain = gather_weights(weights[0], spread, spot)
    gain = jnp.broadcast_to(gain[0, 0:1].astype(jnp.float32), (8, WIDTH))

    x = checkpoints[0]
    left, right = shift(x, 1), shift(x, -1)
    parts = (shift(left, 1), left, x, right, shift(right, -1))
    source = max(sections - 3, 0)
    cot = (cotangent, hop(cotangent, source, sections - 1, 1), hop(cotangent, source, sections - 1, 2))

    segs = segments(lengths, block)
    gathered, h, q, k, v, p, pt, o, a = forward(
        spot, pairs, parts, gain, segs[:, :, None], segs[:, None, :]
    )
    gathered = gathered.reshape(4, WIDTH, WIDTH)
    kept = (q, k, v, p, pt, o)

    kept_grads = [[None] * MICRO for _ in range(sections)]
    arriving, behind = ([part[micro] for part in cot] for micro in range(MICRO))
    for at in range(sections - 1, -1, -1):
        flag = (section == at).astype(jnp.int32).reshape(1)
        first = list(backward(0, flag, arriving, gathered, kept, x, gain))
        leaving = first[0]
        if at > 0:
            arriving = [hop(leaving, at, at - 1, back) for back in (2, 1, 0)][::-1]
        if at < sections - 1:
            second[0] = tie(second[0], arriving[0] if at > 0 else leaving)
            behind = [hop(second[0], at + 1, at, back) for back in (2, 1, 0)][::-1]
        second = list(backward(1, flag, behind, gathered, kept, x, gain))
        kept_grads[at] = [first, second]

    place = section.astype(jnp.int32).reshape(1)
    frame, gain_part, parts = collect(place, spot, h, a, kept_grads)
    weight_part, gain_sum = sum_terms(parts, gain_part, spot[0])
    gain_sum = lax.dynamic_slice(gain_sum, (0, block * share), (1, share))
    return (frame[None], weight_part[None], gain_sum)


def solution(mesh):
    placed = (
        P("section", None, ("dp", "fsdp"), None),
        P(None, ("dp", "fsdp"), None),
        P("section", None, ("dp", "fsdp"), None),
        P("section", ("dp", "fsdp")),
        P(),
    )
    return jax.shard_map(
        body,
        mesh=mesh,
        in_specs=placed,
        out_specs=(
            P("section", None, ("dp", "fsdp"), None),
            P("section", None, ("dp", "fsdp"), None),
            P("section", ("dp", "fsdp")),
        ),
        check_vma=False,
    )
```

```python
from functools import partial
import math

import jax
import jax.numpy as jnp
from jax import lax
from jax.experimental import pallas as pl
from jax.experimental.pallas import tpu as pltpu
from jax.sharding import PartitionSpec as P

HEAD = 128
BLOCK = 128
WIDTH = 1024
HEADS = WIDTH // HEAD
MICRO = 2
SCALE = 1.0 / math.sqrt(HEAD)
GROUP = ("dp", "fsdp")
EVERY = ("dp", "section", "fsdp")
MIB = 1024 * 1024
HEAD_ROWS = 16


def dot(left, right):
    return lax.dot_general(left, right, (((1,), (0,)), ((), ())), preferred_element_type=jnp.float32)


def dot_nt(left, right):
    return lax.dot_general(left, right, (((1,), (1,)), ((), ())), preferred_element_type=jnp.float32)


def dot_tn(left, right):
    return lax.dot_general(left, right, (((0,), (0,)), ((), ())), preferred_element_type=jnp.float32)


def shift(value, steps):
    count = lax.axis_size(GROUP)
    pairs = [(b, b + steps) for b in range(count) if 0 <= b + steps < count]
    return lax.ppermute(value, GROUP, pairs)


def hop(value, source, target, back):
    sections, rows = lax.axis_size("section"), lax.axis_size("fsdp")
    count = lax.axis_size(GROUP)

    def place(section, block):
        return (block // rows * sections + section) * rows + block % rows

    pairs = [(place(source, b), place(target, b - back)) for b in range(back, count)]
    return lax.ppermute(value, EVERY, pairs)


def group_dims():
    dp, fsdp = lax.axis_size("dp"), lax.axis_size("fsdp")
    planes = 2 if dp % 2 == 0 else 1
    return (planes, dp // planes, fsdp)


def turn(value, axis, steps):
    dims = group_dims()
    pairs = []
    for z in range(dims[0]):
        for y in range(dims[1]):
            for x in range(dims[2]):
                at = [z, y, x]
                to = list(at)
                to[axis] = (at[axis] + steps) % dims[axis]
                index = lambda p: (p[0] * dims[1] + p[1]) * dims[2] + p[2]
                pairs.append((index(at), index(to)))
    return lax.ppermute(value, GROUP, pairs)


def tie_kernel(*refs):
    del refs


def tie(value, *others):
    if not others:
        return value
    anywhere = pl.BlockSpec(memory_space=pl.ANY)
    return pl.pallas_call(
        tie_kernel,
        in_specs=[anywhere] * (1 + len(others)),
        out_specs=anywhere,
        out_shape=jax.ShapeDtypeStruct(value.shape, value.dtype),
        input_output_aliases={0: 0},
        compiler_params=pltpu.CompilerParams(vmem_limit_bytes=MIB),
        name="tie",
    )(value, *others)


def ring(value, axis, head):
    size, half = group_dims()[axis], (value.shape[0] - head) // 2
    both = (head, head + half)
    pieces, heads = [(0, value, both)], [value[:head]]
    if size == 2:
        other = turn(value, axis, 1)
        pieces.append((1, other, both))
        heads.append(other[:head])
    if size == 4:
        behind, ahead = turn(value, axis, 1), turn(value, axis, -1)
        up = turn(behind[: head + half], axis, 1)
        down = turn(ahead[head + half :], axis, -1)
        pieces += [(1, ahead, both), (2, up, (head, None)), (2, down, (None, 0)), (3, behind, both)]
        heads += [ahead[:head], behind[:head], up[:head]]
    return pieces, sum(heads[1:], heads[0])


def arrange_kernel(layouts, dims, *refs):
    spot, refs = refs[0], refs[1:]
    count = sum(len(layout) + (axis == 2) for axis, layout in layouts)
    ins, targets, outs = refs[:count], refs[count : count + 2], refs[count + 2 : count + 4]
    sems, out_sems = refs[count + 4 :]
    copies, offset = [], 0
    for out, (axis, layout) in zip(outs, layouts):
        head, size = int(axis == 2), dims[axis]
        if head:
            copies.append((ins[offset], out.at[pl.ds(0, 1)]))
            offset += 1
        for place, begins in layout:
            for m, begin in enumerate(begins):
                for plane in range(dims[0]):
                    if begin is not None:
                        to = head + (m * dims[0] + plane) * size
                        to += lax.rem(spot[axis] + place, size)
                        source = ins[offset].at[pl.ds(begin + plane, 1)]
                        copies.append((source, out.at[pl.ds(to, 1)]))
            offset += 1
    copies = [
        pltpu.make_async_copy(source, target, sems.at[at])
        for at, (source, target) in enumerate(copies)
    ]
    for copy in copies:
        copy.start()
    for copy in copies:
        copy.wait()
    stores = [
        pltpu.make_async_copy(out, target, out_sems.at[at])
        for at, (out, target) in enumerate(zip(outs, targets))
    ]
    for copy in stores:
        copy.start()
    for copy in stores:
        copy.wait()


def arrange(spot, rings):
    dims = group_dims()
    operands, layouts, shapes = [], [], []
    for axis, head, pieces in rings:
        operands += ([] if head is None else [head]) + [piece for _, piece, _ in pieces]
        layouts.append((axis, [(place, begins) for place, _, begins in pieces]))
        units = (head is not None) + 2 * dims[0] * dims[axis]
        shapes.append((units,) + pieces[0][1].shape[1:])
    return pl.pallas_call(
        partial(arrange_kernel, layouts, dims),
        in_specs=[pl.BlockSpec(memory_space=pltpu.SMEM)]
        + [pl.BlockSpec(memory_space=pl.ANY)] * len(operands),
        out_specs=[pl.BlockSpec(memory_space=pl.ANY)] * 2,
        out_shape=[jax.ShapeDtypeStruct(shape, jnp.bfloat16) for shape in shapes],
        scratch_shapes=[pltpu.VMEM(shape, jnp.bfloat16) for shape in shapes]
        + [
            pltpu.SemaphoreType.DMA((sum(shape[0] for shape in shapes),)),
            pltpu.SemaphoreType.DMA((2,)),
        ],
        compiler_params=pltpu.CompilerParams(vmem_limit_bytes=16 * MIB),
        name="arrange",
    )(spot, *operands)


def gather_weights(shard, gain, spot):
    value = jnp.concatenate([gain, shard])
    gains, planes = gain, [value]
    if group_dims()[0] == 2:
        other = turn(value, 0, 1)
        gains = gain + other[:1]
        planes = [jnp.where(spot[0] == 0, value, other), jnp.where(spot[0] == 0, other, value)]
    rows = [plane[1 + m : 2 + m] for m in range(4) for plane in planes]
    half = len(rows) // 2
    first, gains = ring(jnp.concatenate([gains] + rows[:half]), 2, 1)
    second, _ = ring(jnp.concatenate(rows[half:]), 1, 0)
    first, second = arrange(spot, [(2, gains, first), (1, None, second)])
    first, gains = ring(first, 1, 1)
    second, _ = ring(second, 2, 0)
    return [first, second], gains


def normed(x, gain):
    as_float = x.astype(jnp.float32)
    rscale = lax.rsqrt(jnp.mean(as_float * as_float, axis=-1, keepdims=True) + 1e-06)
    return (as_float * rscale * gain).astype(jnp.bfloat16)


def forward_kernel(layout, dims, *refs):
    count = sum(len(pieces) for pieces in layout)
    spot, pieces, refs = refs[0], refs[1 : 1 + count], refs[1 + count :]
    l2, l1, own, r1, r2, gain, seg_col, seg_row = refs[:8]
    w_out, h_out, q_out, k_out, v_out, p_out, pt_out, o_out, a_out = refs[8:17]
    w, h5, q3, k5, v5, barred, sems = refs[17:]
    step = pl.program_id(0)
    planes, size_y, size_x = dims

    def loads(pair):
        copies, offset = [], sum(len(pieces) for pieces in layout[:pair])
        axis, units = (1, size_x) if pair == 0 else (2, size_y)
        for at, (place, begins) in enumerate(layout[pair]):
            to = lax.rem(spot[axis] + place, dims[axis])
            for m, begin in enumerate(begins):
                for plane in range(planes):
                    if begin is not None:
                        target = w.at[2 * pair + m, plane]
                        target = target.at[to] if pair == 0 else target.at[:, to]
                        source = pieces[offset + at].at[pl.ds(begin + plane * units, units)]
                        copies.append(
                            pltpu.make_async_copy(source, target, sems.at[pair, len(copies)])
                        )
        return copies

    def projection(m, cols):
        return w[m, :, :, :, :, cols].reshape(WIDTH, 256)

    def store(pair):
        half = pl.ds(2 * pair, 2)
        return pltpu.make_async_copy(w.at[half], w_out.at[half], sems.at[2, pair])

    @pl.when(step == 0)
    def _():
        for copy in loads(0) + loads(1):
            copy.start()

    gain_row = gain[0:1, :]
    for at, part in enumerate((l2, l1, own, r1, r2)):
        h5[at * BLOCK : (at + 1) * BLOCK, :] = normed(part[0], gain_row)
    h_out[0] = h5[2 * BLOCK : 3 * BLOCK, :]

    @pl.when(step == 0)
    def _():
        for copy in loads(0):
            copy.wait()
        store(0).start()

    for n in range(0, WIDTH, 256):
        cols = slice(n, n + 256)
        q3[:, cols] = dot(h5[2 * BLOCK :, :], projection(0, cols)).astype(jnp.bfloat16)
        k5[:, cols] = dot(h5[...], projection(1, cols)).astype(jnp.bfloat16)

    @pl.when(step == 0)
    def _():
        for copy in loads(1):
            copy.wait()
        store(1).start()

    for n in range(0, WIDTH, 256):
        cols = slice(n, n + 256)
        v5[:, cols] = dot(h5[...], projection(2, cols)).astype(jnp.bfloat16)
    q_out[0] = q3[...]
    k_out[0] = k5[: 3 * BLOCK, :]
    v_out[0] = v5[: 3 * BLOCK, :]
    for j in range(3):
        allowed = (
            seg_col[0, (j + 2) * BLOCK : (j + 3) * BLOCK, 0:1]
            == seg_row[0, 0:1, j * BLOCK : (j + 3) * BLOCK]
        )
        barred[j * BLOCK : (j + 1) * BLOCK, :] = jnp.where(allowed, 0.0, -1e30)
    for head in range(HEADS):
        cols = slice(head * HEAD, (head + 1) * HEAD)
        for j in range(3):
            rows = slice(j * BLOCK, (j + 1) * BLOCK)
            keys = slice(j * BLOCK, (j + 3) * BLOCK)
            score = dot_nt(q3[rows, cols], k5[keys, cols]) + barred[rows, :]
            top = jnp.max(score, axis=-1, keepdims=True)
            expo = jnp.exp((score - top) * SCALE)
            p = expo * (1.0 / jnp.sum(expo, axis=-1, keepdims=True))
            high = p.astype(jnp.bfloat16)
            low = (p - high.astype(jnp.float32)).astype(jnp.bfloat16)
            both = dot(jnp.concatenate([high, low]), v5[keys, cols])
            mixed = both[:BLOCK]
            o_out[0, rows, cols] = mixed + both[BLOCK:]
            if j == 0:
                p_out[0, head] = p
                a_out[0, :, cols] = mixed.astype(jnp.bfloat16)
            own_keys = slice((2 - j) * BLOCK, (3 - j) * BLOCK)
            pt_out[0, head, :, rows] = p[:, own_keys].T

    @pl.when(step == MICRO - 1)
    def _():
        store(0).wait()
        store(1).wait()


def forward(spot, pairs, parts, gain, seg_col, seg_row):
    anywhere = pl.BlockSpec(memory_space=pl.ANY)
    pieces = [piece for pair in pairs for _, piece, _ in pair]
    layout = [[(place, begins) for place, _, begins in pair] for pair in pairs]
    dims = group_dims()
    wide = (4, *dims, WIDTH // (dims[0] * dims[1] * dims[2]), WIDTH)

    def per_micro(shape):
        return pl.BlockSpec((1,) + shape, lambda m: (m,) + (0,) * len(shape))

    def whole(shape):
        return pl.BlockSpec(shape, lambda m: (0,) * len(shape), pipeline_mode=pl.Buffered(1))

    outs = [
        ((BLOCK, WIDTH), jnp.bfloat16),
        ((3 * BLOCK, WIDTH), jnp.bfloat16),
        ((3 * BLOCK, WIDTH), jnp.bfloat16),
        ((3 * BLOCK, WIDTH), jnp.bfloat16),
        ((HEADS, BLOCK, 3 * BLOCK), jnp.float32),
        ((HEADS, BLOCK, 3 * BLOCK), jnp.float32),
        ((3 * BLOCK, WIDTH), jnp.float32),
        ((BLOCK, WIDTH), jnp.bfloat16),
    ]
    return pl.pallas_call(
        partial(forward_kernel, layout, dims),
        grid=(MICRO,),
        in_specs=[pl.BlockSpec(memory_space=pltpu.SMEM)]
        + [anywhere] * len(pieces)
        + [per_micro((BLOCK, WIDTH))] * 5
        + [
            whole((8, WIDTH)),
            per_micro((5 * BLOCK, 1)),
            per_micro((1, 5 * BLOCK)),
        ],
        out_specs=[anywhere] + [per_micro(shape) for shape, _ in outs],
        out_shape=[jax.ShapeDtypeStruct(wide, jnp.bfloat16)]
        + [jax.ShapeDtypeStruct((MICRO,) + shape, kind) for shape, kind in outs],
        scratch_shapes=[
            pltpu.VMEM(wide, jnp.bfloat16),
            pltpu.VMEM((5 * BLOCK, WIDTH), jnp.bfloat16),
            pltpu.VMEM((3 * BLOCK, WIDTH), jnp.bfloat16),
            pltpu.VMEM((5 * BLOCK, WIDTH), jnp.bfloat16),
            pltpu.VMEM((5 * BLOCK, WIDTH), jnp.bfloat16),
            pltpu.VMEM((3 * BLOCK, 3 * BLOCK), jnp.float32),
            pltpu.SemaphoreType.DMA((3, 16)),
        ],
        compiler_params=pltpu.CompilerParams(vmem_limit_bytes=44 * MIB),
        cost_estimate=pl.CostEstimate(
            flops=2 * 2 * 15 * BLOCK * WIDTH * WIDTH, bytes_accessed=28 << 20, transcendentals=0
        ),
        name="forward",
    )(spot, *pieces, *parts, gain, seg_col, seg_row)


def backward_kernel(micro, *refs):
    flag, g0, g1, g2, w, q_in, k_in, v_in, p_in, pt_in, o_in, x_in, gain_in = refs[:13]
    refs = refs[13:]
    frame_out, g_out, dq_out, dk_out, dv_out, gain_out = refs[:6]
    g, wv, q, k, v, p, pt, o, x, gain, da, dq, dk, dv, dh, frame, gain_sum, sems = refs[6:]

    @pl.when(flag[0] == 1)
    def _():
        def move(at, source, target):
            copy = pltpu.make_async_copy(source, target, sems.at[at])
            copy.start()
            return copy

        load_g = [
            move(at, part, g.at[pl.ds(at * BLOCK, BLOCK), :]) for at, part in enumerate((g0, g1, g2))
        ]
        load_wo = move(3, w.at[3], wv.at[3])
        load_o = move(4, o_in.at[micro], o)
        load_v = move(5, v_in.at[micro], v)
        load_p = move(6, p_in.at[micro], p)
        load_k = move(7, k_in.at[micro], k)
        load_pt = move(8, pt_in.at[micro], pt)
        load_q = move(9, q_in.at[micro], q)
        load_w = move(10, w.at[pl.ds(0, 3)], wv.at[pl.ds(0, 3)])
        load_x = move(11, x_in.at[micro], x)
        load_gain = move(12, gain_in, gain)
        for copy in load_g:
            copy.wait()
        load_wo.wait()
        store_g = move(13, g.at[pl.ds(0, BLOCK), :], g_out)
        for n in range(0, WIDTH, 256):
            cols = slice(n, n + 256)
            da[:, cols] = dot_nt(g[...], wv[3, cols, :]).astype(jnp.bfloat16)
        for copy in (load_o, load_v, load_p, load_k, load_pt, load_q):
            copy.wait()
        for head in range(HEADS):
            cols = slice(head * HEAD, (head + 1) * HEAD)
            da_h = da[:, cols]
            inner = jnp.sum(da_h.astype(jnp.float32) * o[:, cols], axis=-1, keepdims=True)
            dp = dot_nt(da_h[:BLOCK], v[:, cols])
            ds = (p[head] * (dp - inner[:BLOCK]) * SCALE).astype(jnp.bfloat16)
            dq[:, cols] = dot(ds, k[:, cols]).astype(jnp.bfloat16)
            inner_row = jnp.broadcast_to(inner, (3 * BLOCK, HEAD)).T
            p_t = pt[head]
            dp_t = dot_nt(v[2 * BLOCK :, cols], da_h)
            ds_t = (p_t * (dp_t - inner_row) * SCALE).astype(jnp.bfloat16)
            dk[:, cols] = dot(ds_t, q[:, cols]).astype(jnp.bfloat16)
            dv[:, cols] = dot(p_t.astype(jnp.bfloat16), da_h).astype(jnp.bfloat16)
        stores = [
            store_g,
            move(14, dq, dq_out),
            move(15, dk, dk_out),
            move(16, dv, dv_out),
        ]
        load_w.wait()
        for n in range(0, WIDTH, 256):
            cols = slice(n, n + 256)
            dh[:, cols] = (
                dot_nt(dq[...], wv[0, cols, :])
                + dot_nt(dk[...], wv[1, cols, :])
                + dot_nt(dv[...], wv[2, cols, :])
            )
        load_x.wait()
        load_gain.wait()
        as_float = x[...].astype(jnp.float32)
        rscale = lax.rsqrt(jnp.mean(as_float * as_float, axis=-1, keepdims=True) + 1e-06)
        d_normed = dh[...]
        scaled = gain[0:1, :] * d_normed
        cubic = rscale * rscale * rscale
        frame_f = (
            g[:BLOCK, :].astype(jnp.float32)
            + rscale * scaled
            - as_float * (cubic * jnp.mean(scaled * as_float, axis=-1, keepdims=True))
        )
        frame[...] = frame_f.astype(jnp.bfloat16)
        stores.append(move(17, frame, frame_out))
        term = jnp.sum(d_normed * as_float * rscale, axis=0, keepdims=True)
        gain_sum[...] = jnp.broadcast_to(term, (8, WIDTH))
        stores.append(move(18, gain_sum, gain_out))
        for copy in stores:
            copy.wait()


def in_place(value):
    return pltpu.with_memory_space_constraint(value, pltpu.HBM)


def backward(micro, flag, incoming, w, kept, x, gain):
    block = pltpu.HBM((BLOCK, WIDTH), jnp.bfloat16)
    outs = [block] * 5 + [pltpu.HBM((8, WIDTH), jnp.float32)]
    operands = [flag, *incoming] + [in_place(value) for value in (w, *kept, x, gain)]
    anywhere = pl.BlockSpec(memory_space=pl.ANY)
    in_hbm = pl.BlockSpec(memory_space=pltpu.HBM)
    bf16, f32 = jnp.bfloat16, jnp.float32
    scratch = [
        ((3 * BLOCK, WIDTH), bf16),
        ((4, WIDTH, WIDTH), bf16),
        ((3 * BLOCK, WIDTH), bf16),
        ((3 * BLOCK, WIDTH), bf16),
        ((3 * BLOCK, WIDTH), bf16),
        ((HEADS, BLOCK, 3 * BLOCK), f32),
        ((HEADS, BLOCK, 3 * BLOCK), f32),
        ((3 * BLOCK, WIDTH), f32),
        ((BLOCK, WIDTH), bf16),
        ((8, WIDTH), f32),
        ((3 * BLOCK, WIDTH), bf16),
        ((BLOCK, WIDTH), bf16),
        ((BLOCK, WIDTH), bf16),
        ((BLOCK, WIDTH), bf16),
        ((BLOCK, WIDTH), f32),
        ((BLOCK, WIDTH), bf16),
        ((8, WIDTH), f32),
    ]
    return pl.pallas_call(
        partial(backward_kernel, micro),
        in_specs=[pl.BlockSpec(memory_space=pltpu.SMEM)] + [anywhere] * (len(operands) - 1),
        out_specs=[in_hbm] * 6,
        out_shape=outs,
        scratch_shapes=[pltpu.VMEM(shape, kind) for shape, kind in scratch]
        + [pltpu.SemaphoreType.DMA((19,))],
        compiler_params=pltpu.CompilerParams(vmem_limit_bytes=48 * MIB),
        cost_estimate=pl.CostEstimate(
            flops=2 * 7 * BLOCK * WIDTH * WIDTH, bytes_accessed=16 << 20, transcendentals=0
        ),
        name="backward",
    )(*operands)


def ring_slots(size):
    if size == 4:
        return (2, 2, 2, 1, 1), {
            (0, 0): (0, 0), (1, 0): (0, 1),
            (0, 1): (3, 0), (1, 1): (1, 1),
            (0, 2): (1, 0), (1, 2): (2, 1),
            (0, 3): (2, 0), (1, 3): (4, 0),
        }
    return (2,) * size, {(m, f): (f, m) for m in range(2) for f in range(size)}


def ring_heads(size):
    return (1, 2) if size == 4 else (1,) * (size == 2)


def add(*values):
    return sum(value.astype(jnp.float32) for value in values)


def ring_sum(parts, axis, gain):
    size, head = group_dims()[axis], 0 if gain is None else HEAD_ROWS
    rows = parts[0].shape[0] // 2
    if size == 4:
        keep, up, down, late_up, late_down = parts
        up, down = turn(up, axis, 1), turn(down, axis, -1)
        late_up = add(late_up, up[head : head + rows]).astype(jnp.bfloat16)
        late_down = add(late_down, down[head + rows :]).astype(jnp.bfloat16)
        if head:
            late_up = jnp.concatenate([up[:head], late_up])
        late_up, late_down = turn(late_up, axis, 1), turn(late_down, axis, -1)
        total = [
            add(keep[:rows], late_up[head:], down[head : head + rows]),
            add(keep[rows:], up[head + rows :], late_down),
        ]
        if head:
            gain = add(gain, up[:head], down[:head], late_up[:head])
        return jnp.stack(total), gain
    if size == 2:
        other = turn(parts[1], axis, 1)
        if head:
            gain = add(gain, other[:head])
        return add(parts[0], other[head:]).reshape(2, rows, WIDTH), gain
    return parts[0].astype(jnp.float32).reshape(2, rows, WIDTH), gain


def collect_kernel(sections, dims, counts, *refs):
    place, spot, h_in, a_in = refs[:4]
    kept = refs[4 : 4 + 12 * sections]
    refs = refs[4 + 12 * sections :]
    frame_out, gain_out, outs = refs[0], refs[1], refs[2 : 2 + sum(counts)]
    left, right, term, frame, gain, gain_head, sems, out_sems = refs[2 + sum(counts) :]
    planes, size_y, size_x = dims
    share = WIDTH // (planes * size_y * size_x)
    own_y, own_x = spot[1], spot[2]
    names = ("frame", "g", "dq", "dk", "dv", "gain")

    def copies(at):
        found = []
        for micro in range(MICRO):
            results = dict(zip(names, kept[(at * MICRO + micro) * 6 : (at * MICRO + micro + 1) * 6]))
            rows = pl.ds(micro * BLOCK, BLOCK)
            pairs = [(results[name], right.at[n, rows]) for n, name in enumerate(("dq", "dk", "dv", "g"))]
            pairs += [(results["frame"], frame.at[micro]), (results["gain"], gain.at[micro])]
            pairs += [(h_in.at[micro], left.at[0, rows]), (a_in.at[micro], left.at[1, rows])]
            found += [
                pltpu.make_async_copy(source, target, sems.at[micro, n])
                for n, (source, target) in enumerate(pairs)
            ]
        return found

    for at in range(sections):

        @pl.when(place[0] == at)
        def _(at=at):
            started = copies(at)
            for copy in started:
                copy.start()
            for copy in started:
                copy.wait()

    frame_copy = pltpu.make_async_copy(frame, frame_out, out_sems.at[4, 0])
    frame_copy.start()
    gain_term = (gain[0, 0:1, :] + gain[1, 0:1, :]).astype(jnp.bfloat16)
    gain_head[...] = jnp.broadcast_to(gain_term, (HEAD_ROWS, WIDTH))
    started = [frame_copy]
    heads = [gain_out] + [outs[at].at[pl.ds(0, HEAD_ROWS), :] for at in ring_heads(size_x)]
    for at, target in enumerate(heads):
        copy = pltpu.make_async_copy(gain_head, target, out_sems.at[4, 1 + at])
        copy.start()
        started.append(copy)
    for m in range(4):
        pair = m // 2
        first_size, second_size = (size_x, size_y) if pair == 0 else (size_y, size_x)
        _, slots = ring_slots(first_size)
        arrays = outs[: counts[0]] if pair == 0 else outs[counts[0] :]
        factor = left[1 if m == 3 else 0]
        for n in range(0, WIDTH, 256):
            cols = slice(n, n + 256)
            term[m, :, cols] = dot_tn(factor, right[m, :, cols]).astype(jnp.bfloat16)
        number = 0
        for f in range(first_size):
            array, row = slots[m % 2, f]
            for r in range(second_size):
                ahead_x, ahead_y = (f, r) if pair == 0 else (r, f)
                column = lax.rem(own_y + ahead_y, size_y) * size_x + lax.rem(own_x + ahead_x, size_x)
                for plane in range(planes):
                    at = (plane * size_y * size_x + column) * share
                    to = ((row * second_size + r) * planes + plane) * share
                    if pair == 0 and array in ring_heads(first_size):
                        to += HEAD_ROWS
                    copy = pltpu.make_async_copy(
                        term.at[m, pl.ds(pl.multiple_of(at, share), share), :],
                        arrays[array].at[pl.ds(to, share), :],
                        out_sems.at[m, number],
                    )
                    copy.start()
                    started.append(copy)
                    number += 1
    for copy in started:
        copy.wait()


def collect(section, spot, h, a, kept):
    dims, sections = group_dims(), len(kept)
    planes, size_y, size_x = dims
    total = planes * size_y * size_x
    share = WIDTH // total
    anywhere = pl.BlockSpec(memory_space=pl.ANY)
    in_hbm = pl.BlockSpec(memory_space=pltpu.HBM)
    smem = pl.BlockSpec(memory_space=pltpu.SMEM)
    shapes, counts = [], []
    for first_size, second_size in ((size_x, size_y), (size_y, size_x)):
        rows, _ = ring_slots(first_size)
        counts.append(len(rows))
        for at, n in enumerate(rows):
            n = n * second_size * planes * share
            if len(counts) == 1 and at in ring_heads(first_size):
                n += HEAD_ROWS
            shapes.append(jax.ShapeDtypeStruct((n, WIDTH), jnp.bfloat16))
    operands = [in_place(result) for both in kept for results in both for result in results]
    outs = pl.pallas_call(
        partial(collect_kernel, sections, dims, counts),
        in_specs=[smem, smem] + [anywhere] * (2 + len(operands)),
        out_specs=[in_hbm] * (2 + len(shapes)),
        out_shape=[
            jax.ShapeDtypeStruct((MICRO, BLOCK, WIDTH), jnp.bfloat16),
            jax.ShapeDtypeStruct((HEAD_ROWS, WIDTH), jnp.bfloat16),
        ]
        + shapes,
        scratch_shapes=[
            pltpu.VMEM((2, MICRO * BLOCK, WIDTH), jnp.bfloat16),
            pltpu.VMEM((4, MICRO * BLOCK, WIDTH), jnp.bfloat16),
            pltpu.VMEM((4, WIDTH, WIDTH), jnp.bfloat16),
            pltpu.VMEM((MICRO, BLOCK, WIDTH), jnp.bfloat16),
            pltpu.VMEM((MICRO, 8, WIDTH), jnp.float32),
            pltpu.VMEM((HEAD_ROWS, WIDTH), jnp.bfloat16),
            pltpu.SemaphoreType.DMA((MICRO, 8)),
            pltpu.SemaphoreType.DMA((5, max(total, 4))),
        ],
        compiler_params=pltpu.CompilerParams(vmem_limit_bytes=48 * MIB),
        cost_estimate=pl.CostEstimate(
            flops=2 * 8 * BLOCK * WIDTH * WIDTH, bytes_accessed=14 << 20, transcendentals=0
        ),
        name="collect",
    )(section, spot, h, a, *operands)
    frame, gain = outs[:2]
    return frame, gain, [outs[2 : 2 + counts[0]], outs[2 + counts[0] :]]


def sum_terms(parts, gain, plane):
    dims, totals = group_dims(), []
    for pair, (first, second) in zip(parts, ((2, 1), (1, 2))):
        own = gain if first == 2 else None
        value, own = ring_sum(pair, first, own)
        value = value.astype(jnp.bfloat16).reshape(2, dims[second], -1, WIDTH)
        rows, slots = ring_slots(dims[second])
        arrays = [[None] * n for n in rows]
        for (m, f), (array, row) in slots.items():
            arrays[array][row] = value[m, f]
        if own is not None:
            own = own.astype(jnp.bfloat16)
            for array in ring_heads(dims[second]):
                arrays[array].insert(0, own)
        value, own = ring_sum([jnp.concatenate(array) for array in arrays], second, own)
        totals.append(value)
        gain = gain if own is None else own
    value = jnp.concatenate(totals)
    if dims[0] == 1:
        return value, gain
    share = value.shape[1] // 2
    value = value.reshape(4, 2, share, WIDTH)
    other = lax.dynamic_index_in_dim(value, 1 - plane, 1, keepdims=False).astype(jnp.bfloat16)
    own = lax.dynamic_index_in_dim(value, plane, 1, keepdims=False)
    other = jnp.concatenate([gain.astype(jnp.bfloat16), other.reshape(4 * share, WIDTH)])
    other = turn(other, 0, 1)
    return add(own, other[HEAD_ROWS:].reshape(own.shape)), add(gain, other[:HEAD_ROWS])


def segments(lengths, block):
    bounds = jnp.cumsum(lengths, axis=1)
    total = lax.axis_size(GROUP) * BLOCK
    places = (block - 2) * BLOCK + jnp.arange(5 * BLOCK, dtype=jnp.int32)
    counted = jnp.sum((places[None, :, None] >= bounds[:, None, :]).astype(jnp.int32), axis=2)
    return jnp.where(places < 0, -1, jnp.where(places >= total, -2, counted))


def body(checkpoints, cotangent, weights, gains, lengths):
    sections, section = lax.axis_size("section"), lax.axis_index("section")
    block = lax.axis_index(GROUP)
    share = gains.shape[1]

    planes, size_y, _ = group_dims()
    dp = lax.axis_index("dp")
    spot = jnp.stack([dp // size_y, dp % size_y, lax.axis_index("fsdp")]).astype(jnp.int32)
    spread = lax.dynamic_update_slice(
        jnp.zeros((1, share, WIDTH), jnp.bfloat16), gains[None], (0, 0, block * share)
    )
    pairs, gain = gather_weights(weights[0], spread, spot)
    gain = jnp.broadcast_to(gain[0, 0:1].astype(jnp.float32), (8, WIDTH))

    x = checkpoints[0]
    left, right = shift(x, 1), shift(x, -1)
    parts = (shift(left, 1), left, x, right, shift(right, -1))
    source = max(sections - 3, 0)
    cot = (cotangent, hop(cotangent, source, sections - 1, 1), hop(cotangent, source, sections - 1, 2))

    segs = segments(lengths, block)
    gathered, h, q, k, v, p, pt, o, a = forward(
        spot, pairs, parts, gain, segs[:, :, None], segs[:, None, :]
    )
    gathered = gathered.reshape(4, WIDTH, WIDTH)
    kept = (q, k, v, p, pt, o)

    kept_grads = [[None] * MICRO for _ in range(sections)]
    arriving, behind = ([part[micro] for part in cot] for micro in range(MICRO))
    for at in range(sections - 1, -1, -1):
        flag = (section == at).astype(jnp.int32).reshape(1)
        first = list(backward(0, flag, arriving, gathered, kept, x, gain))
        leaving = first[0]
        if at > 0:
            arriving = [hop(leaving, at, at - 1, back) for back in (2, 1, 0)][::-1]
        if at < sections - 1:
            second[0] = tie(second[0], arriving[0] if at > 0 else leaving)
            behind = [hop(second[0], at + 1, at, back) for back in (2, 1, 0)][::-1]
        second = list(backward(1, flag, behind, gathered, kept, x, gain))
        kept_grads[at] = [first, second]

    place = section.astype(jnp.int32).reshape(1)
    frame, gain_part, parts = collect(place, spot, h, a, kept_grads)
    weight_part, gain_sum = sum_terms(parts, gain_part, spot[0])
    gain_sum = lax.dynamic_slice(gain_sum, (0, block * share), (1, share))
    return (frame[None], weight_part[None], gain_sum)


def solution(mesh):
    placed = (
        P("section", None, ("dp", "fsdp"), None),
        P(None, ("dp", "fsdp"), None),
        P("section", None, ("dp", "fsdp"), None),
        P("section", ("dp", "fsdp")),
        P(),
    )
    return jax.shard_map(
        body,
        mesh=mesh,
        in_specs=placed,
        out_specs=(
            P("section", None, ("dp", "fsdp"), None),
            P("section", None, ("dp", "fsdp"), None),
            P("section", ("dp", "fsdp")),
        ),
        check_vma=False,
    )
```

```python
from functools import partial
import math

import jax
import jax.numpy as jnp
from jax import lax
from jax.experimental import pallas as pl
from jax.experimental.pallas import tpu as pltpu
from jax.sharding import PartitionSpec as P

HEAD = 128
BLOCK = 128
WIDTH = 1024
HEADS = WIDTH // HEAD
MICRO = 2
SCALE = 1.0 / math.sqrt(HEAD)
GROUP = ("dp", "fsdp")
EVERY = ("dp", "section", "fsdp")
MIB = 1024 * 1024
HEAD_ROWS = 16


def dot(left, right):
    return lax.dot_general(left, right, (((1,), (0,)), ((), ())), preferred_element_type=jnp.float32)


def dot_nt(left, right):
    return lax.dot_general(left, right, (((1,), (1,)), ((), ())), preferred_element_type=jnp.float32)


def dot_tn(left, right):
    return lax.dot_general(left, right, (((0,), (0,)), ((), ())), preferred_element_type=jnp.float32)


def shift(value, steps):
    count = lax.axis_size(GROUP)
    pairs = [(b, b + steps) for b in range(count) if 0 <= b + steps < count]
    return lax.ppermute(value, GROUP, pairs)


def hop(value, source, target, back):
    sections, rows = lax.axis_size("section"), lax.axis_size("fsdp")
    count = lax.axis_size(GROUP)

    def place(section, block):
        return (block // rows * sections + section) * rows + block % rows

    pairs = [(place(source, b), place(target, b - back)) for b in range(back, count)]
    return lax.ppermute(value, EVERY, pairs)


def group_dims():
    dp, fsdp = lax.axis_size("dp"), lax.axis_size("fsdp")
    planes = 2 if dp % 2 == 0 else 1
    return (planes, dp // planes, fsdp)


def turn(value, axis, steps):
    dims = group_dims()
    pairs = []
    for z in range(dims[0]):
        for y in range(dims[1]):
            for x in range(dims[2]):
                at = [z, y, x]
                to = list(at)
                to[axis] = (at[axis] + steps) % dims[axis]
                index = lambda p: (p[0] * dims[1] + p[1]) * dims[2] + p[2]
                pairs.append((index(at), index(to)))
    return lax.ppermute(value, GROUP, pairs)


def tie_kernel(*refs):
    del refs


def tie(value, *others):
    if not others:
        return value
    anywhere = pl.BlockSpec(memory_space=pl.ANY)
    return pl.pallas_call(
        tie_kernel,
        in_specs=[anywhere] * (1 + len(others)),
        out_specs=anywhere,
        out_shape=jax.ShapeDtypeStruct(value.shape, value.dtype),
        input_output_aliases={0: 0},
        compiler_params=pltpu.CompilerParams(vmem_limit_bytes=MIB),
        name="tie",
    )(value, *others)


def tie_all(values):
    anywhere = pl.BlockSpec(memory_space=pl.ANY)
    return pl.pallas_call(
        tie_kernel,
        in_specs=[anywhere] * len(values),
        out_specs=[anywhere] * len(values),
        out_shape=[jax.ShapeDtypeStruct(value.shape, value.dtype) for value in values],
        input_output_aliases={at: at for at in range(len(values))},
        compiler_params=pltpu.CompilerParams(vmem_limit_bytes=MIB),
        name="tie",
    )(*values)


def ring(value, axis, head):
    size, half = group_dims()[axis], (value.shape[0] - head) // 2
    both = (head, head + half)
    pieces, heads = [(0, value, both)], [value[:head]]
    if size == 2:
        other = turn(value, axis, 1)
        pieces.append((1, other, both))
        heads.append(other[:head])
    if size == 4:
        behind, ahead = turn(value, axis, 1), turn(value, axis, -1)
        up = turn(behind[: head + half], axis, 1)
        down = turn(ahead[head + half :], axis, -1)
        pieces += [(1, ahead, both), (2, up, (head, None)), (2, down, (None, 0)), (3, behind, both)]
        heads += [ahead[:head], behind[:head], up[:head]]
    return pieces, sum(heads[1:], heads[0])


def arrange_kernel(layouts, dims, *refs):
    spot, refs = refs[0], refs[1:]
    count = sum(len(layout) + (axis == 2) for axis, layout in layouts)
    ins, targets, outs = refs[:count], refs[count : count + 2], refs[count + 2 : count + 4]
    sems, out_sems = refs[count + 4 :]
    copies, offset = [], 0
    for out, (axis, layout) in zip(outs, layouts):
        head, size = int(axis == 2), dims[axis]
        if head:
            copies.append((ins[offset], out.at[pl.ds(0, 1)]))
            offset += 1
        for place, begins in layout:
            for m, begin in enumerate(begins):
                for plane in range(dims[0]):
                    if begin is not None:
                        to = head + (m * dims[0] + plane) * size
                        to += lax.rem(spot[axis] + place, size)
                        source = ins[offset].at[pl.ds(begin + plane, 1)]
                        copies.append((source, out.at[pl.ds(to, 1)]))
            offset += 1
    copies = [
        pltpu.make_async_copy(source, target, sems.at[at])
        for at, (source, target) in enumerate(copies)
    ]
    for copy in copies:
        copy.start()
    for copy in copies:
        copy.wait()
    stores = [
        pltpu.make_async_copy(out, target, out_sems.at[at])
        for at, (out, target) in enumerate(zip(outs, targets))
    ]
    for copy in stores:
        copy.start()
    for copy in stores:
        copy.wait()


def arrange(spot, rings):
    dims = group_dims()
    operands, layouts, shapes = [], [], []
    for axis, head, pieces in rings:
        operands += ([] if head is None else [head]) + [piece for _, piece, _ in pieces]
        layouts.append((axis, [(place, begins) for place, _, begins in pieces]))
        units = (head is not None) + 2 * dims[0] * dims[axis]
        shapes.append((units,) + pieces[0][1].shape[1:])
    return pl.pallas_call(
        partial(arrange_kernel, layouts, dims),
        in_specs=[pl.BlockSpec(memory_space=pltpu.SMEM)]
        + [pl.BlockSpec(memory_space=pl.ANY)] * len(operands),
        out_specs=[pl.BlockSpec(memory_space=pl.ANY)] * 2,
        out_shape=[jax.ShapeDtypeStruct(shape, jnp.bfloat16) for shape in shapes],
        scratch_shapes=[pltpu.VMEM(shape, jnp.bfloat16) for shape in shapes]
        + [
            pltpu.SemaphoreType.DMA((sum(shape[0] for shape in shapes),)),
            pltpu.SemaphoreType.DMA((2,)),
        ],
        compiler_params=pltpu.CompilerParams(vmem_limit_bytes=16 * MIB),
        name="arrange",
    )(spot, *operands)


def gather_weights(shard, gain, spot):
    value = jnp.concatenate([gain, shard])
    gains, planes = gain, [value]
    if group_dims()[0] == 2:
        other = turn(value, 0, 1)
        gains = gain + other[:1]
        planes = [jnp.where(spot[0] == 0, value, other), jnp.where(spot[0] == 0, other, value)]
    rows = [plane[1 + m : 2 + m] for m in range(4) for plane in planes]
    half = len(rows) // 2
    first, gains = ring(jnp.concatenate([gains] + rows[:half]), 2, 1)
    second, _ = ring(jnp.concatenate(rows[half:]), 1, 0)
    first, second = arrange(spot, [(2, gains, first), (1, None, second)])
    first, gains = ring(first, 1, 1)
    second, _ = ring(second, 2, 0)
    return [first, second], gains


def normed(x, gain):
    as_float = x.astype(jnp.float32)
    rscale = lax.rsqrt(jnp.mean(as_float * as_float, axis=-1, keepdims=True) + 1e-06)
    return (as_float * rscale * gain).astype(jnp.bfloat16)


def forward_kernel(layout, dims, *refs):
    count = sum(len(pieces) for pieces in layout)
    spot, pieces, refs = refs[0], refs[1 : 1 + count], refs[1 + count :]
    l2, l1, own, r1, r2, gain, seg_col, seg_row = refs[:8]
    w_out, h_out, q_out, k_out, v_out, p_out, pt_out, o_out, a_out = refs[8:17]
    w, h5, q3, k5, v5, barred, sems = refs[17:]
    step = pl.program_id(0)
    planes, size_y, size_x = dims

    def loads(pair):
        copies, offset = [], sum(len(pieces) for pieces in layout[:pair])
        axis, units = (1, size_x) if pair == 0 else (2, size_y)
        for at, (place, begins) in enumerate(layout[pair]):
            to = lax.rem(spot[axis] + place, dims[axis])
            for m, begin in enumerate(begins):
                for plane in range(planes):
                    if begin is not None:
                        target = w.at[2 * pair + m, plane]
                        target = target.at[to] if pair == 0 else target.at[:, to]
                        source = pieces[offset + at].at[pl.ds(begin + plane * units, units)]
                        copies.append(
                            pltpu.make_async_copy(source, target, sems.at[pair, len(copies)])
                        )
        return copies

    def projection(m, cols):
        return w[m, :, :, :, :, cols].reshape(WIDTH, 256)

    def store(pair):
        half = pl.ds(2 * pair, 2)
        return pltpu.make_async_copy(w.at[half], w_out.at[half], sems.at[2, pair])

    @pl.when(step == 0)
    def _():
        for copy in loads(0) + loads(1):
            copy.start()

    gain_row = gain[0:1, :]
    for at, part in enumerate((l2, l1, own, r1, r2)):
        h5[at * BLOCK : (at + 1) * BLOCK, :] = normed(part[0], gain_row)
    h_out[0] = h5[2 * BLOCK : 3 * BLOCK, :]

    @pl.when(step == 0)
    def _():
        for copy in loads(0):
            copy.wait()
        store(0).start()

    for n in range(0, WIDTH, 256):
        cols = slice(n, n + 256)
        q3[:, cols] = dot(h5[2 * BLOCK :, :], projection(0, cols)).astype(jnp.bfloat16)
        k5[:, cols] = dot(h5[...], projection(1, cols)).astype(jnp.bfloat16)

    @pl.when(step == 0)
    def _():
        for copy in loads(1):
            copy.wait()
        store(1).start()

    for n in range(0, WIDTH, 256):
        cols = slice(n, n + 256)
        v5[:, cols] = dot(h5[...], projection(2, cols)).astype(jnp.bfloat16)
    q_out[0] = q3[...]
    k_out[0] = k5[: 3 * BLOCK, :]
    v_out[0] = v5[: 3 * BLOCK, :]
    for j in range(3):
        allowed = (
            seg_col[0, (j + 2) * BLOCK : (j + 3) * BLOCK, 0:1]
            == seg_row[0, 0:1, j * BLOCK : (j + 3) * BLOCK]
        )
        barred[j * BLOCK : (j + 1) * BLOCK, :] = jnp.where(allowed, 0.0, -1e30)
    for head in range(HEADS):
        cols = slice(head * HEAD, (head + 1) * HEAD)
        for j in range(3):
            rows = slice(j * BLOCK, (j + 1) * BLOCK)
            keys = slice(j * BLOCK, (j + 3) * BLOCK)
            score = dot_nt(q3[rows, cols], k5[keys, cols]) + barred[rows, :]
            top = jnp.max(score, axis=-1, keepdims=True)
            expo = jnp.exp((score - top) * SCALE)
            p = expo * (1.0 / jnp.sum(expo, axis=-1, keepdims=True))
            high = p.astype(jnp.bfloat16)
            low = (p - high.astype(jnp.float32)).astype(jnp.bfloat16)
            both = dot(jnp.concatenate([high, low]), v5[keys, cols])
            mixed = both[:BLOCK]
            o_out[0, rows, cols] = mixed + both[BLOCK:]
            if j == 0:
                p_out[0, head] = p
                a_out[0, :, cols] = mixed.astype(jnp.bfloat16)
            own_keys = slice((2 - j) * BLOCK, (3 - j) * BLOCK)
            pt_out[0, head, :, rows] = p[:, own_keys].T

    @pl.when(step == MICRO - 1)
    def _():
        store(0).wait()
        store(1).wait()


def forward(spot, pairs, parts, gain, seg_col, seg_row):
    anywhere = pl.BlockSpec(memory_space=pl.ANY)
    pieces = [piece for pair in pairs for _, piece, _ in pair]
    layout = [[(place, begins) for place, _, begins in pair] for pair in pairs]
    dims = group_dims()
    wide = (4, *dims, WIDTH // (dims[0] * dims[1] * dims[2]), WIDTH)

    def per_micro(shape):
        return pl.BlockSpec((1,) + shape, lambda m: (m,) + (0,) * len(shape))

    def whole(shape):
        return pl.BlockSpec(shape, lambda m: (0,) * len(shape), pipeline_mode=pl.Buffered(1))

    outs = [
        ((BLOCK, WIDTH), jnp.bfloat16),
        ((3 * BLOCK, WIDTH), jnp.bfloat16),
        ((3 * BLOCK, WIDTH), jnp.bfloat16),
        ((3 * BLOCK, WIDTH), jnp.bfloat16),
        ((HEADS, BLOCK, 3 * BLOCK), jnp.float32),
        ((HEADS, BLOCK, 3 * BLOCK), jnp.float32),
        ((3 * BLOCK, WIDTH), jnp.float32),
        ((BLOCK, WIDTH), jnp.bfloat16),
    ]
    return pl.pallas_call(
        partial(forward_kernel, layout, dims),
        grid=(MICRO,),
        in_specs=[pl.BlockSpec(memory_space=pltpu.SMEM)]
        + [anywhere] * len(pieces)
        + [per_micro((BLOCK, WIDTH))] * 5
        + [
            whole((8, WIDTH)),
            per_micro((5 * BLOCK, 1)),
            per_micro((1, 5 * BLOCK)),
        ],
        out_specs=[anywhere] + [per_micro(shape) for shape, _ in outs],
        out_shape=[jax.ShapeDtypeStruct(wide, jnp.bfloat16)]
        + [jax.ShapeDtypeStruct((MICRO,) + shape, kind) for shape, kind in outs],
        scratch_shapes=[
            pltpu.VMEM(wide, jnp.bfloat16),
            pltpu.VMEM((5 * BLOCK, WIDTH), jnp.bfloat16),
            pltpu.VMEM((3 * BLOCK, WIDTH), jnp.bfloat16),
            pltpu.VMEM((5 * BLOCK, WIDTH), jnp.bfloat16),
            pltpu.VMEM((5 * BLOCK, WIDTH), jnp.bfloat16),
            pltpu.VMEM((3 * BLOCK, 3 * BLOCK), jnp.float32),
            pltpu.SemaphoreType.DMA((3, 16)),
        ],
        compiler_params=pltpu.CompilerParams(vmem_limit_bytes=44 * MIB),
        cost_estimate=pl.CostEstimate(
            flops=2 * 2 * 15 * BLOCK * WIDTH * WIDTH, bytes_accessed=28 << 20, transcendentals=0
        ),
        name="forward",
    )(spot, *pieces, *parts, gain, seg_col, seg_row)


def backward_kernel(micro, *refs):
    flag, g0, g1, g2, w, q_in, k_in, v_in, p_in, pt_in, o_in, x_in, gain_in = refs[:13]
    refs = refs[13:]
    frame_out, g_out, dq_out, dk_out, dv_out, gain_out = refs[:6]
    g, wv, q, k, v, p, pt, o, x, gain, da, dq, dk, dv, dh, frame, gain_sum, sems = refs[6:]

    @pl.when(flag[0] == 1)
    def _():
        def move(at, source, target):
            copy = pltpu.make_async_copy(source, target, sems.at[at])
            copy.start()
            return copy

        load_g = [
            move(at, part, g.at[pl.ds(at * BLOCK, BLOCK), :]) for at, part in enumerate((g0, g1, g2))
        ]
        load_wo = move(3, w.at[3], wv.at[3])
        load_o = move(4, o_in.at[micro], o)
        load_v = move(5, v_in.at[micro], v)
        load_p = move(6, p_in.at[micro], p)
        load_k = move(7, k_in.at[micro], k)
        load_pt = move(8, pt_in.at[micro], pt)
        load_q = move(9, q_in.at[micro], q)
        load_w = move(10, w.at[pl.ds(0, 3)], wv.at[pl.ds(0, 3)])
        load_x = move(11, x_in.at[micro], x)
        load_gain = move(12, gain_in, gain)
        for copy in load_g:
            copy.wait()
        load_wo.wait()
        store_g = move(13, g.at[pl.ds(0, BLOCK), :], g_out)
        for n in range(0, WIDTH, 256):
            cols = slice(n, n + 256)
            da[:, cols] = dot_nt(g[...], wv[3, cols, :]).astype(jnp.bfloat16)
        for copy in (load_o, load_v, load_p, load_k, load_pt, load_q):
            copy.wait()
        for head in range(HEADS):
            cols = slice(head * HEAD, (head + 1) * HEAD)
            da_h = da[:, cols]
            inner = jnp.sum(da_h.astype(jnp.float32) * o[:, cols], axis=-1, keepdims=True)
            dp = dot_nt(da_h[:BLOCK], v[:, cols])
            ds = (p[head] * (dp - inner[:BLOCK]) * SCALE).astype(jnp.bfloat16)
            dq[:, cols] = dot(ds, k[:, cols]).astype(jnp.bfloat16)
            inner_row = jnp.broadcast_to(inner, (3 * BLOCK, HEAD)).T
            p_t = pt[head]
            dp_t = dot_nt(v[2 * BLOCK :, cols], da_h)
            ds_t = (p_t * (dp_t - inner_row) * SCALE).astype(jnp.bfloat16)
            dk[:, cols] = dot(ds_t, q[:, cols]).astype(jnp.bfloat16)
            dv[:, cols] = dot(p_t.astype(jnp.bfloat16), da_h).astype(jnp.bfloat16)
        stores = [
            store_g,
            move(14, dq, dq_out),
            move(15, dk, dk_out),
            move(16, dv, dv_out),
        ]
        load_w.wait()
        for n in range(0, WIDTH, 256):
            cols = slice(n, n + 256)
            dh[:, cols] = (
                dot_nt(dq[...], wv[0, cols, :])
                + dot_nt(dk[...], wv[1, cols, :])
                + dot_nt(dv[...], wv[2, cols, :])
            )
        load_x.wait()
        load_gain.wait()
        as_float = x[...].astype(jnp.float32)
        rscale = lax.rsqrt(jnp.mean(as_float * as_float, axis=-1, keepdims=True) + 1e-06)
        d_normed = dh[...]
        scaled = gain[0:1, :] * d_normed
        cubic = rscale * rscale * rscale
        frame_f = (
            g[:BLOCK, :].astype(jnp.float32)
            + rscale * scaled
            - as_float * (cubic * jnp.mean(scaled * as_float, axis=-1, keepdims=True))
        )
        frame[...] = frame_f.astype(jnp.bfloat16)
        stores.append(move(17, frame, frame_out))
        term = jnp.sum(d_normed * as_float * rscale, axis=0, keepdims=True)
        gain_sum[...] = jnp.broadcast_to(term, (8, WIDTH))
        stores.append(move(18, gain_sum, gain_out))
        for copy in stores:
            copy.wait()


def in_place(value):
    return pltpu.with_memory_space_constraint(value, pltpu.HBM)


def backward(micro, flag, incoming, w, kept, x, gain):
    block = pltpu.HBM((BLOCK, WIDTH), jnp.bfloat16)
    outs = [block] * 5 + [pltpu.HBM((8, WIDTH), jnp.float32)]
    operands = [flag, *incoming] + [in_place(value) for value in (w, *kept, x, gain)]
    anywhere = pl.BlockSpec(memory_space=pl.ANY)
    in_hbm = pl.BlockSpec(memory_space=pltpu.HBM)
    bf16, f32 = jnp.bfloat16, jnp.float32
    scratch = [
        ((3 * BLOCK, WIDTH), bf16),
        ((4, WIDTH, WIDTH), bf16),
        ((3 * BLOCK, WIDTH), bf16),
        ((3 * BLOCK, WIDTH), bf16),
        ((3 * BLOCK, WIDTH), bf16),
        ((HEADS, BLOCK, 3 * BLOCK), f32),
        ((HEADS, BLOCK, 3 * BLOCK), f32),
        ((3 * BLOCK, WIDTH), f32),
        ((BLOCK, WIDTH), bf16),
        ((8, WIDTH), f32),
        ((3 * BLOCK, WIDTH), bf16),
        ((BLOCK, WIDTH), bf16),
        ((BLOCK, WIDTH), bf16),
        ((BLOCK, WIDTH), bf16),
        ((BLOCK, WIDTH), f32),
        ((BLOCK, WIDTH), bf16),
        ((8, WIDTH), f32),
    ]
    return pl.pallas_call(
        partial(backward_kernel, micro),
        in_specs=[pl.BlockSpec(memory_space=pltpu.SMEM)] + [anywhere] * (len(operands) - 1),
        out_specs=[in_hbm] * 6,
        out_shape=outs,
        scratch_shapes=[pltpu.VMEM(shape, kind) for shape, kind in scratch]
        + [pltpu.SemaphoreType.DMA((19,))],
        compiler_params=pltpu.CompilerParams(vmem_limit_bytes=48 * MIB),
        cost_estimate=pl.CostEstimate(
            flops=2 * 7 * BLOCK * WIDTH * WIDTH, bytes_accessed=16 << 20, transcendentals=0
        ),
        name="backward",
    )(*operands)


def ring_slots(size):
    if size == 4:
        return (2, 2, 2, 1, 1), {
            (0, 0): (0, 0), (1, 0): (0, 1),
            (0, 1): (3, 0), (1, 1): (1, 1),
            (0, 2): (1, 0), (1, 2): (2, 1),
            (0, 3): (2, 0), (1, 3): (4, 0),
        }
    return (2,) * size, {(m, f): (f, m) for m in range(2) for f in range(size)}


def ring_heads(size):
    return (1, 2) if size == 4 else (1,) * (size == 2)


def add(*values):
    return sum(value.astype(jnp.float32) for value in values)


def ring_send(parts, axis):
    size = group_dims()[axis]
    if size == 4:
        return [turn(parts[1], axis, 1), turn(parts[2], axis, -1)]
    return [turn(parts[1], axis, 1)] if size == 2 else []


def ring_sum(parts, arrived, axis, gain):
    size, head = group_dims()[axis], 0 if gain is None else HEAD_ROWS
    rows = parts[0].shape[0] // 2
    if size == 4:
        keep, _, _, late_up, late_down = parts
        up, down = arrived
        late_up = add(late_up, up[head : head + rows]).astype(jnp.bfloat16)
        late_down = add(late_down, down[head + rows :]).astype(jnp.bfloat16)
        if head:
            late_up = jnp.concatenate([up[:head], late_up])
        late_up, late_down = turn(late_up, axis, 1), turn(late_down, axis, -1)
        total = [
            add(keep[:rows], late_up[head:], down[head : head + rows]),
            add(keep[rows:], up[head + rows :], late_down),
        ]
        if head:
            gain = add(gain, up[:head], down[:head], late_up[:head])
        return jnp.stack(total), gain
    if size == 2:
        (other,) = arrived
        if head:
            gain = add(gain, other[:head])
        return add(parts[0], other[head:]).reshape(2, rows, WIDTH), gain
    return parts[0].astype(jnp.float32).reshape(2, rows, WIDTH), gain


def collect_kernel(sections, dims, counts, *refs):
    place, spot, h_in, a_in = refs[:4]
    kept = refs[4 : 4 + 12 * sections]
    refs = refs[4 + 12 * sections :]
    frame_out, gain_out, outs = refs[0], refs[1], refs[2 : 2 + sum(counts)]
    left, right, term, frame, gain, gain_head, sems, out_sems = refs[2 + sum(counts) :]
    planes, size_y, size_x = dims
    share = WIDTH // (planes * size_y * size_x)
    own_y, own_x = spot[1], spot[2]
    names = ("frame", "g", "dq", "dk", "dv", "gain")

    def copies(at):
        found = []
        for micro in range(MICRO):
            results = dict(zip(names, kept[(at * MICRO + micro) * 6 : (at * MICRO + micro + 1) * 6]))
            rows = pl.ds(micro * BLOCK, BLOCK)
            pairs = [(results[name], right.at[n, rows]) for n, name in enumerate(("dq", "dk", "dv", "g"))]
            pairs += [(results["frame"], frame.at[micro]), (results["gain"], gain.at[micro])]
            pairs += [(h_in.at[micro], left.at[0, rows]), (a_in.at[micro], left.at[1, rows])]
            found += [
                pltpu.make_async_copy(source, target, sems.at[micro, n])
                for n, (source, target) in enumerate(pairs)
            ]
        return found

    for at in range(sections):

        @pl.when(place[0] == at)
        def _(at=at):
            started = copies(at)
            for copy in started:
                copy.start()
            for copy in started:
                copy.wait()

    frame_copy = pltpu.make_async_copy(frame, frame_out, out_sems.at[4, 0])
    frame_copy.start()
    gain_term = (gain[0, 0:1, :] + gain[1, 0:1, :]).astype(jnp.bfloat16)
    gain_head[...] = jnp.broadcast_to(gain_term, (HEAD_ROWS, WIDTH))
    started = [frame_copy]
    heads = [gain_out] + [outs[at].at[pl.ds(0, HEAD_ROWS), :] for at in ring_heads(size_x)]
    for at, target in enumerate(heads):
        copy = pltpu.make_async_copy(gain_head, target, out_sems.at[4, 1 + at])
        copy.start()
        started.append(copy)
    for m in range(4):
        pair = m // 2
        first_size, second_size = (size_x, size_y) if pair == 0 else (size_y, size_x)
        _, slots = ring_slots(first_size)
        arrays = outs[: counts[0]] if pair == 0 else outs[counts[0] :]
        factor = left[1 if m == 3 else 0]
        for n in range(0, WIDTH, 256):
            cols = slice(n, n + 256)
            term[m, :, cols] = dot_tn(factor, right[m, :, cols]).astype(jnp.bfloat16)
        number = 0
        for f in range(first_size):
            array, row = slots[m % 2, f]
            for r in range(second_size):
                ahead_x, ahead_y = (f, r) if pair == 0 else (r, f)
                column = lax.rem(own_y + ahead_y, size_y) * size_x + lax.rem(own_x + ahead_x, size_x)
                for plane in range(planes):
                    at = (plane * size_y * size_x + column) * share
                    to = ((row * second_size + r) * planes + plane) * share
                    if pair == 0 and array in ring_heads(first_size):
                        to += HEAD_ROWS
                    copy = pltpu.make_async_copy(
                        term.at[m, pl.ds(pl.multiple_of(at, share), share), :],
                        arrays[array].at[pl.ds(to, share), :],
                        out_sems.at[m, number],
                    )
                    copy.start()
                    started.append(copy)
                    number += 1
    for copy in started:
        copy.wait()


def collect(section, spot, h, a, kept):
    dims, sections = group_dims(), len(kept)
    planes, size_y, size_x = dims
    total = planes * size_y * size_x
    share = WIDTH // total
    anywhere = pl.BlockSpec(memory_space=pl.ANY)
    in_hbm = pl.BlockSpec(memory_space=pltpu.HBM)
    smem = pl.BlockSpec(memory_space=pltpu.SMEM)
    shapes, counts = [], []
    for first_size, second_size in ((size_x, size_y), (size_y, size_x)):
        rows, _ = ring_slots(first_size)
        counts.append(len(rows))
        for at, n in enumerate(rows):
            n = n * second_size * planes * share
            if len(counts) == 1 and at in ring_heads(first_size):
                n += HEAD_ROWS
            shapes.append(jax.ShapeDtypeStruct((n, WIDTH), jnp.bfloat16))
    operands = [in_place(result) for both in kept for results in both for result in results]
    outs = pl.pallas_call(
        partial(collect_kernel, sections, dims, counts),
        in_specs=[smem, smem] + [anywhere] * (2 + len(operands)),
        out_specs=[in_hbm] * (2 + len(shapes)),
        out_shape=[
            jax.ShapeDtypeStruct((MICRO, BLOCK, WIDTH), jnp.bfloat16),
            jax.ShapeDtypeStruct((HEAD_ROWS, WIDTH), jnp.bfloat16),
        ]
        + shapes,
        scratch_shapes=[
            pltpu.VMEM((2, MICRO * BLOCK, WIDTH), jnp.bfloat16),
            pltpu.VMEM((4, MICRO * BLOCK, WIDTH), jnp.bfloat16),
            pltpu.VMEM((4, WIDTH, WIDTH), jnp.bfloat16),
            pltpu.VMEM((MICRO, BLOCK, WIDTH), jnp.bfloat16),
            pltpu.VMEM((MICRO, 8, WIDTH), jnp.float32),
            pltpu.VMEM((HEAD_ROWS, WIDTH), jnp.bfloat16),
            pltpu.SemaphoreType.DMA((MICRO, 8)),
            pltpu.SemaphoreType.DMA((5, max(total, 4))),
        ],
        compiler_params=pltpu.CompilerParams(vmem_limit_bytes=48 * MIB),
        cost_estimate=pl.CostEstimate(
            flops=2 * 8 * BLOCK * WIDTH * WIDTH, bytes_accessed=14 << 20, transcendentals=0
        ),
        name="collect",
    )(section, spot, h, a, *operands)
    frame, gain = outs[:2]
    return frame, gain, [outs[2 : 2 + counts[0]], outs[2 + counts[0] :]]


def ring_parts(value, size, gain):
    value = value.astype(jnp.bfloat16).reshape(2, size, -1, WIDTH)
    rows, slots = ring_slots(size)
    arrays = [[None] * n for n in rows]
    for (m, f), (array, row) in slots.items():
        arrays[array][row] = value[m, f]
    if gain is not None:
        gain = gain.astype(jnp.bfloat16)
        for array in ring_heads(size):
            arrays[array].insert(0, gain)
    return [jnp.concatenate(array) for array in arrays], gain


def sum_terms(parts, gain, plane):
    dims, orders = group_dims(), ((2, 1), (1, 2))
    gains = [gain, None]
    for stage in range(2):
        axes = [order[stage] for order in orders]
        arrived = [ring_send(pair, axis) for pair, axis in zip(parts, axes)]
        tied = tie_all(arrived[0] + arrived[1])
        arrived = [tied[: len(arrived[0])], tied[len(arrived[0]) :]]
        sums = [ring_sum(*each) for each in zip(parts, arrived, axes, gains)]
        totals, gains = [total for total, _ in sums], [own for _, own in sums]
        if stage == 0:
            parts, gains = zip(*[
                ring_parts(total, dims[second], own)
                for total, own, (_, second) in zip(totals, gains, orders)
            ])
    gain = gains[0]
    value = jnp.concatenate(totals)
    if dims[0] == 1:
        return value, gain
    share = value.shape[1] // 2
    value = value.reshape(4, 2, share, WIDTH)
    other = lax.dynamic_index_in_dim(value, 1 - plane, 1, keepdims=False).astype(jnp.bfloat16)
    own = lax.dynamic_index_in_dim(value, plane, 1, keepdims=False)
    other = jnp.concatenate([gain.astype(jnp.bfloat16), other.reshape(4 * share, WIDTH)])
    other = turn(other, 0, 1)
    return add(own, other[HEAD_ROWS:].reshape(own.shape)), add(gain, other[:HEAD_ROWS])


def segments(lengths, block):
    bounds = jnp.cumsum(lengths, axis=1)
    total = lax.axis_size(GROUP) * BLOCK
    places = (block - 2) * BLOCK + jnp.arange(5 * BLOCK, dtype=jnp.int32)
    counted = jnp.sum((places[None, :, None] >= bounds[:, None, :]).astype(jnp.int32), axis=2)
    return jnp.where(places < 0, -1, jnp.where(places >= total, -2, counted))


def body(checkpoints, cotangent, weights, gains, lengths):
    sections, section = lax.axis_size("section"), lax.axis_index("section")
    block = lax.axis_index(GROUP)
    share = gains.shape[1]

    planes, size_y, _ = group_dims()
    dp = lax.axis_index("dp")
    spot = jnp.stack([dp // size_y, dp % size_y, lax.axis_index("fsdp")]).astype(jnp.int32)
    spread = lax.dynamic_update_slice(
        jnp.zeros((1, share, WIDTH), jnp.bfloat16), gains[None], (0, 0, block * share)
    )
    pairs, gain = gather_weights(weights[0], spread, spot)
    gain = jnp.broadcast_to(gain[0, 0:1].astype(jnp.float32), (8, WIDTH))

    x = checkpoints[0]
    left, right = shift(x, 1), shift(x, -1)
    parts = (shift(left, 1), left, x, right, shift(right, -1))
    source = max(sections - 3, 0)
    cot = (cotangent, hop(cotangent, source, sections - 1, 1), hop(cotangent, source, sections - 1, 2))

    segs = segments(lengths, block)
    gathered, h, q, k, v, p, pt, o, a = forward(
        spot, pairs, parts, gain, segs[:, :, None], segs[:, None, :]
    )
    gathered = gathered.reshape(4, WIDTH, WIDTH)
    kept = (q, k, v, p, pt, o)

    kept_grads = [[None] * MICRO for _ in range(sections)]
    arriving, behind = ([part[micro] for part in cot] for micro in range(MICRO))
    for at in range(sections - 1, -1, -1):
        flag = (section == at).astype(jnp.int32).reshape(1)
        first = list(backward(0, flag, arriving, gathered, kept, x, gain))
        leaving = first[0]
        if at > 0:
            arriving = [hop(leaving, at, at - 1, back) for back in (2, 1, 0)][::-1]
        if at < sections - 1:
            second[0] = tie(second[0], arriving[0] if at > 0 else leaving)
            behind = [hop(second[0], at + 1, at, back) for back in (2, 1, 0)][::-1]
        second = list(backward(1, flag, behind, gathered, kept, x, gain))
        kept_grads[at] = [first, second]

    place = section.astype(jnp.int32).reshape(1)
    frame, gain_part, parts = collect(place, spot, h, a, kept_grads)
    weight_part, gain_sum = sum_terms(parts, gain_part, spot[0])
    gain_sum = lax.dynamic_slice(gain_sum, (0, block * share), (1, share))
    return (frame[None], weight_part[None], gain_sum)


def solution(mesh):
    placed = (
        P("section", None, ("dp", "fsdp"), None),
        P(None, ("dp", "fsdp"), None),
        P("section", None, ("dp", "fsdp"), None),
        P("section", ("dp", "fsdp")),
        P(),
    )
    return jax.shard_map(
        body,
        mesh=mesh,
        in_specs=placed,
        out_specs=(
            P("section", None, ("dp", "fsdp"), None),
            P("section", None, ("dp", "fsdp"), None),
            P("section", ("dp", "fsdp")),
        ),
        check_vma=False,
    )
```
